32 devices in a mesh: groups: 2 (over x), space: 8 (over z, y), member: 2 (over core).
Axes of the slice: x: 2, y: 2, z: 4, core: 2. Of those that a mesh axis runs over, the one named last changes fastest.
Arguments:
- latent: bfloat16 [8, 512, 1024], P(('groups', 'member'), 'space'), parts along dimension 0, may hold values from -6 to 6
- edge_node_index: int32 [8192, 4], P(('groups', 'space')), parts along dimension 0, may hold values from 0 to 511, as said below
- edge_mask: int32 [8192, 4], P(('groups', 'space')), parts along dimension 0, may hold values 0 or 1
- edge_weight: float32 [8192, 4], P(('groups', 'space')), parts along dimension 0, may hold values from 0.2 to 1
- valid: int32 [8192], P(('groups', 'space')), parts along dimension 0, may hold values 0 or 1
- area: float32 [8192], P(('groups', 'space')), parts along dimension 0, may hold values from 0.3 to 3
- state: float32 [8192, 100], P(('groups', 'space')), parts along dimension 0, may hold values from -6 to 6
- target: float32 [8192, 100], P(('groups', 'space')), parts along dimension 0, may hold values from -8 to 8
- var_weight: float32 [100], replicated, may hold values from 0.1 to 1
- gain: float32 [1024], replicated, may hold values from 0.25 to 1.75
- hidden_weight: bfloat16 [1024, 1024], replicated, may hold values from -0.1875 to 0.1875
- output_weight: bfloat16 [1024, 100], replicated, may hold values from -0.1875 to 0.1875
Outputs:
- loss: float32 [2], P('groups'), parts along dimension 0
- grad_hidden: float32 [2048, 1024], P('groups'), parts along dimension 0
- grad_out: float32 [2048, 100], P('groups'), parts along dimension 0
- grad_gain: float32 [2048], P('groups'), parts along dimension 0
- grad_latent: float32 [8, 512, 1024], P(('groups', 'member'), 'space'), parts along dimension 0
The draws below stay inside these ranges and needn't reach their ends.
There are 2 independent parts, one for each index of `groups`. The reference program is written for one: setup_inputs(seed, part) draws one part's arguments, and reference() takes and returns one part's arrays. A program takes and returns all parts, laid end to end along the dimension named above; an argument that names none is the same for every part. Nothing has to cross between parts.
Inputs may be any that keep to these rules, and one draw needn't show every extreme that they name: `edge_node_index`: grid points p * 512 to (p+1) * 512 - 1 name only mesh nodes from p * 64 - 16 to (p+1) * 64 + 15; within every such block both ends of that range are named where they lie inside the mesh.
All inputs are finite; a program needn't handle non-finite values. No bound on the sum of `edge_mask` or of `valid` on one device may be relied on, other than what follows from the above.
Results may differ from the reference program's by a relative error of at most 0.015.
Values may be sent and summed in bfloat16 or wider, within the bound.
No kernel may reach another device: no remote copies, remote signals or barrier semaphores. Data moves between devices by JAX's collectives and lax.ppermute only.
A program may use at most 64 MiB of HBM per device.

```python
import math
import jax
import jax.numpy as jnp
from jax import lax

HID = 1024
VARS = 100
DEG = 4
GRID_DEV = 512
MESH_DEV = 64
RIM = 16
MEMBERS = 4
GRID = 4096
MESH = 512


def draw_edge_node_index(key, part):
    key = jax.random.fold_in(key, 11)
    rows = jnp.arange(GRID, dtype=jnp.int32)
    block = rows // GRID_DEV
    lowest = block * MESH_DEV - RIM
    offset = jax.random.randint(key, (GRID, DEG), 0, MESH_DEV + 2 * RIM, dtype=jnp.int32)
    chosen = lowest[:, None] + offset
    place = rows % GRID_DEV
    second = jnp.where(place == 0, lowest, jnp.where(place == 1, lowest + MESH_DEV + 2 * RIM - 1, chosen[:, 1]))
    chosen = chosen.at[:, 1].set(second)
    return jnp.clip(chosen, 0, MESH - 1).astype(jnp.int32)


def touch_ends(array, own_key, smallest, high):
    spot = [jax.random.randint(jax.random.fold_in(own_key, axis), (), 0, length) for axis, length in enumerate(array.shape)]
    longest = array.shape.index(max(array.shape))
    beside = spot[:longest] + [(spot[longest] + 1) % array.shape[longest]] + spot[longest + 1:]
    return array.at[tuple(spot)].set(smallest).at[tuple(beside)].set(high)


def block_scale(rng, dims, cuts, low, top_value):
    loudness = 1.0
    for axis_at, parts in cuts:
        steps = jax.random.uniform(jax.random.fold_in(jax.random.fold_in(rng, 6), axis_at), (parts,), jnp.float32, low / len(cuts), top_value / len(cuts))
        loudness = loudness * jnp.repeat(jnp.exp(steps), dims[axis_at] // parts).reshape((-1,) + (1,) * (len(dims) - 1 - axis_at))
    return loudness


def gaussian(own_key, extent, scale, limit, shards=(), held_as=jnp.bfloat16):
    drawn = jax.random.normal(own_key, extent, jnp.float32) * scale
    if len(shards) > 0:
        drawn = block_scale(own_key, extent, shards, -0.22, 0.18) * drawn
    return jnp.clip(drawn, min=-limit, max=limit).astype(held_as)


def setup_inputs(seed: int = 0, part: int = 0) -> dict:
    key_list = jax.random.split(jax.random.key(seed), 13)
    own_keys = jax.random.split(jax.random.fold_in(key_list[12], part), 13)
    return {
        "latent": gaussian(own_keys[0], (MEMBERS, MESH, HID), 1.0, 6.0, ((0, 2), (1, 8))),
        "edge_node_index": draw_edge_node_index(jax.random.fold_in(jax.random.fold_in(key_list[12], part), 71), part),
        "edge_mask": touch_ends((jax.random.randint(own_keys[2], (GRID, DEG), 0, 4) < 3).astype(jnp.int32), jax.random.fold_in(own_keys[2], 1), 0, 1),
        "edge_weight": jnp.clip(jnp.exp(math.log(1.0) - 1.609438 * jax.random.uniform(own_keys[3], (GRID, DEG), jnp.float32) ** block_scale(own_keys[3], (GRID, DEG), ((0, 8),), -0.2, 0.2)), 0.2, 1.0),
        "valid": touch_ends((jax.random.randint(own_keys[4], (GRID,), 0, 8) < 7).astype(jnp.int32), jax.random.fold_in(own_keys[4], 1), 0, 1),
        "area": jnp.clip(jnp.exp(math.log(3.0) - 2.3025851 * jax.random.uniform(own_keys[5], (GRID,), jnp.float32) ** block_scale(own_keys[5], (GRID,), ((0, 8),), -0.2, 0.2)), 0.3, 3.0),
        "state": gaussian(own_keys[6], (GRID, VARS), 1.0, 6.0, ((0, 8),), jnp.float32),
        "target": gaussian(own_keys[7], (GRID, VARS), 1.5, 8.0, ((0, 8),), jnp.float32),
        "var_weight": jnp.clip(jnp.exp(jax.random.uniform(key_list[8], (VARS,), jnp.float32, math.log(0.1), math.log(1.0))), 0.1, 1.0),
        "gain": jnp.clip(1.0 + 0.15 * jax.random.normal(key_list[9], (HID,), jnp.float32), 0.25, 1.75),
        "hidden_weight": gaussian(key_list[10], (HID, HID), HID ** -0.5, 0.1875),
        "output_weight": gaussian(key_list[11], (HID, VARS), HID ** -0.5, 0.1875),
    }


SMOOTH_SQ = 0.01

def smooth(diff):
    return jnp.sqrt(diff * diff + SMOOTH_SQ)

def forward_pass(latent_single, edge_node_index, coefficient, gain, hidden_weight, output_weight, state):
    summed = jnp.zeros((edge_node_index.shape[0], latent_single.shape[1]), jnp.float32)
    for slot in range(edge_node_index.shape[1]):
        summed = summed + coefficient[:, slot][:, None] * latent_single[edge_node_index[:, slot]].astype(jnp.float32)
    centered_values = summed - lax.optimization_barrier(jnp.mean(summed, axis=1, keepdims=True))
    inverse_deviation = 1.0 / jnp.sqrt(lax.optimization_barrier(jnp.mean(centered_values * centered_values, axis=1, keepdims=True)) + 1e-05)
    standardized_input = centered_values * inverse_deviation
    normed_rows = (standardized_input * gain[None, :]).astype(jnp.bfloat16)
    preactivation = jnp.dot(normed_rows, hidden_weight, preferred_element_type=jnp.float32)
    hidden_rows = jax.nn.silu(preactivation).astype(jnp.bfloat16)
    prediction = state + jnp.dot(hidden_rows, output_weight, preferred_element_type=jnp.float32)
    return (prediction, standardized_input, inverse_deviation, normed_rows, preactivation, hidden_rows)

def reference(latent, edge_node_index, edge_mask, edge_weight, valid, area, state, target, var_weight, gain, hidden_weight, output_weight):
    coefficient = edge_weight * edge_mask.astype(jnp.float32)
    total = latent.shape[0]

    def pred_only(latent_single):
        return forward_pass(latent_single, edge_node_index, coefficient, gain, hidden_weight, output_weight, state)[0]
    preds = lax.map(pred_only, latent)
    weight = (valid.astype(jnp.float32) * area / GRID_DEV)[:, None] * var_weight[None, :]
    own_err = preds - target[None]
    pair = preds[:, None] - preds[None]
    loss = jnp.sum(weight * (lax.optimization_barrier(jnp.sum(smooth(own_err), axis=0)) / total - lax.optimization_barrier(jnp.sum(smooth(pair), axis=(0, 1))) / (2.0 * total * (total - 1))))
    gpred = (weight[None] * (own_err / smooth(own_err) / total - lax.optimization_barrier(jnp.sum(pair / smooth(pair), axis=1)) / (total * (total - 1)))).astype(jnp.bfloat16)

    def backward(carry, items):
        acc_hidden, acc_out, accumulated_gain = carry
        latent_single, grad_one = items
        prediction, standardized_input, inverse_deviation, normed_rows, preactivation, hidden_rows = forward_pass(latent_single, edge_node_index, coefficient, gain, hidden_weight, output_weight, state)
        acc_out = acc_out + jnp.dot(hidden_rows.T, grad_one, preferred_element_type=jnp.float32)
        ghid = jnp.dot(grad_one, output_weight.T, preferred_element_type=jnp.float32)
        sig = jax.nn.sigmoid(preactivation)
        gpre = (ghid * sig * (1.0 + preactivation * (1.0 - sig))).astype(jnp.bfloat16)
        acc_hidden = acc_hidden + jnp.dot(normed_rows.T, gpre, preferred_element_type=jnp.float32)
        grad_preact_normed = jnp.dot(gpre, hidden_weight.T, preferred_element_type=jnp.float32)
        accumulated_gain = accumulated_gain + lax.optimization_barrier(jnp.sum(grad_preact_normed * standardized_input, axis=0))
        grad_input_rows = grad_preact_normed * gain[None, :]
        grad_preact = inverse_deviation * (grad_input_rows - lax.optimization_barrier(jnp.mean(grad_input_rows, axis=1, keepdims=True)) - standardized_input * lax.optimization_barrier(jnp.mean(grad_input_rows * standardized_input, axis=1, keepdims=True)))
        glat = jnp.zeros(latent_single.shape, jnp.float32)
        for slot in range(edge_node_index.shape[1]):
            glat = glat.at[edge_node_index[:, slot]].add(coefficient[:, slot][:, None] * grad_preact)
        return ((acc_hidden, acc_out, accumulated_gain), glat)
    start = (jnp.zeros(hidden_weight.shape, jnp.float32), jnp.zeros(output_weight.shape, jnp.float32), jnp.zeros(gain.shape, jnp.float32))
    (grad_hidden, grad_out, grad_gain), grad_latent = lax.scan(backward, start, (latent, gpred))
    return (loss.reshape(1), grad_hidden, grad_out, grad_gain, grad_latent)
```

```python
import jax
import jax.numpy as jnp
from jax import lax
from jax.sharding import PartitionSpec as P

RIM = 16


SMOOTH_SQ = 0.01


def with_halo(block, axis, dim, width):
    count = lax.axis_size(axis)
    forward = [(i, i + 1) for i in range(count - 1)]
    backward = [(target, source) for source, target in forward]
    low = lax.ppermute(
        lax.slice_in_dim(block, block.shape[dim] - width, None, axis=dim), axis, forward
    )
    high = lax.ppermute(lax.slice_in_dim(block, 0, width, axis=dim), axis, backward)
    return jnp.concatenate([low, block, high], axis=dim)


def from_behind(value, axis, steps):
    count = lax.axis_size(axis)
    first, last = (max(0, -steps), min(count, count - steps))
    return lax.ppermute(value, axis, [(source, source + steps) for source in range(first, last)])


def smooth(diff):
    return jnp.sqrt(diff * diff + SMOOTH_SQ)


def split_parts(values):
    upper = values.astype(jnp.bfloat16)
    lower = (values - upper.astype(jnp.float32)).astype(jnp.bfloat16)
    return (upper, lower)


def swap(value, axis, bit):
    count = lax.axis_size(axis)
    return lax.ppermute(value, axis, [(i, i ^ (1 << bit)) for i in range(count)])


def halve(value, axis, bit):
    rows = value.shape[0] // 2
    upper = (lax.axis_index(axis) >> bit) & 1
    low, high = value[:rows], value[rows:]
    sent = jnp.where(upper == 0, high, low).astype(jnp.bfloat16)
    kept = jnp.where(upper == 0, low, high)
    return kept + swap(sent, axis, bit).astype(jnp.float32)


def double(value, axis, bit):
    upper = (lax.axis_index(axis) >> bit) & 1
    other = swap(value, axis, bit)
    return jnp.where(
        upper == 0, jnp.concatenate([value, other]), jnp.concatenate([other, value])
    )


def sum_stream(value, axis, order):
    for bit in order[:-1]:
        value = halve(value, axis, bit)
    mine = value.astype(jnp.bfloat16)
    other = swap(mine, axis, order[-1])
    value = (mine.astype(jnp.float32) + other.astype(jnp.float32)).astype(jnp.bfloat16)
    for bit in reversed(order[:-1]):
        value = double(value, axis, bit)
    return value


def sum_small(value, axis):
    for bit in range(lax.axis_size(axis).bit_length() - 1):
        value = value + swap(value, axis, bit)
    return value


def sum_weights(value):
    bits = lax.axis_size("space").bit_length() - 1
    value = halve(value, "member", 0)
    half = value.shape[0] // 2
    rest = list(range(2, bits))
    first = sum_stream(value[:half], "space", [0, 1] + rest)
    second = sum_stream(value[half:], "space", [1, 0] + rest)
    return double(jnp.concatenate([first, second]), "member", 0)


def local(
    latent,
    edge_node_index,
    edge_mask,
    edge_weight,
    valid,
    area,
    state,
    target,
    var_weight,
    gain,
    hidden_weight,
    output_weight,
):
    members, nodes, width = latent.shape
    points = state.shape[0]
    extended = with_halo(latent, "space", 1, RIM)
    span = nodes + 2 * RIM
    anchor = lax.axis_index("space") * nodes - RIM
    local_index = edge_node_index - anchor
    coefficient = edge_weight * edge_mask.astype(jnp.float32)
    slots = jnp.arange(span, dtype=jnp.int32)
    adjacency = jnp.zeros((points, span), jnp.float32)
    for slot in range(edge_node_index.shape[1]):
        adjacency = adjacency + coefficient[:, slot][:, None] * (
            local_index[:, slot][:, None] == slots[None, :]
        ).astype(jnp.float32)
    adj_upper, adj_lower = split_parts(adjacency)
    summed = jnp.einsum("ge,mec->mgc", adj_upper, extended, preferred_element_type=jnp.float32)
    summed = summed + jnp.einsum(
        "ge,mec->mgc", adj_lower, extended, preferred_element_type=jnp.float32
    )
    summed = summed.reshape(members * points, width)
    centered_values = summed - jnp.mean(summed, axis=1, keepdims=True)
    inverse_deviation = 1.0 / jnp.sqrt(
        jnp.mean(centered_values * centered_values, axis=1, keepdims=True) + 1e-05
    )
    standardized_input = centered_values * inverse_deviation
    normed_rows = (standardized_input * gain[None, :]).astype(jnp.bfloat16)
    preactivation = jnp.dot(normed_rows, hidden_weight, preferred_element_type=jnp.float32)
    hidden_rows = jax.nn.silu(preactivation).astype(jnp.bfloat16)
    outputs = jnp.dot(hidden_rows, output_weight, preferred_element_type=jnp.float32)
    preds = state[None] + outputs.reshape(members, points, -1)
    others = swap(preds, "member", 0)
    total = 2 * members
    ensemble = jnp.concatenate([preds, others], axis=0)
    weight = (valid.astype(jnp.float32) * area / points)[:, None] * var_weight[None, :]
    own_err = preds - target[None]
    pair = preds[:, None] - ensemble[None]
    loss_local = jnp.sum(
        weight
        * (
            jnp.sum(smooth(own_err), axis=0) / total
            - jnp.sum(smooth(pair), axis=(0, 1)) / (2.0 * total * (total - 1))
        )
    )
    gpred = (
        weight[None]
        * (
            own_err / smooth(own_err) / total
            - jnp.sum(pair / smooth(pair), axis=1) / (total * (total - 1))
        )
    ).astype(jnp.bfloat16)
    gpred = gpred.reshape(members * points, -1)
    variables = gpred.shape[1]
    part_out = jnp.dot(hidden_rows.T, gpred, preferred_element_type=jnp.float32)
    ghid = jnp.dot(gpred, output_weight.T, preferred_element_type=jnp.float32)
    sig = jax.nn.sigmoid(preactivation)
    gpre = (ghid * sig * (1.0 + preactivation * (1.0 - sig))).astype(jnp.bfloat16)
    part_hidden = jnp.dot(normed_rows.T, gpre, preferred_element_type=jnp.float32)
    part_out = jnp.pad(part_out, ((0, 0), (0, -variables % 128)))
    weights = sum_weights(jnp.concatenate([part_hidden, part_out], axis=1))
    grad_hidden = weights[:, :width].astype(jnp.float32)
    grad_out = weights[:, width : width + variables].astype(jnp.float32)
    grad_preact_normed = jnp.dot(gpre, hidden_weight.T, preferred_element_type=jnp.float32)
    partial_gain = jnp.sum(grad_preact_normed * standardized_input, axis=0)
    small = jnp.concatenate([partial_gain, jnp.full((128,), loss_local)])
    small = sum_small(sum_small(small, "member"), "space")
    grad_gain, loss = small[:width], small[width : width + 1]
    scaled_rows = grad_preact_normed * gain[None, :]
    grad_preact = inverse_deviation * (
        scaled_rows
        - jnp.mean(scaled_rows, axis=1, keepdims=True)
        - standardized_input * jnp.mean(scaled_rows * standardized_input, axis=1, keepdims=True)
    )
    grad_preact = grad_preact.reshape(members, points, width)
    gz_upper, gz_lower = split_parts(grad_preact)
    grad_ext = jnp.einsum("ge,mgc->mec", adj_upper, gz_upper, preferred_element_type=jnp.float32)
    grad_ext = grad_ext + jnp.einsum(
        "ge,mgc->mec", adj_upper, gz_lower, preferred_element_type=jnp.float32
    )
    grad_ext = grad_ext + jnp.einsum(
        "ge,mgc->mec", adj_lower, gz_upper, preferred_element_type=jnp.float32
    )
    lower_rim = grad_ext[:, :RIM]
    upper_rim = grad_ext[:, RIM + nodes :]
    from_below = from_behind(upper_rim.astype(jnp.bfloat16), "space", 1).astype(upper_rim.dtype)
    from_above = from_behind(lower_rim.astype(jnp.bfloat16), "space", -1).astype(lower_rim.dtype)
    grad_latent = grad_ext[:, RIM : RIM + nodes]
    grad_latent = grad_latent.at[:, :RIM].add(from_below)
    grad_latent = grad_latent.at[:, nodes - RIM :].add(from_above)
    return (loss, grad_hidden, grad_out, grad_gain, grad_latent)


def solution(mesh):
    in_specs = (
        P(("groups", "member"), "space", None),
        P(("groups", "space"), None),
        P(("groups", "space"), None),
        P(("groups", "space"), None),
        P(("groups", "space")),
        P(("groups", "space")),
        P(("groups", "space"), None),
        P(("groups", "space"), None),
        P(),
        P(),
        P(),
        P(),
    )
    out_specs = (
        P("groups"),
        P("groups", None),
        P("groups", None),
        P("groups"),
        P(("groups", "member"), "space", None),
    )
    return jax.shard_map(local, mesh=mesh, in_specs=in_specs, out_specs=out_specs, check_vma=False)
```

```python
import jax
import jax.numpy as jnp
from jax import lax
from jax.experimental import pallas as pl
from jax.experimental.pallas import tpu as pltpu
from jax.sharding import PartitionSpec as P

RIM = 16
SMOOTH_SQ = 0.01
LANES = 128
BF16 = jnp.bfloat16
F32 = jnp.float32
VMEM = pl.BlockSpec(memory_space=pltpu.VMEM)
SMEM = pl.BlockSpec(memory_space=pltpu.SMEM)
PARAMS = pltpu.CompilerParams(vmem_limit_bytes=32 * 1024 * 1024)


def shift(value, axis, steps):
    count = lax.axis_size(axis)
    first, last = (max(0, -steps), min(count, count - steps))
    return lax.ppermute(value, axis, [(source, source + steps) for source in range(first, last)])


def swap_cores(value):
    return lax.ppermute(value, "member", [(0, 1), (1, 0)])


def swap_bits(value, bits):
    pairs = [
        (s * 2 + c, (s ^ (1 << bits[c])) * 2 + c)
        for s in range(lax.axis_size("space"))
        for c in range(2)
    ]
    return lax.ppermute(value, ("space", "member"), pairs)


def orders(chunk, count):
    first = [[(0, 1), (1, 0), (2, 2)], [(0, 2), (2, 0), (1, 1)]][chunk]
    return first + [(bit, bit) for bit in range(3, count)]


def turn(chunk, count, space, half):
    value = 0
    stages = orders(chunk, count)[:-1]
    for level, bits in enumerate(stages):
        value = value + ((1 - ((space >> bits[half]) & 1)) << (len(stages) - 1 - level))
    return value


def dot(a, b, dims=((1,), (0,))):
    return lax.dot_general(a, b, (dims, ((), ())), preferred_element_type=F32)


def adjacency_kernel(place, index, mask, weight, valid, area, var_weight, adj, adj_t, score_weight):
    points = index.shape[1]
    nodes = jax.lax.broadcasted_iota(jnp.int32, (LANES, points), 0) + place[0]
    total = jnp.zeros((LANES, points), F32)
    for slot in range(index.shape[0]):
        coefficient = weight[slot : slot + 1, :] * mask[slot : slot + 1, :].astype(F32)
        total = total + jnp.where(index[slot : slot + 1, :] == nodes, coefficient, 0.0)
    upper = total.astype(BF16).astype(F32)
    lower = total - upper
    adj_t[:LANES, :] = upper.astype(BF16)
    adj_t[LANES:, :] = lower.astype(BF16)
    adj[:, :LANES] = upper.T.astype(BF16)
    adj[:, LANES:] = lower.T.astype(BF16)
    score_weight[...] = var_weight[...] * (valid[...].astype(F32) * area[...] / points)


def forward_kernel(
    adj, low, own, high, gain, hidden_weight, output_weight,
    normed, hidden, slope, outputs, deviation, extended, summed, projected,
):
    members, nodes, width = own.shape
    points = adj.shape[0]
    tile = 256
    for member in range(members):
        for part in range(2):
            start = part * LANES
            extended[start : start + RIM, :] = low[member]
            extended[start + RIM : start + RIM + nodes, :] = own[member]
            extended[start + RIM + nodes : start + 2 * RIM + nodes, :] = high[member]
            extended[start + 2 * RIM + nodes : start + LANES, :] = jnp.zeros(
                (LANES - 2 * RIM - nodes, width), BF16
            )
        summed[...] = dot(adj[...], extended[...])

        @pl.loop(0, points // 32, unroll=4)
        def _(step):
            rows = pl.ds(pl.multiple_of(step * 32, 32), 32)
            target = pl.ds(pl.multiple_of(member * points + step * 32, 32), 32)
            value = summed[rows, :]
            value = value - jnp.sum(value, axis=1, keepdims=True) * (1.0 / width)
            spread = jnp.sum(value * value, axis=1, keepdims=True) * (1.0 / width)
            inverse = lax.rsqrt(spread + 1e-05)
            deviation[target, :] = inverse
            normed[target, :] = (value * inverse * gain[...]).astype(BF16)

    for member in range(members):
        rows = slice(member * points, (member + 1) * points)
        for column in range(0, width, tile):
            columns = slice(column, column + tile)
            pre = dot(normed[rows, :], hidden_weight[:, columns])
            sig = 0.5 * jnp.tanh(0.5 * pre) + 0.5
            hid = pre * sig
            slope[rows, columns] = (sig + hid * (1.0 - sig)).astype(BF16)
            hid = hid.astype(BF16)
            hidden[rows, columns] = hid
            term = dot(hid, output_weight[:, columns], ((1,), (1,)))
            if column == 0:
                projected[...] = term
            else:
                projected[...] += term
        outputs[member] = projected[...].T[: outputs.shape[1], :]


def own_rows(place, count, width):
    half_rows, chunk_rows = width // 2, width // 4
    size = chunk_rows >> (count - 1)
    for half in range(2):
        for chunk in range(2):
            mask = turn(chunk, count, place[0], half)
            for block in range(chunk_rows // size):
                row = half * half_rows + chunk * chunk_rows
                start = (1 - (place[1] ^ half)) * half_rows + chunk * chunk_rows
                start = start + (block ^ mask) * size
                yield row + block * size, size, pl.multiple_of(start, size)


def transpose_kernel(count, place, normed, normed_t):
    width = normed.shape[1]
    value = None
    for row, size, target in own_rows(place, count, width):
        if row % LANES == 0:
            value = normed[:, row : row + LANES].T
        offset = row % LANES
        normed_t[pl.ds(target, size), :] = value[offset : offset + size]


def score_kernel(
    count, place, outputs, others, state, target, score_weight, output_weight, slope, hidden, normed_t,
    loss, grad_pre, grad_out, sent,
    grad_pred, grad_pred_t,
):
    members, variables, points = outputs.shape
    width = hidden.shape[1]
    total = 2 * members
    weight = score_weight[...]
    grad_pred_t[...] = jnp.zeros_like(grad_pred_t)
    grad_pred[...] = jnp.zeros_like(grad_pred)
    base = state[...] - target[...]
    values = [outputs[m] for m in range(members)]
    grads = [None] * members
    pair_grads = [jnp.zeros((variables, points), F32) for _ in range(members)]
    errors = jnp.zeros((variables, points), F32)
    pairs = jnp.full((variables, points), members * SMOOTH_SQ**0.5, F32)
    for m in range(members):
        diff = values[m] + base
        square = diff * diff + SMOOTH_SQ
        inverse = lax.rsqrt(square)
        errors = errors + square * inverse
        grads[m] = diff * inverse
        for n in range(m + 1, members):
            diff = values[m] - values[n]
            square = diff * diff + SMOOTH_SQ
            inverse = lax.rsqrt(square)
            pairs = pairs + 2.0 * (square * inverse)
            pair_grads[m] = pair_grads[m] + diff * inverse
            pair_grads[n] = pair_grads[n] - diff * inverse
        for n in range(members):
            diff = values[m] - others[n]
            square = diff * diff + SMOOTH_SQ
            inverse = lax.rsqrt(square)
            pairs = pairs + square * inverse
            pair_grads[m] = pair_grads[m] + diff * inverse
    score = weight * (errors * (1.0 / total) - pairs * (1.0 / (2.0 * total * (total - 1))))
    loss[...] = jnp.sum(jnp.sum(score, axis=0, keepdims=True), axis=1, keepdims=True)
    for m in range(members):
        grad = weight * (grads[m] * (1.0 / total) - pair_grads[m] * (1.0 / (total * (total - 1))))
        columns = slice(m * points, (m + 1) * points)
        grad_pred_t[:variables, columns] = grad
        grad_pred[columns, :] = grad_pred_t[:, columns].T.astype(BF16)
    for m in range(members):
        rows = slice(m * points, (m + 1) * points)
        for column in range(0, width, 256):
            columns = slice(column, column + 256)
            grad_hid = dot(grad_pred[rows, :], output_weight[:, columns])
            grad_pre[rows, columns] = (grad_hid * slope[rows, columns].astype(F32)).astype(BF16)
    value = dot(grad_pred_t[...].astype(BF16), hidden[...]).T
    for row, size, place_row in own_rows(place, count, width):
        grad_out[pl.ds(place_row, size), :] = value[row : row + size]
    half = width // 2
    for column in range(0, width, 256):
        columns = slice(column, column + 256)
        sent[:, columns] = dot(normed_t[:half, :], grad_pre[:, columns]).astype(BF16)
    sent[:, width:] = grad_out[:half, :].astype(BF16)


def product_kernel(normed_t, grad_pre, grad_out, kept):
    width = grad_pre.shape[1]
    half = width // 2
    for column in range(0, width, 256):
        columns = slice(column, column + 256)
        kept[:, columns] = dot(normed_t[half:, :], grad_pre[:, columns])
    kept[:, width:] = grad_out[half:, :]


def backward_kernel(
    grad_pre, hidden_weight, normed, gain, deviation, adj_t,
    grad_gain, inner, below, above,
    product, rows_grad,
):
    members, nodes, width = inner.shape
    points = adj_t.shape[1]
    inverse_gain = 1.0 / gain[...]
    total = jnp.zeros((8, width), F32)
    for member in range(members):
        rows = slice(member * points, (member + 1) * points)
        for column in range(0, width, 256):
            columns = slice(column, column + 256)
            product[:, columns] = dot(grad_pre[rows, :], hidden_weight[columns, :], ((1,), (1,)))

        def step(index, total):
            here = pl.ds(pl.multiple_of(index * 32, 32), 32)
            there = pl.ds(pl.multiple_of(member * points + index * 32, 32), 32)
            value = product[here, :]
            zn = normed[there, :].astype(F32)
            both = value * zn
            scaled = value * gain[...]
            mean = jnp.sum(scaled, axis=1, keepdims=True) * (1.0 / width)
            slant = jnp.sum(both, axis=1, keepdims=True) * (1.0 / width)
            grad = deviation[there, :] * (scaled - mean - (zn * inverse_gain) * slant)
            rows_grad[here, :] = grad.astype(BF16)
            return total + jnp.sum(both.reshape(4, 8, width), axis=0)

        total = lax.fori_loop(0, points // 32, step, total, unroll=4)
        value = dot(adj_t[...], rows_grad[...])
        value = value[:LANES] + value[LANES:]
        below[member] = value[:RIM].astype(BF16)
        inner[member] = value[RIM : RIM + nodes]
        above[member] = value[RIM + nodes : nodes + 2 * RIM].astype(BF16)
    grad_gain[...] = jnp.sum(total, axis=0, keepdims=True) * inverse_gain


def write_half(count, place, half, source, target, wide, sems):
    rows, width = wide.shape
    chunk_rows = rows // 2
    size = chunk_rows >> (count - 1)
    copies = []
    for chunk in range(2):
        mask = jnp.where(half == 0, turn(chunk, count, place[0], 0), turn(chunk, count, place[0], 1))
        for block in range(chunk_rows // size):
            start = chunk * chunk_rows + block * size
            here = slice(start, start + size)
            wide[here, :] = source[here, :width].astype(F32)
            row = half * rows + chunk * chunk_rows + (block ^ mask) * size
            copy = pltpu.make_async_copy(
                wide.at[here, :],
                target.at[pl.ds(pl.multiple_of(row, size), size), :],
                sems.at[start // size],
            )
            copy.start()
            copies.append(copy)
    return copies


def first_write_kernel(count, place, source, target, wide, sems):
    for copy in write_half(count, place, place[1], source, target, wide, sems):
        copy.wait()


def last_write_kernel(count, place, own, source, before, target, grad_out_t, wide, narrow, sems):
    del before
    copies = write_half(count, place, 1 - place[1], source, target, wide, sems)
    half, width = wide.shape
    for row, size, place_row in own_rows(place, count, width):
        here = pl.ds(pl.multiple_of(place_row % half, size), size)
        mine = own[here, width:].astype(F32)
        other = source[here, width:].astype(F32)
        narrow[row : row + size, :] = jnp.where(place_row >= half, mine, other)
    grad_out_t[...] = narrow[...].T[: grad_out_t.shape[0], :]
    for copy in copies:
        copy.wait()


def add_parts(mine, other):
    return (mine.astype(F32) + other.astype(F32)).astype(BF16)


def sum_chunk(value, chunk, count):
    stages = orders(chunk, count)
    for bits in stages[:-1]:
        rows = value.shape[0] // 2
        value = add_parts(value[rows:], swap_bits(value[:rows], bits))
    value = add_parts(value, swap_bits(value, stages[-1]))
    for bits in reversed(stages[:-1]):
        value = jnp.concatenate([swap_bits(value, bits), value])
    return value


def sum_small(value):
    value = value + swap_cores(value)
    for bit in range(lax.axis_size("space").bit_length() - 1):
        value = value + swap_bits(value, (bit, bit))
    return value


def cost(flops, moved):
    return pl.CostEstimate(flops=flops, bytes_accessed=moved, transcendentals=0)


def local(
    latent,
    edge_node_index,
    edge_mask,
    edge_weight,
    valid,
    area,
    state,
    target,
    var_weight,
    gain,
    hidden_weight,
    output_weight,
):
    members, nodes, width = latent.shape
    points, variables = state.shape
    rows = members * points
    count = lax.axis_size("space").bit_length() - 1
    space, core = lax.axis_index("space"), lax.axis_index("member")
    place = jnp.stack([space, core]).astype(jnp.int32)
    low = shift(latent[:, nodes - RIM :], "space", 1)
    high = shift(latent[:, :RIM], "space", -1)
    gain = gain.reshape(1, width)
    output_weight = jnp.pad(output_weight.T, ((0, LANES - variables), (0, 0)))

    adj, adj_t, score_weight = pl.pallas_call(
        adjacency_kernel,
        out_shape=(
            pltpu.VMEM((points, 2 * LANES), BF16),
            pltpu.VMEM((2 * LANES, points), BF16),
            pltpu.VMEM((variables, points), F32),
        ),
        in_specs=[SMEM] + [VMEM] * 6,
        out_specs=(VMEM,) * 3,
        compiler_params=PARAMS,
        name="adjacency",
    )(
        (space * nodes - RIM).astype(jnp.int32).reshape(1),
        edge_node_index.T,
        edge_mask.T,
        edge_weight.T,
        valid.reshape(1, points),
        area.reshape(1, points),
        var_weight.reshape(variables, 1),
    )
    normed, hidden, slope, outputs, deviation = pl.pallas_call(
        forward_kernel,
        out_shape=(
            pltpu.VMEM((rows, width), BF16),
            pltpu.VMEM((rows, width), BF16),
            pltpu.VMEM((rows, width), BF16),
            jax.ShapeDtypeStruct((members, variables, points), F32),
            pltpu.VMEM((rows, 1), F32),
        ),
        in_specs=[VMEM] * 7,
        out_specs=(VMEM,) * 5,
        scratch_shapes=[
            pltpu.VMEM((2 * LANES, width), BF16),
            pltpu.VMEM((points, width), F32),
            pltpu.VMEM((points, LANES), F32),
        ],
        compiler_params=PARAMS,
        name="forward",
    )(adj, low, latent, high, gain, hidden_weight, output_weight)
    others = swap_cores(outputs)
    normed_t = pl.pallas_call(
        lambda *refs: transpose_kernel(count, *refs),
        out_shape=pltpu.VMEM((width, rows), BF16),
        in_specs=[SMEM, VMEM],
        out_specs=VMEM,
        compiler_params=PARAMS,
        cost_estimate=cost(10**9, 4 * 10**6),
        name="transpose",
    )(place, normed)
    loss, grad_pre, grad_out, sent = pl.pallas_call(
        lambda *refs: score_kernel(count, *refs),
        out_shape=(
            jax.ShapeDtypeStruct((1, 1), F32),
            pltpu.VMEM((rows, width), BF16),
            pltpu.VMEM((width, LANES), F32),
            jax.ShapeDtypeStruct((width // 2, width + LANES), BF16),
        ),
        in_specs=[SMEM] + [VMEM] * 9,
        out_specs=(VMEM,) * 4,
        scratch_shapes=[pltpu.VMEM((rows, LANES), BF16), pltpu.VMEM((LANES, rows), F32)],
        compiler_params=PARAMS,
        name="score",
    )(place, outputs, others, state.T, target.T, score_weight, output_weight, slope, hidden, normed_t)
    received = swap_cores(sent)
    kept = pl.pallas_call(
        product_kernel,
        out_shape=jax.ShapeDtypeStruct((width // 2, width + LANES), F32),
        in_specs=[VMEM] * 3,
        out_specs=VMEM,
        compiler_params=PARAMS,
        cost_estimate=cost(2 * 10**9, 4 * 10**6),
        name="product",
    )(normed_t, grad_pre, grad_out)
    value = add_parts(kept, received)
    grad_gain, inner, below, above = pl.pallas_call(
        backward_kernel,
        out_shape=(
            jax.ShapeDtypeStruct((1, width), F32),
            jax.ShapeDtypeStruct((members, nodes, width), F32),
            jax.ShapeDtypeStruct((members, RIM, width), BF16),
            jax.ShapeDtypeStruct((members, RIM, width), BF16),
        ),
        in_specs=[VMEM] * 6,
        out_specs=(VMEM,) * 4,
        scratch_shapes=[pltpu.VMEM((points, width), F32), pltpu.VMEM((points, width), BF16)],
        compiler_params=PARAMS,
        cost_estimate=cost(5 * 10**9, 8 * 10**6),
        name="backward",
    )(grad_pre, hidden_weight, normed, gain, deviation, adj_t)
    small = jnp.concatenate([grad_gain.reshape(width), jnp.broadcast_to(loss.reshape(1), (LANES,))])
    small = sum_small(small)
    from_below, from_above = shift(above, "space", 1), shift(below, "space", -1)
    grad_latent = inner.at[:, :RIM].add(from_below.astype(F32))
    grad_latent = grad_latent.at[:, nodes - RIM :].add(from_above.astype(F32))

    chunk_rows = width // 4
    own = jnp.concatenate(
        [sum_chunk(value[k * chunk_rows : (k + 1) * chunk_rows], k, count) for k in range(2)]
    )
    other = swap_cores(own)
    blocks = 1 << count
    write_scratch = [pltpu.VMEM((width // 2, width), F32), pltpu.SemaphoreType.DMA((blocks,))]
    hidden_shape = jax.ShapeDtypeStruct((width, width), F32)
    grad_hidden = pl.pallas_call(
        lambda *refs: first_write_kernel(count, *refs),
        out_shape=hidden_shape,
        in_specs=[SMEM, VMEM],
        out_specs=pl.BlockSpec(memory_space=pl.ANY),
        scratch_shapes=write_scratch,
        compiler_params=PARAMS,
        cost_estimate=cost(10**6, 3 * 10**6),
        name="first_write",
    )(place, own)
    grad_hidden, grad_out = pl.pallas_call(
        lambda *refs: last_write_kernel(count, *refs),
        out_shape=(hidden_shape, jax.ShapeDtypeStruct((variables, width), F32)),
        in_specs=[SMEM, VMEM, VMEM, pl.BlockSpec(memory_space=pl.ANY)],
        out_specs=(pl.BlockSpec(memory_space=pl.ANY), VMEM),
        scratch_shapes=[write_scratch[0], pltpu.VMEM((width, LANES), F32), write_scratch[1]],
        input_output_aliases={3: 0},
        compiler_params=PARAMS,
        name="last_write",
    )(place, own, other, grad_hidden)
    return (small[width : width + 1], grad_hidden, grad_out.T, small[:width], grad_latent)


def solution(mesh):
    in_specs = (
        P(("groups", "member"), "space", None),
        P(("groups", "space"), None),
        P(("groups", "space"), None),
        P(("groups", "space"), None),
        P(("groups", "space")),
        P(("groups", "space")),
        P(("groups", "space"), None),
        P(("groups", "space"), None),
        P(),
        P(),
        P(),
        P(),
    )
    out_specs = (
        P("groups"),
        P("groups", None),
        P("groups", None),
        P("groups"),
        P(("groups", "member"), "space", None),
    )
    return jax.shard_map(local, mesh=mesh, in_specs=in_specs, out_specs=out_specs, check_vma=False)
```

```python
import jax
import jax.numpy as jnp
from jax import lax
from jax.experimental import pallas as pl
from jax.experimental.pallas import tpu as pltpu
from jax.sharding import PartitionSpec as P

RIM = 16
SMOOTH_SQ = 0.01
LANES = 128
BF16 = jnp.bfloat16
F32 = jnp.float32
VMEM = pl.BlockSpec(memory_space=pltpu.VMEM)
SMEM = pl.BlockSpec(memory_space=pltpu.SMEM)
HBM = pl.BlockSpec(memory_space=pltpu.HBM)
PARAMS = pltpu.CompilerParams(vmem_limit_bytes=16 * 1024 * 1024)


def shift(value, axis, steps):
    count = lax.axis_size(axis)
    first, last = (max(0, -steps), min(count, count - steps))
    return lax.ppermute(value, axis, [(source, source + steps) for source in range(first, last)])


def swap_cores(value):
    return lax.ppermute(value, "member", [(0, 1), (1, 0)])


def swap_bits(value, bits):
    pairs = [
        (s * 2 + c, (s ^ (1 << bits[c])) * 2 + c)
        for s in range(lax.axis_size("space"))
        for c in range(2)
    ]
    return lax.ppermute(value, ("space", "member"), pairs)


def orders(chunk, count):
    first = [[(0, 1), (1, 0), (2, 2)], [(0, 2), (2, 0), (1, 1)]][chunk]
    return first + [(bit, bit) for bit in range(3, count)]


def turn(chunk, count, space, half):
    value = 0
    stages = orders(chunk, count)[:-1]
    for level, bits in enumerate(stages):
        value = value + ((1 - ((space >> bits[half]) & 1)) << (len(stages) - 1 - level))
    return value


def dot(a, b, dims=((1,), (0,))):
    return lax.dot_general(a, b, (dims, ((), ())), preferred_element_type=F32)


def fetch(sources, targets, sems):
    copies = [
        pltpu.make_async_copy(source, target, sems.at[i])
        for i, (source, target) in enumerate(zip(sources, targets))
    ]
    for copy in copies:
        copy.start()
    return copies


def prepare_kernel(
    place, index_in, mask_in, weight_in, valid_in, area_in, var_weight_in, state_in, target_in, projection_in, gain_in,
    adj, adj_t, score_weight, base, projection, gain,
    index, mask, weight, valid, area, var_weight, state, target, narrow, sems,
):
    sources = (
        index_in, mask_in, weight_in, valid_in, area_in, var_weight_in, projection_in, state_in, target_in, gain_in
    )
    targets = (index, mask, weight, valid, area, var_weight, narrow, state, target, gain)
    copies = fetch(sources, targets, sems)
    for copy in copies[:6]:
        copy.wait()
    points = index.shape[1]
    variables = state.shape[0]
    nodes = jax.lax.broadcasted_iota(jnp.int32, (LANES, points), 0) + place[2]
    total = jnp.zeros((LANES, points), F32)
    for slot in range(index.shape[0]):
        coefficient = weight[slot : slot + 1, :] * mask[slot : slot + 1, :].astype(F32)
        total = total + jnp.where(index[slot : slot + 1, :] == nodes, coefficient, 0.0)
    upper = total.astype(BF16).astype(F32)
    lower = total - upper
    adj_t[:LANES, :] = upper.astype(BF16)
    adj_t[LANES:, :] = lower.astype(BF16)
    adj[:, :LANES] = upper.T.astype(BF16)
    adj[:, LANES:] = lower.T.astype(BF16)
    diagonal = jax.lax.broadcasted_iota(jnp.int32, (variables, variables), 0) == (
        jax.lax.broadcasted_iota(jnp.int32, (variables, variables), 1)
    )
    column = jnp.sum(jnp.where(diagonal, var_weight[...], 0.0), axis=1, keepdims=True)
    score_weight[...] = column * (valid[...].astype(F32) * area[...] / points)
    copies[6].wait()
    projection[...] = jnp.zeros_like(projection)
    projection[:variables, :] = narrow[...]
    copies[7].wait()
    copies[8].wait()
    copies[9].wait()
    base[...] = state[...] - target[...]


def forward_kernel(
    adj, low, own_in, high, gain, hidden_weight_in, output_weight,
    normed, hidden, slope, outputs, deviation, extended, summed, projected, own, hidden_weight, sems,
):
    members, nodes, width = own.shape
    points = adj.shape[0]
    tile = 256
    copies = fetch((own_in, hidden_weight_in), (own, hidden_weight), sems)
    copies[0].wait()
    for member in range(members):
        for part in range(2):
            start = part * LANES
            extended[start : start + RIM, :] = low[member]
            extended[start + RIM : start + RIM + nodes, :] = own[member]
            extended[start + RIM + nodes : start + 2 * RIM + nodes, :] = high[member]
            extended[start + 2 * RIM + nodes : start + LANES, :] = jnp.zeros(
                (LANES - 2 * RIM - nodes, width), BF16
            )
        summed[...] = dot(adj[...], extended[...])

        @pl.loop(0, points // 32, unroll=4)
        def _(step):
            rows = pl.ds(pl.multiple_of(step * 32, 32), 32)
            target = pl.ds(pl.multiple_of(member * points + step * 32, 32), 32)
            value = summed[rows, :]
            value = value - jnp.sum(value, axis=1, keepdims=True) * (1.0 / width)
            spread = jnp.sum(value * value, axis=1, keepdims=True) * (1.0 / width)
            inverse = lax.rsqrt(spread + 1e-05)
            deviation[target, :] = inverse
            normed[target, :] = (value * inverse * gain[...]).astype(BF16)

    copies[1].wait()
    for member in range(members):
        rows = slice(member * points, (member + 1) * points)
        for column in range(0, width, tile):
            columns = slice(column, column + tile)
            pre = dot(normed[rows, :], hidden_weight[:, columns])
            sig = 0.5 * jnp.tanh(0.5 * pre) + 0.5
            hid = pre * sig
            slope[rows, columns] = (sig + hid * (1.0 - sig)).astype(BF16)
            hid = hid.astype(BF16)
            hidden[rows, columns] = hid
            term = dot(hid, output_weight[:, columns], ((1,), (1,)))
            if column == 0:
                projected[...] = term
            else:
                projected[...] += term
        outputs[member] = projected[...].T[: outputs.shape[1], :]


def own_rows(place, count, width):
    half_rows, chunk_rows = width // 2, width // 4
    size = chunk_rows >> (count - 1)
    for half in range(2):
        for chunk in range(2):
            mask = turn(chunk, count, place[0], half)
            for block in range(chunk_rows // size):
                row = half * half_rows + chunk * chunk_rows
                start = (1 - (place[1] ^ half)) * half_rows + chunk * chunk_rows
                start = start + (block ^ mask) * size
                yield row + block * size, size, pl.multiple_of(start, size)


def transpose_kernel(count, place, normed, normed_t):
    width = normed.shape[1]
    value = None
    for row, size, target in own_rows(place, count, width):
        if row % LANES == 0:
            value = normed[:, row : row + LANES].T
        offset = row % LANES
        normed_t[pl.ds(target, size), :] = value[offset : offset + size]


def score_kernel(
    count, place, outputs, others, base, score_weight, output_weight, slope, hidden, normed_t,
    loss, grad_pre, grad_out, sent,
    grad_pred, grad_pred_t,
):
    members, variables, points = outputs.shape
    width = hidden.shape[1]
    total = 2 * members
    weight = score_weight[...]
    grad_pred_t[...] = jnp.zeros_like(grad_pred_t)
    grad_pred[...] = jnp.zeros_like(grad_pred)
    values = [outputs[m] for m in range(members)]
    grads = [None] * members
    pair_grads = [jnp.zeros((variables, points), F32) for _ in range(members)]
    errors = jnp.zeros((variables, points), F32)
    pairs = jnp.full((variables, points), members * SMOOTH_SQ**0.5, F32)
    for m in range(members):
        diff = values[m] + base[...]
        square = diff * diff + SMOOTH_SQ
        inverse = lax.rsqrt(square)
        errors = errors + square * inverse
        grads[m] = diff * inverse
        for n in range(m + 1, members):
            diff = values[m] - values[n]
            square = diff * diff + SMOOTH_SQ
            inverse = lax.rsqrt(square)
            pairs = pairs + 2.0 * (square * inverse)
            pair_grads[m] = pair_grads[m] + diff * inverse
            pair_grads[n] = pair_grads[n] - diff * inverse
        for n in range(members):
            diff = values[m] - others[n]
            square = diff * diff + SMOOTH_SQ
            inverse = lax.rsqrt(square)
            pairs = pairs + square * inverse
            pair_grads[m] = pair_grads[m] + diff * inverse
    score = weight * (errors * (1.0 / total) - pairs * (1.0 / (2.0 * total * (total - 1))))
    loss[...] = jnp.sum(jnp.sum(score, axis=0, keepdims=True), axis=1, keepdims=True)
    for m in range(members):
        grad = weight * (grads[m] * (1.0 / total) - pair_grads[m] * (1.0 / (total * (total - 1))))
        columns = slice(m * points, (m + 1) * points)
        grad_pred_t[:variables, columns] = grad
        grad_pred[columns, :] = grad_pred_t[:, columns].T.astype(BF16)
    for m in range(members):
        rows = slice(m * points, (m + 1) * points)
        for column in range(0, width, 256):
            columns = slice(column, column + 256)
            grad_hid = dot(grad_pred[rows, :], output_weight[:, columns])
            grad_pre[rows, columns] = (grad_hid * slope[rows, columns].astype(F32)).astype(BF16)
    value = dot(grad_pred_t[...].astype(BF16), hidden[...]).T
    for row, size, place_row in own_rows(place, count, width):
        grad_out[pl.ds(place_row, size), :] = value[row : row + size]
    half = width // 2
    for column in range(0, width, 256):
        columns = slice(column, column + 256)
        sent[:, columns] = dot(normed_t[:half, :], grad_pre[:, columns]).astype(BF16)
    sent[:, width:] = grad_out[:half, :].astype(BF16)


def product_kernel(normed_t, grad_pre, grad_out, kept):
    width = grad_pre.shape[1]
    half = width // 2
    for column in range(0, width, 256):
        columns = slice(column, column + 256)
        kept[:, columns] = dot(normed_t[half:, :], grad_pre[:, columns])
    kept[:, width:] = grad_out[half:, :]


def backward_kernel(
    grad_pre, hidden_weight_in, normed, gain, deviation, adj_t,
    grad_gain, inner, below, above,
    product, rows_grad, hidden_weight, sems,
):
    members, nodes, width = inner.shape
    points = adj_t.shape[1]
    parts = [pl.ds(column, 256) for column in range(0, width, 256)]
    copies = fetch(
        [hidden_weight_in.at[part, :] for part in parts], [hidden_weight.at[part, :] for part in parts], sems
    )
    inverse_gain = 1.0 / gain[...]
    total = jnp.zeros((8, width), F32)
    for member in range(members):
        rows = slice(member * points, (member + 1) * points)
        for column in range(0, width, 256):
            columns = slice(column, column + 256)
            if member == 0:
                copies[column // 256].wait()
            product[:, columns] = dot(grad_pre[rows, :], hidden_weight[columns, :], ((1,), (1,)))

        def step(index, total):
            here = pl.ds(pl.multiple_of(index * 32, 32), 32)
            there = pl.ds(pl.multiple_of(member * points + index * 32, 32), 32)
            value = product[here, :]
            zn = normed[there, :].astype(F32)
            both = value * zn
            scaled = value * gain[...]
            mean = jnp.sum(scaled, axis=1, keepdims=True) * (1.0 / width)
            slant = jnp.sum(both, axis=1, keepdims=True) * (1.0 / width)
            grad = deviation[there, :] * (scaled - mean - (zn * inverse_gain) * slant)
            rows_grad[here, :] = grad.astype(BF16)
            return total + jnp.sum(both.reshape(4, 8, width), axis=0)

        total = lax.fori_loop(0, points // 32, step, total, unroll=4)
        value = dot(adj_t[...], rows_grad[...])
        value = value[:LANES] + value[LANES:]
        below[member] = value[:RIM].astype(BF16)
        inner[member] = value[RIM : RIM + nodes]
        above[member] = value[RIM + nodes : nodes + 2 * RIM].astype(BF16)
    grad_gain[...] = jnp.sum(total, axis=0, keepdims=True) * inverse_gain


def latent_kernel(inner, from_below, from_above, grad_latent):
    nodes = inner.shape[1]
    grad_latent[...] = inner[...]
    grad_latent[:, :RIM, :] += from_below[...].astype(F32)
    grad_latent[:, nodes - RIM :, :] += from_above[...].astype(F32)


def write_half(count, place, half, source, target, wide, sems):
    rows, width = wide.shape
    chunk_rows = rows // 2
    size = chunk_rows >> (count - 1)
    copies = []
    for chunk in range(2):
        mask = jnp.where(half == 0, turn(chunk, count, place[0], 0), turn(chunk, count, place[0], 1))
        for block in range(chunk_rows // size):
            start = chunk * chunk_rows + block * size
            here = slice(start, start + size)
            wide[here, :] = source[here, :width].astype(F32)
            row = half * rows + chunk * chunk_rows + (block ^ mask) * size
            copy = pltpu.make_async_copy(
                wide.at[here, :],
                target.at[pl.ds(pl.multiple_of(row, size), size), :],
                sems.at[start // size],
            )
            copy.start()
            copies.append(copy)
    return copies


def first_write_kernel(count, place, source, target, wide, sems):
    for copy in write_half(count, place, place[1], source, target, wide, sems):
        copy.wait()


def last_write_kernel(count, place, own, source, before, target, grad_out_t, wide, narrow, sems):
    del before
    copies = write_half(count, place, 1 - place[1], source, target, wide, sems)
    half, width = wide.shape
    for row, size, place_row in own_rows(place, count, width):
        here = pl.ds(pl.multiple_of(place_row % half, size), size)
        mine = own[here, width:].astype(F32)
        other = source[here, width:].astype(F32)
        narrow[row : row + size, :] = jnp.where(place_row >= half, mine, other)
    grad_out_t[...] = narrow[...].T[: grad_out_t.shape[0], :]
    for copy in copies:
        copy.wait()


def add_parts(mine, other):
    return (mine.astype(F32) + other.astype(F32)).astype(BF16)


def swap_with(value, small, bits):
    upper = small.astype(BF16)
    lower = (small - upper.astype(F32)).astype(BF16)
    rest = jnp.zeros((6, small.shape[1]), BF16)
    other = swap_bits(jnp.concatenate([value, upper, lower, rest]), bits)
    rows = value.shape[0]
    mine = upper.astype(F32) + lower.astype(F32)
    small = mine + (other[rows : rows + 1].astype(F32) + other[rows + 1 : rows + 2].astype(F32))
    return other[:rows], small


def sum_chunk(value, chunk, count, small=None, beside=()):
    stages = orders(chunk, count)
    for level, bits in enumerate(stages):
        rows = value.shape[0] // 2 if level < count - 1 else 0
        sent = value[:rows] if rows else value
        if small is None or level == 0:
            other = swap_bits(sent, bits)
        else:
            other, small = swap_with(sent, small, bits)
        value = add_parts(value[rows:], other)
    for level, bits in reversed(list(enumerate(stages[:-1]))):
        if level == 0:
            value, beside = lax.optimization_barrier((value, beside))
        if small is None or level > 0:
            other = swap_bits(value, bits)
        else:
            other, small = swap_with(value, small, bits)
        value = jnp.concatenate([other, value])
    return value, small, beside


def in_hbm(*values):
    return [pltpu.with_memory_space_constraint(value, pltpu.HBM) for value in values]


def cost(flops, moved):
    return pl.CostEstimate(flops=flops, bytes_accessed=moved, transcendentals=0)


def local(
    latent,
    edge_node_index,
    edge_mask,
    edge_weight,
    valid,
    area,
    state,
    target,
    var_weight,
    gain,
    hidden_weight,
    output_weight,
):
    members, nodes, width = latent.shape
    points, variables = state.shape
    rows = members * points
    count = lax.axis_size("space").bit_length() - 1
    space, core = lax.axis_index("space"), lax.axis_index("member")
    place = jnp.stack([space, core, space * nodes - RIM]).astype(jnp.int32)
    low = shift(latent[:, nodes - RIM :], "space", 1)
    high = shift(latent[:, :RIM], "space", -1)
    adj, adj_t, score_weight, base, projection, gain = pl.pallas_call(
        prepare_kernel,
        out_shape=(
            pltpu.VMEM((points, 2 * LANES), BF16),
            pltpu.VMEM((2 * LANES, points), BF16),
            pltpu.VMEM((variables, points), F32),
            pltpu.VMEM((variables, points), F32),
            pltpu.VMEM((LANES, width), BF16),
            pltpu.VMEM((1, width), F32),
        ),
        in_specs=[SMEM] + [HBM] * 10,
        out_specs=(VMEM,) * 6,
        scratch_shapes=[
            pltpu.VMEM(edge_mask.T.shape, jnp.int32),
            pltpu.VMEM(edge_mask.T.shape, jnp.int32),
            pltpu.VMEM(edge_mask.T.shape, F32),
            pltpu.VMEM((1, points), jnp.int32),
            pltpu.VMEM((1, points), F32),
            pltpu.VMEM((1, variables), F32),
            pltpu.VMEM((variables, points), F32),
            pltpu.VMEM((variables, points), F32),
            pltpu.VMEM((variables, width), BF16),
            pltpu.SemaphoreType.DMA((10,)),
        ],
        compiler_params=PARAMS,
        name="prepare",
    )(
        place,
        *in_hbm(
            edge_node_index.T,
            edge_mask.T,
            edge_weight.T,
            valid.reshape(1, points),
            area.reshape(1, points),
            var_weight.reshape(1, variables),
            state.T,
            target.T,
            output_weight.T,
            gain.reshape(1, width),
        ),
    )
    normed, hidden, slope, outputs, deviation = pl.pallas_call(
        forward_kernel,
        out_shape=(
            pltpu.VMEM((rows, width), BF16),
            pltpu.VMEM((rows, width), BF16),
            pltpu.VMEM((rows, width), BF16),
            jax.ShapeDtypeStruct((members, variables, points), F32),
            pltpu.VMEM((rows, 1), F32),
        ),
        in_specs=[VMEM, VMEM, HBM, VMEM, VMEM, HBM, VMEM],
        out_specs=(VMEM,) * 5,
        scratch_shapes=[
            pltpu.VMEM((2 * LANES, width), BF16),
            pltpu.VMEM((points, width), F32),
            pltpu.VMEM((points, LANES), F32),
            pltpu.VMEM(latent.shape, BF16),
            pltpu.VMEM((width, width), BF16),
            pltpu.SemaphoreType.DMA((2,)),
        ],
        compiler_params=PARAMS,
        name="forward",
    )(adj, low, *in_hbm(latent), high, gain, *in_hbm(hidden_weight), projection)
    others = swap_cores(outputs)
    normed_t = pl.pallas_call(
        lambda *refs: transpose_kernel(count, *refs),
        out_shape=pltpu.VMEM((width, rows), BF16),
        in_specs=[SMEM, VMEM],
        out_specs=VMEM,
        compiler_params=PARAMS,
        cost_estimate=cost(10**9, 4 * 10**6),
        name="transpose",
    )(place, normed)
    loss, grad_pre, grad_out, sent = pl.pallas_call(
        lambda *refs: score_kernel(count, *refs),
        out_shape=(
            jax.ShapeDtypeStruct((1, 1), F32),
            pltpu.VMEM((rows, width), BF16),
            pltpu.VMEM((width, LANES), F32),
            jax.ShapeDtypeStruct((width // 2, width + LANES), BF16),
        ),
        in_specs=[SMEM] + [VMEM] * 8,
        out_specs=(VMEM,) * 4,
        scratch_shapes=[pltpu.VMEM((rows, LANES), BF16), pltpu.VMEM((LANES, rows), F32)],
        compiler_params=PARAMS,
        name="score",
    )(place, outputs, others, base, score_weight, projection, slope, hidden, normed_t)
    received = swap_cores(sent)
    kept = pl.pallas_call(
        product_kernel,
        out_shape=jax.ShapeDtypeStruct((width // 2, width + LANES), F32),
        in_specs=[VMEM] * 3,
        out_specs=VMEM,
        compiler_params=PARAMS,
        cost_estimate=cost(2 * 10**9, 4 * 10**6),
        name="product",
    )(normed_t, grad_pre, grad_out)
    value = add_parts(kept, received)
    grad_gain, inner, below, above = pl.pallas_call(
        backward_kernel,
        out_shape=(
            jax.ShapeDtypeStruct((1, width), F32),
            pltpu.VMEM((members, nodes, width), F32),
            jax.ShapeDtypeStruct((members, RIM, width), BF16),
            jax.ShapeDtypeStruct((members, RIM, width), BF16),
        ),
        in_specs=[VMEM, HBM] + [VMEM] * 4,
        out_specs=(VMEM,) * 4,
        scratch_shapes=[
            pltpu.VMEM((points, width), F32),
            pltpu.VMEM((points, width), BF16),
            pltpu.VMEM((width, width), BF16),
            pltpu.SemaphoreType.DMA((width // 256,)),
        ],
        compiler_params=PARAMS,
        cost_estimate=cost(5 * 10**9, 8 * 10**6),
        name="backward",
    )(grad_pre, *in_hbm(hidden_weight), normed, gain, deviation, adj_t)
    small = jnp.concatenate([grad_gain, jnp.broadcast_to(loss, (1, LANES))], axis=1)
    rims = (shift(above, "space", 1), shift(below, "space", -1))
    chunk_rows = width // 4
    first, small, _ = sum_chunk(value[:chunk_rows], 0, count, small)
    second, _, rims = sum_chunk(value[chunk_rows:], 1, count, beside=rims)
    grad_latent = pl.pallas_call(
        latent_kernel,
        out_shape=jax.ShapeDtypeStruct((members, nodes, width), F32),
        in_specs=[VMEM] * 3,
        out_specs=VMEM,
        compiler_params=PARAMS,
        cost_estimate=cost(10**6, 10**6),
        name="latent",
    )(inner, *rims)
    own = jnp.concatenate([first, second])
    small = (small + swap_cores(small)).reshape(width + LANES)
    other = swap_cores(own)
    blocks = 1 << count
    write_scratch = [pltpu.VMEM((width // 2, width), F32), pltpu.SemaphoreType.DMA((blocks,))]
    hidden_shape = jax.ShapeDtypeStruct((width, width), F32)
    grad_hidden = pl.pallas_call(
        lambda *refs: first_write_kernel(count, *refs),
        out_shape=hidden_shape,
        in_specs=[SMEM, VMEM],
        out_specs=pl.BlockSpec(memory_space=pl.ANY),
        scratch_shapes=write_scratch,
        compiler_params=PARAMS,
        cost_estimate=cost(10**6, 3 * 10**6),
        name="first_write",
    )(place, own)
    grad_hidden, grad_out = pl.pallas_call(
        lambda *refs: last_write_kernel(count, *refs),
        out_shape=(hidden_shape, jax.ShapeDtypeStruct((variables, width), F32)),
        in_specs=[SMEM, VMEM, VMEM, pl.BlockSpec(memory_space=pl.ANY)],
        out_specs=(pl.BlockSpec(memory_space=pl.ANY), VMEM),
        scratch_shapes=[write_scratch[0], pltpu.VMEM((width, LANES), F32), write_scratch[1]],
        input_output_aliases={3: 0},
        compiler_params=PARAMS,
        name="last_write",
    )(place, own, other, grad_hidden)
    return (small[width : width + 1], grad_hidden, grad_out.T, small[:width], grad_latent)


def solution(mesh):
    in_specs = (
        P(("groups", "member"), "space", None),
        P(("groups", "space"), None),
        P(("groups", "space"), None),
        P(("groups", "space"), None),
        P(("groups", "space")),
        P(("groups", "space")),
        P(("groups", "space"), None),
        P(("groups", "space"), None),
        P(),
        P(),
        P(),
        P(),
    )
    out_specs = (
        P("groups"),
        P("groups", None),
        P("groups", None),
        P("groups"),
        P(("groups", "member"), "space", None),
    )
    return jax.shard_map(local, mesh=mesh, in_specs=in_specs, out_specs=out_specs, check_vma=False)
```

```python
import jax
import jax.numpy as jnp
from jax import lax
from jax.experimental import pallas as pl
from jax.experimental.pallas import tpu as pltpu
from jax.sharding import PartitionSpec as P

RIM = 16
SMOOTH_SQ = 0.01
LANES = 128
BF16 = jnp.bfloat16
F32 = jnp.float32
VMEM = pl.BlockSpec(memory_space=pltpu.VMEM)
SMEM = pl.BlockSpec(memory_space=pltpu.SMEM)
HBM = pl.BlockSpec(memory_space=pltpu.HBM)
PARAMS = pltpu.CompilerParams(vmem_limit_bytes=16 * 1024 * 1024)


def shift(value, axis, steps):
    count = lax.axis_size(axis)
    first, last = (max(0, -steps), min(count, count - steps))
    return lax.ppermute(value, axis, [(source, source + steps) for source in range(first, last)])


def swap_cores(value):
    return lax.ppermute(value, "member", [(0, 1), (1, 0)])


def swap_bits(value, bits):
    pairs = [
        (s * 2 + c, (s ^ (1 << bits[c])) * 2 + c)
        for s in range(lax.axis_size("space"))
        for c in range(2)
    ]
    return lax.ppermute(value, ("space", "member"), pairs)


def orders(count):
    return [(0, 1), (1, 0)] + [(bit, bit) for bit in range(2, count)]


def turn(count, space, half):
    value = 0
    stages = orders(count)[:-1]
    for level, bits in enumerate(stages):
        value = value + ((1 - ((space >> bits[half]) & 1)) << (len(stages) - 1 - level))
    return value


def dot(a, b, dims=((1,), (0,))):
    return lax.dot_general(a, b, (dims, ((), ())), preferred_element_type=F32)


def fetch(sources, targets, sems):
    copies = [
        pltpu.make_async_copy(source, target, sems.at[i])
        for i, (source, target) in enumerate(zip(sources, targets))
    ]
    for copy in copies:
        copy.start()
    return copies


def prepare_kernel(
    place, index_in, mask_in, weight_in, valid_in, area_in, var_weight_in, state_in, target_in, projection_in, gain_in, hidden_weight_in,
    own_in, adj, adj_t, score_weight, base, projection, gain, hidden_weight, own,
    index, mask, weight, valid, area, var_weight, state, target, narrow, sems,
):
    sources = (
        index_in, mask_in, weight_in, valid_in, area_in, var_weight_in, projection_in, state_in, target_in, gain_in,
        hidden_weight_in, own_in,
    )
    targets = (index, mask, weight, valid, area, var_weight, narrow, state, target, gain, hidden_weight, own)
    copies = fetch(sources, targets, sems)
    for copy in copies[:6]:
        copy.wait()
    points = index.shape[1]
    variables = state.shape[0]
    nodes = jax.lax.broadcasted_iota(jnp.int32, (LANES, points), 0) + place[2]
    total = jnp.zeros((LANES, points), F32)
    for slot in range(index.shape[0]):
        coefficient = weight[slot : slot + 1, :] * mask[slot : slot + 1, :].astype(F32)
        total = total + jnp.where(index[slot : slot + 1, :] == nodes, coefficient, 0.0)
    upper = total.astype(BF16).astype(F32)
    lower = total - upper
    adj_t[:LANES, :] = upper.astype(BF16)
    adj_t[LANES:, :] = lower.astype(BF16)
    adj[:, :LANES] = upper.T.astype(BF16)
    adj[:, LANES:] = lower.T.astype(BF16)
    diagonal = jax.lax.broadcasted_iota(jnp.int32, (variables, variables), 0) == (
        jax.lax.broadcasted_iota(jnp.int32, (variables, variables), 1)
    )
    column = jnp.sum(jnp.where(diagonal, var_weight[...], 0.0), axis=1, keepdims=True)
    score_weight[...] = column * (valid[...].astype(F32) * area[...] / points)
    copies[6].wait()
    projection[...] = jnp.zeros_like(projection)
    projection[:variables, :] = narrow[...]
    copies[7].wait()
    copies[8].wait()
    base[...] = state[...] - target[...]
    for copy in copies[9:]:
        copy.wait()


def forward_kernel(
    adj, low, own, high, gain, hidden_weight, output_weight,
    normed, hidden, slope, outputs, deviation, extended, summed, projected,
):
    members, nodes, width = own.shape
    points = adj.shape[0]
    tile = 256
    for member in range(members):
        for part in range(2):
            start = part * LANES
            extended[member, start : start + RIM, :] = low[member]
            extended[member, start + RIM : start + RIM + nodes, :] = own[member]
            extended[member, start + RIM + nodes : start + 2 * RIM + nodes, :] = high[member]
            extended[member, start + 2 * RIM + nodes : start + LANES, :] = jnp.zeros(
                (LANES - 2 * RIM - nodes, width), BF16
            )

    def gather(member):
        summed[member] = dot(adj[...], extended[member])

    def norm(member, first, size):
        for row in range(first, first + size, 32):
            value = summed[member, row : row + 32, :]
            value = value - jnp.sum(value, axis=1, keepdims=True) * (1.0 / width)
            spread = jnp.sum(value * value, axis=1, keepdims=True) * (1.0 / width)
            inverse = lax.rsqrt(spread + 1e-05)
            target = slice(member * points + row, member * points + row + 32)
            deviation[target, :] = inverse
            normed[target, :] = (value * inverse * gain[...]).astype(BF16)

    def layer(member, column):
        rows = slice(member * points, (member + 1) * points)
        columns = slice(column, column + tile)
        pre = dot(normed[rows, :], hidden_weight[:, columns])
        sig = 0.5 * jnp.tanh(0.5 * pre) + 0.5
        hid = pre * sig
        slope[rows, columns] = (sig + hid * (1.0 - sig)).astype(BF16)
        hid = hid.astype(BF16)
        hidden[rows, columns] = hid
        term = dot(hid, output_weight[:, columns], ((1,), (1,)))
        if column == 0:
            projected[...] = term
        else:
            projected[...] += term

    gather(0)
    norm(0, 0, points)
    for member in range(members):
        if member + 1 < members:
            gather(member + 1)
        for column in range(0, width, tile):
            if member + 1 < members:
                size = points * tile // width
                norm(member + 1, points * column // width, size)
            layer(member, column)
        outputs[member] = projected[...].T[: outputs.shape[1], :]


def own_rows(place, count, width):
    half_rows, chunk_rows = width // 2, width // 4
    size = chunk_rows >> (count - 1)
    for half in range(2):
        for chunk in range(2):
            mask = turn(count, place[0], half)
            for block in range(chunk_rows // size):
                row = half * half_rows + chunk * chunk_rows
                start = (1 - (place[1] ^ half)) * half_rows + chunk * chunk_rows
                start = start + (block ^ mask) * size
                yield row + block * size, size, pl.multiple_of(start, size)


def narrow_rows(place, count, width):
    chunk_rows = width // 4
    size = chunk_rows >> (count - 1)
    for half in range(2):
        mask = turn(count, place[0], half)
        for block in range(chunk_rows // size):
            row = half * 2 * chunk_rows + block * 2 * size
            yield (row, row + size), size, 1 - (place[1] ^ half), pl.multiple_of((block ^ mask) * size, size)


def transpose_kernel(count, place, normed, normed_t):
    width = normed.shape[1]
    value = None
    for row, size, target in own_rows(place, count, width):
        if row % LANES == 0:
            value = normed[:, row : row + LANES].T
        offset = row % LANES
        normed_t[pl.ds(target, size), :] = value[offset : offset + size]


def score_kernel(
    place, outputs, others, base, score_weight, output_weight, slope, normed_t,
    loss, grad_pre, grad_pred_t, sent,
    grad_pred, grad_wide,
):
    members, variables, points = outputs.shape
    width = slope.shape[1]
    total = 2 * members
    weight = score_weight[...]
    grad_wide[...] = jnp.zeros_like(grad_wide)
    grad_pred[...] = jnp.zeros_like(grad_pred)
    values = [outputs[m] for m in range(members)]
    grads = [None] * members
    pair_grads = [jnp.zeros((variables, points), F32) for _ in range(members)]
    errors = jnp.zeros((variables, points), F32)
    pairs = jnp.full((variables, points), members * SMOOTH_SQ**0.5, F32)
    for m in range(members):
        diff = values[m] + base[...]
        square = diff * diff + SMOOTH_SQ
        inverse = lax.rsqrt(square)
        errors = errors + square * inverse
        grads[m] = diff * inverse
        for n in range(m + 1, members):
            diff = values[m] - values[n]
            square = diff * diff + SMOOTH_SQ
            inverse = lax.rsqrt(square)
            pairs = pairs + 2.0 * (square * inverse)
            pair_grads[m] = pair_grads[m] + diff * inverse
            pair_grads[n] = pair_grads[n] - diff * inverse
        for n in range(members):
            diff = values[m] - others[n]
            square = diff * diff + SMOOTH_SQ
            inverse = lax.rsqrt(square)
            pairs = pairs + square * inverse
            pair_grads[m] = pair_grads[m] + diff * inverse
    score = weight * (errors * (1.0 / total) - pairs * (1.0 / (2.0 * total * (total - 1))))
    loss[...] = jnp.sum(jnp.sum(score, axis=0, keepdims=True), axis=1, keepdims=True)
    for m in range(members):
        grad = weight * (grads[m] * (1.0 / total) - pair_grads[m] * (1.0 / (total * (total - 1))))
        columns = slice(m * points, (m + 1) * points)
        grad_wide[:variables, columns] = grad
        grad_pred[columns, :] = grad_wide[:, columns].T.astype(BF16)
    grad_pred_t[...] = grad_wide[...].astype(BF16)
    for m in range(members):
        rows = slice(m * points, (m + 1) * points)
        for column in range(0, width, 256):
            columns = slice(column, column + 256)
            grad_hid = dot(grad_pred[rows, :], output_weight[:, columns])
            grad_pre[rows, columns] = (grad_hid * slope[rows, columns].astype(F32)).astype(BF16)
    products(normed_t, grad_pre, slice(width // 4, width // 2), sent)


def products(normed_t, grad_pre, rows, target):
    width = grad_pre.shape[1]
    for column in range(0, width, 256):
        columns = slice(column, column + 256)
        target[:, columns] = dot(normed_t[rows, :], grad_pre[:, columns]).astype(target.dtype)


def sent_kernel(count, place, normed_t, grad_pre, grad_pred_t, hidden, sent, kept_narrow):
    width = grad_pre.shape[1]
    products(normed_t, grad_pre, slice(0, width // 4), sent)
    value = dot(grad_pred_t[...], hidden[...]).T
    for rows, size, own, place_row in narrow_rows(place, count, width):
        here = pl.ds(place_row, size)
        for side, row in enumerate(rows):
            part = value[row : row + size]
            start = width + side * LANES

            @pl.when(own == 1)
            def _():
                kept_narrow[here, side * LANES : (side + 1) * LANES] = part

            @pl.when(own == 0)
            def _():
                sent[here, start : start + LANES] = part.astype(BF16)


def kept_kernel(normed_t, grad_pre, *refs):
    width = grad_pre.shape[1]
    kept = refs[-1]
    if len(refs) == 1:
        products(normed_t, grad_pre, slice(3 * width // 4, width), kept)
    else:
        products(normed_t, grad_pre, slice(width // 2, 3 * width // 4), kept)
        kept[:, width:] = refs[0][...]


def backward_kernel(member, grad_pre, hidden_weight, normed, gain, deviation, adj_t, *refs):
    before, (small, inner, below, above, product, rows_grad) = refs[:-6], refs[-6:]
    nodes, width = inner.shape
    points = adj_t.shape[1]
    inverse_gain = 1.0 / gain[...]
    for column in range(0, width, 256):
        columns = slice(column, column + 256)
        product[:, columns] = dot(
            grad_pre[member * points : (member + 1) * points, :], hidden_weight[columns, :], ((1,), (1,))
        )

    def step(index, total):
        here = pl.ds(pl.multiple_of(index * 32, 32), 32)
        there = pl.ds(pl.multiple_of(member * points + index * 32, 32), 32)
        value = product[here, :]
        zn = normed[there, :].astype(F32)
        both = value * zn
        scaled = value * gain[...]
        mean = jnp.sum(scaled, axis=1, keepdims=True) * (1.0 / width)
        slant = jnp.sum(both, axis=1, keepdims=True) * (1.0 / width)
        grad = deviation[there, :] * (scaled - mean - (zn * inverse_gain) * slant)
        rows_grad[here, :] = grad.astype(BF16)
        return total + jnp.sum(both.reshape(4, 8, width), axis=0)

    total = before[0][...] if before else jnp.zeros((8, width), F32)
    total = lax.fori_loop(0, points // 32, step, total, unroll=4)
    value = dot(adj_t[...], rows_grad[...])
    value = value[:LANES] + value[LANES:]
    below[...] = value[:RIM].astype(BF16)
    inner[...] = value[RIM : RIM + nodes]
    above[...] = value[RIM + nodes : nodes + 2 * RIM].astype(BF16)
    if not before:
        small[...] = total
        return
    row = jnp.concatenate(
        [
            jnp.sum(total, axis=0, keepdims=True) * inverse_gain,
            jnp.broadcast_to(before[1][...], (1, 2 * LANES)),
        ],
        axis=1,
    )
    upper = row.astype(BF16).astype(F32)
    index = jax.lax.broadcasted_iota(jnp.int32, (8, row.shape[1]), 0)
    small[...] = jnp.where(index == 0, upper, jnp.where(index == 1, row - upper, 0.0)).astype(BF16)


def latent_kernel(*refs):
    grad_latent = refs[-1]
    members, nodes = grad_latent.shape[:2]
    inner, (from_below, from_above) = refs[:members], refs[members:-1]
    for member in range(members):
        grad_latent[member] = inner[member][...]
    grad_latent[:, :RIM, :] += from_below[...].astype(F32)
    grad_latent[:, nodes - RIM :, :] += from_above[...].astype(F32)


def write_rows(count, chunk, side, place, source, target, wide, start, sems):
    chunk_rows, width = source.shape[0], target.shape[1]
    size = chunk_rows >> (count - 1)
    half = place[1] ^ side
    mask = jnp.where(half == 0, turn(count, place[0], 0), turn(count, place[0], 1))
    copies = []
    for block in range(chunk_rows // size):
        here = slice(block * size, (block + 1) * size)
        there = slice(start + block * size, start + (block + 1) * size)
        wide[there, :] = source[here, :width].astype(F32)
        row = (half * 2 + chunk) * chunk_rows + (block ^ mask) * size
        copy = pltpu.make_async_copy(
            wide.at[there, :],
            target.at[pl.ds(pl.multiple_of(row, size), size), :],
            sems.at[start // size + block],
        )
        copy.start()
        copies.append(copy)
    return copies


def write_kernel(count, place, second, other_second, first, target, wide, sems):
    rows = first.shape[0]
    copies = write_rows(count, 1, 0, place, second, target, wide, 0, sems)
    copies += write_rows(count, 1, 1, place, other_second, target, wide, rows, sems)
    copies += write_rows(count, 0, 0, place, first, target, wide, 2 * rows, sems)
    for copy in copies:
        copy.wait()


def last_write_kernel(
    count, place, own, other, small, other_small, before,
    target, grad_out_t, grad_gain, loss,
    wide, narrow, narrow_t, gain_row, loss_cell, sems, last_sems,
):
    del before
    copies = write_rows(count, 0, 1, place, other, target, wide, 0, sems)
    width = target.shape[1]
    for rows, size, mine, place_row in narrow_rows(place, count, width):
        here = pl.ds(place_row, size)
        for side, row in enumerate(rows):
            lanes = slice(width + side * LANES, width + (side + 1) * LANES)
            value = jnp.where(mine == 1, own[here, lanes].astype(F32), other[here, lanes].astype(F32))
            narrow[row : row + size, :] = value
    narrow_t[...] = narrow[...].T[: grad_out_t.shape[0], :]
    total = small[...].astype(F32) + other_small[...].astype(F32)
    total = total[:1] + total[1:2]
    gain_row[...] = total[:, :width]
    loss_cell[...] = total[:, width : width + 1]
    copies += fetch((narrow_t, gain_row, loss_cell), (grad_out_t, grad_gain, loss), last_sems)
    for copy in copies:
        copy.wait()


def add_parts(mine, other):
    return (mine.astype(F32) + other.astype(F32)).astype(BF16)


def unpack(small):
    return small[:1].astype(F32) + small[1:2].astype(F32)


def swap_with(value, small, bits):
    rows = value.shape[0]
    other = swap_bits(jnp.concatenate([value, small]), bits)
    total = unpack(small) + unpack(other[rows:])
    upper = total.astype(BF16)
    lower = (total - upper.astype(F32)).astype(BF16)
    rest = jnp.zeros((small.shape[0] - 2, small.shape[1]), BF16)
    return other[:rows], jnp.concatenate([upper, lower, rest])


def first_stage(value, count):
    rows = value.shape[0] // 2
    return value[:rows], swap_bits(value[:rows], orders(count)[0]), value[rows:]


def next_stages(value, count, small=None):
    stages = orders(count)
    for level, bits in list(enumerate(stages))[1:]:
        rows = value.shape[0] // 2 if level < count - 1 else 0
        sent = value[:rows] if rows else value
        if small is None:
            other = swap_bits(sent, bits)
        else:
            other, small = swap_with(sent, small, bits)
        value = add_parts(value[rows:], other)
    for bits in reversed(stages[1:-1]):
        value = jnp.concatenate([swap_bits(value, bits), value])
    return value, small


def after(value, *others):
    return lax.optimization_barrier((value, *others))[0]


def in_hbm(*values):
    return [pltpu.with_memory_space_constraint(value, pltpu.HBM) for value in values]


def cost(flops, moved):
    return pl.CostEstimate(flops=flops, bytes_accessed=moved, transcendentals=0)


def local(
    latent,
    edge_node_index,
    edge_mask,
    edge_weight,
    valid,
    area,
    state,
    target,
    var_weight,
    gain,
    hidden_weight,
    output_weight,
):
    members, nodes, width = latent.shape
    points, variables = state.shape
    rows = members * points
    count = lax.axis_size("space").bit_length() - 1
    space, core = lax.axis_index("space"), lax.axis_index("member")
    place = jnp.stack([space, core, space * nodes - RIM]).astype(jnp.int32)
    low = shift(latent[:, nodes - RIM :], "space", 1)
    high = shift(latent[:, :RIM], "space", -1)
    adj, adj_t, score_weight, base, projection, gain, hidden_weight, own = pl.pallas_call(
        prepare_kernel,
        out_shape=(
            pltpu.VMEM((points, 2 * LANES), BF16),
            pltpu.VMEM((2 * LANES, points), BF16),
            pltpu.VMEM((variables, points), F32),
            pltpu.VMEM((variables, points), F32),
            pltpu.VMEM((LANES, width), BF16),
            pltpu.VMEM((1, width), F32),
            pltpu.VMEM((width, width), BF16),
            pltpu.VMEM(latent.shape, BF16),
        ),
        in_specs=[SMEM] + [HBM] * 12,
        out_specs=(VMEM,) * 8,
        scratch_shapes=[
            pltpu.VMEM(edge_mask.T.shape, jnp.int32),
            pltpu.VMEM(edge_mask.T.shape, jnp.int32),
            pltpu.VMEM(edge_mask.T.shape, F32),
            pltpu.VMEM((1, points), jnp.int32),
            pltpu.VMEM((1, points), F32),
            pltpu.VMEM((1, variables), F32),
            pltpu.VMEM((variables, points), F32),
            pltpu.VMEM((variables, points), F32),
            pltpu.VMEM((variables, width), BF16),
            pltpu.SemaphoreType.DMA((12,)),
        ],
        compiler_params=PARAMS,
        name="prepare",
    )(
        place,
        *in_hbm(
            edge_node_index.T,
            edge_mask.T,
            edge_weight.T,
            valid.reshape(1, points),
            area.reshape(1, points),
            var_weight.reshape(1, variables),
            state.T,
            target.T,
            output_weight.T,
            gain.reshape(1, width),
            hidden_weight,
            latent,
        ),
    )
    normed, hidden, slope, outputs, deviation = pl.pallas_call(
        forward_kernel,
        out_shape=(
            pltpu.VMEM((rows, width), BF16),
            pltpu.VMEM((rows, width), BF16),
            pltpu.VMEM((rows, width), BF16),
            jax.ShapeDtypeStruct((members, variables, points), F32),
            pltpu.VMEM((rows, 1), F32),
        ),
        in_specs=[VMEM] * 7,
        out_specs=(VMEM,) * 5,
        scratch_shapes=[
            pltpu.VMEM((members, 2 * LANES, width), BF16),
            pltpu.VMEM((members, points, width), F32),
            pltpu.VMEM((points, LANES), F32),
        ],
        compiler_params=PARAMS,
        name="forward",
    )(adj, low, own, high, gain, hidden_weight, projection)
    others = swap_cores(outputs)
    normed_t = pl.pallas_call(
        lambda *refs: transpose_kernel(count, *refs),
        out_shape=pltpu.VMEM((width, rows), BF16),
        in_specs=[SMEM, VMEM],
        out_specs=VMEM,
        compiler_params=PARAMS,
        cost_estimate=cost(10**9, 4 * 10**6),
        name="transpose",
    )(place, normed)
    chunk_rows = width // 4
    loss, grad_pre, grad_pred_t, sent_second = pl.pallas_call(
        score_kernel,
        out_shape=(
            jax.ShapeDtypeStruct((1, 1), F32),
            pltpu.VMEM((rows, width), BF16),
            pltpu.VMEM((LANES, rows), BF16),
            jax.ShapeDtypeStruct((chunk_rows, width), BF16),
        ),
        in_specs=[SMEM] + [VMEM] * 7,
        out_specs=(VMEM,) * 4,
        scratch_shapes=[pltpu.VMEM((rows, LANES), BF16), pltpu.VMEM((LANES, rows), F32)],
        compiler_params=PARAMS,
        name="score",
    )(place, outputs, others, base, score_weight, projection, slope, normed_t)
    received_second = swap_cores(sent_second)
    kept = lambda normed_t, grad_pre, *narrow: pl.pallas_call(
        kept_kernel,
        out_shape=jax.ShapeDtypeStruct((chunk_rows, width + 2 * LANES * len(narrow)), F32),
        in_specs=[VMEM] * (2 + len(narrow)),
        out_specs=VMEM,
        compiler_params=PARAMS,
        cost_estimate=cost(10**9, 2 * 10**6),
        name="kept",
    )(normed_t, grad_pre, *narrow)
    second = add_parts(kept(normed_t, grad_pre), received_second)
    second_sent, second_other, second = first_stage(second, count)
    sent_first, kept_narrow = pl.pallas_call(
        lambda *refs: sent_kernel(count, *refs),
        out_shape=(
            jax.ShapeDtypeStruct((chunk_rows, width + 2 * LANES), BF16),
            pltpu.VMEM((chunk_rows, 2 * LANES), F32),
        ),
        in_specs=[SMEM] + [VMEM] * 4,
        out_specs=(VMEM,) * 2,
        compiler_params=PARAMS,
        cost_estimate=cost(10**9, 4 * 10**6),
        name="sent",
    )(place, normed_t, grad_pre, after(grad_pred_t, second_sent), hidden)
    first = add_parts(kept(normed_t, grad_pre, kept_narrow), swap_cores(sent_first))
    first_sent, first_other, first = first_stage(first, count)

    def backward(member, adj_t, *before):
        last = len(before) > 0
        return pl.pallas_call(
            lambda *refs: backward_kernel(member, *refs),
            out_shape=(
                jax.ShapeDtypeStruct((8, width + 2 * LANES), BF16) if last else pltpu.VMEM((8, width), F32),
                pltpu.VMEM((nodes, width), F32),
                jax.ShapeDtypeStruct((RIM, width), BF16),
                jax.ShapeDtypeStruct((RIM, width), BF16),
            ),
            in_specs=[VMEM] * (6 + len(before)),
            out_specs=(VMEM,) * 4,
            scratch_shapes=[pltpu.VMEM((points, width), F32), pltpu.VMEM((points, width), BF16)],
            compiler_params=PARAMS,
            cost_estimate=cost(3 * 10**9, 4 * 10**6),
            name="backward",
        )(grad_pre, hidden_weight, normed, gain, deviation, adj_t, *before)

    parts = []
    for member in range(members):
        if member == 0:
            parts.append(backward(0, after(adj_t, first_sent)))
            second_other = after(second_other, parts[0][1])
            second = add_parts(second, second_other)
        else:
            total = (parts[-1][0], loss) if member == members - 1 else (parts[-1][0],)
            parts.append(backward(member, after(adj_t, second), *total))
    small = parts[-1][0]
    inner, below, above = zip(*(part[1:] for part in parts))
    below, above = jnp.stack(below), jnp.stack(above)
    first = add_parts(first, first_other)
    first, small = next_stages(first, count, small)
    second, _ = next_stages(second, count)
    first, below, above = lax.optimization_barrier((first, below, above))
    first_other, small = swap_with(first, small, orders(count)[0])
    second = jnp.concatenate([swap_bits(second, orders(count)[0]), second])
    other_second = swap_cores(second)
    rims = (shift(above, "space", 1), shift(below, "space", -1))
    grad_latent = pl.pallas_call(
        latent_kernel,
        out_shape=jax.ShapeDtypeStruct((members, nodes, width), F32),
        in_specs=[VMEM] * (members + 2),
        out_specs=VMEM,
        compiler_params=PARAMS,
        cost_estimate=cost(10**6, 10**6),
        name="latent",
    )(*inner, *rims)

    first = jnp.concatenate([first_other, first])
    other_first = swap_cores(first)
    other_small = swap_cores(small)
    hidden_shape = jax.ShapeDtypeStruct((width, width), F32)
    blocks = 1 << (count - 1)
    grad_hidden = pl.pallas_call(
        lambda *refs: write_kernel(count, *refs),
        out_shape=hidden_shape,
        in_specs=[SMEM] + [VMEM] * 3,
        out_specs=HBM,
        scratch_shapes=[pltpu.VMEM((3 * chunk_rows, width), F32), pltpu.SemaphoreType.DMA((3 * blocks,))],
        compiler_params=PARAMS,
        cost_estimate=cost(10**6, 6 * 10**6),
        name="write",
    )(place, second, other_second, first)
    grad_hidden, grad_out, grad_gain, loss = pl.pallas_call(
        lambda *refs: last_write_kernel(count, *refs),
        out_shape=(
            hidden_shape,
            jax.ShapeDtypeStruct((variables, width), F32),
            jax.ShapeDtypeStruct((1, width), F32),
            jax.ShapeDtypeStruct((1, 1), F32),
        ),
        in_specs=[SMEM] + [VMEM] * 4 + [HBM],
        out_specs=(HBM,) * 4,
        scratch_shapes=[
            pltpu.VMEM((chunk_rows, width), F32),
            pltpu.VMEM((width, LANES), F32),
            pltpu.VMEM((variables, width), F32),
            pltpu.VMEM((1, width), F32),
            pltpu.VMEM((1, 1), F32),
            pltpu.SemaphoreType.DMA((blocks,)),
            pltpu.SemaphoreType.DMA((3,)),
        ],
        input_output_aliases={5: 0},
        compiler_params=PARAMS,
        name="last_write",
    )(place, first, other_first, small, other_small, grad_hidden)
    return (loss.reshape(1), grad_hidden, grad_out.T, grad_gain.reshape(width), grad_latent)


def solution(mesh):
    in_specs = (
        P(("groups", "member"), "space", None),
        P(("groups", "space"), None),
        P(("groups", "space"), None),
        P(("groups", "space"), None),
        P(("groups", "space")),
        P(("groups", "space")),
        P(("groups", "space"), None),
        P(("groups", "space"), None),
        P(),
        P(),
        P(),
        P(),
    )
    out_specs = (
        P("groups"),
        P("groups", None),
        P("groups", None),
        P("groups"),
        P(("groups", "member"), "space", None),
    )
    return jax.shard_map(local, mesh=mesh, in_specs=in_specs, out_specs=out_specs, check_vma=False)
```

```python
import jax
import jax.numpy as jnp
from jax import lax
from jax.experimental import pallas as pl
from jax.experimental.pallas import tpu as pltpu
from jax.sharding import PartitionSpec as P

RIM = 16
SMOOTH_SQ = 0.01
LANES = 128
BF16 = jnp.bfloat16
F32 = jnp.float32
VMEM = pl.BlockSpec(memory_space=pltpu.VMEM)
HBM = pl.BlockSpec(memory_space=pltpu.HBM)
PARAMS = pltpu.CompilerParams(vmem_limit_bytes=16 * 1024 * 1024)


def swap_pairs(value, axis, first):
    count = lax.axis_size(axis)
    pairs = [(i, i + 1) for i in range(first, count - 1, 2)]
    return lax.ppermute(value, axis, pairs + [(b, a) for a, b in pairs])


def swap_cores(value):
    return lax.ppermute(value, "member", [(0, 1), (1, 0)])


def swap_bits(value, bits):
    pairs = [
        (s * 2 + c, (s ^ (1 << bits[c])) * 2 + c)
        for s in range(lax.axis_size("space"))
        for c in range(2)
    ]
    return lax.ppermute(value, ("space", "member"), pairs)


def orders(count):
    return [(0, 1), (1, 0)] + [(bit, bit) for bit in range(2, count)]


def here_index():
    return lax.axis_index("space")


def core_index():
    return lax.axis_index("member")


def chunks(width, count):
    half, unit = width // 2, 16 << (count - 1)
    last = max(unit, half // 2)
    return [(0, half - last), (half - last, last)]


def turn(count, space, half):
    value = 0
    stages = orders(count)[:-1]
    for level, bits in enumerate(stages):
        value = value + ((1 - ((space >> bits[half]) & 1)) << (len(stages) - 1 - level))
    return value


def dot(a, b, dims=((1,), (0,))):
    return lax.dot_general(a, b, (dims, ((), ())), preferred_element_type=F32)


def fetch(sources, targets, sems):
    copies = [
        pltpu.make_async_copy(source, target, sems.at[i])
        for i, (source, target) in enumerate(zip(sources, targets))
    ]
    for copy in copies:
        copy.start()
    return copies


def prepare_kernel(
    index_in, mask_in, weight_in, valid_in, area_in, var_weight_in, projection_in, gain_in, own_in, state_in, target_in,
    hidden_weight_in, adj, adj_t, score_weight, projection, gain, own, base, hidden_weight,
    index, mask, weight, valid, area, var_weight, narrow, state, target, sems,
):
    sources = (
        index_in, mask_in, weight_in, valid_in, area_in, var_weight_in, projection_in, gain_in, own_in,
        state_in, target_in, hidden_weight_in,
    )
    targets = (index, mask, weight, valid, area, var_weight, narrow, gain, own, state, target, hidden_weight)
    copies = fetch(sources, targets, sems)
    for copy in copies[:6]:
        copy.wait()
    points = index.shape[1]
    variables = narrow.shape[0]
    nodes = jax.lax.broadcasted_iota(jnp.int32, (LANES, points), 0) + (here_index() * (own.shape[1]) - RIM)
    total = jnp.zeros((LANES, points), F32)
    for slot in range(index.shape[0]):
        coefficient = weight[slot : slot + 1, :] * mask[slot : slot + 1, :].astype(F32)
        total = total + jnp.where(index[slot : slot + 1, :] == nodes, coefficient, 0.0)
    upper = total.astype(BF16).astype(F32)
    lower = total - upper
    adj_t[:LANES, :] = upper.astype(BF16)
    adj_t[LANES:, :] = lower.astype(BF16)
    adj[:, :LANES] = upper.T.astype(BF16)
    adj[:, LANES:] = lower.T.astype(BF16)
    diagonal = jax.lax.broadcasted_iota(jnp.int32, (variables, variables), 0) == (
        jax.lax.broadcasted_iota(jnp.int32, (variables, variables), 1)
    )
    column = jnp.sum(jnp.where(diagonal, var_weight[...], 0.0), axis=1, keepdims=True)
    score_weight[...] = column * (valid[...].astype(F32) * area[...] / points)
    copies[6].wait()
    projection[...] = jnp.zeros_like(projection)
    projection[:variables, :] = narrow[...]
    for copy in copies[7:]:
        copy.wait()
    base[...] = state[...] - target[...]


def forward_kernel(
    adj, near, own, far, gain, hidden_weight, output_weight,
    normed, hidden, slope, outputs, deviation, extended, summed, projected,
):
    members, nodes, width = own.shape
    points = adj.shape[0]
    tile = 256
    odd = (here_index() & 1) == 1
    for member in range(members):
        for part in range(2):
            start = part * LANES
            extended[member, start : start + RIM, :] = jnp.where(odd, near[member], far[member])
            extended[member, start + RIM : start + RIM + nodes, :] = own[member]
            extended[member, start + RIM + nodes : start + 2 * RIM + nodes, :] = jnp.where(
                odd, far[member], near[member]
            )
            extended[member, start + 2 * RIM + nodes : start + LANES, :] = jnp.zeros(
                (LANES - 2 * RIM - nodes, width), BF16
            )

    def gather(member):
        summed[member] = dot(adj[...], extended[member])

    def norm(member, first, size):
        for row in range(first, first + size, 32):
            value = summed[member, row : row + 32, :]
            value = value - jnp.sum(value, axis=1, keepdims=True) * (1.0 / width)
            spread = jnp.sum(value * value, axis=1, keepdims=True) * (1.0 / width)
            inverse = lax.rsqrt(spread + 1e-05)
            target = slice(member * points + row, member * points + row + 32)
            deviation[target, :] = inverse
            normed[target, :] = (value * inverse * gain[...]).astype(BF16)

    def layer(member, column):
        rows = slice(member * points, (member + 1) * points)
        columns = slice(column, column + tile)
        pre = dot(normed[rows, :], hidden_weight[:, columns])
        sig = 0.5 * jnp.tanh(0.5 * pre) + 0.5
        hid = pre * sig
        slope[rows, columns] = (sig + hid * (1.0 - sig)).astype(BF16)
        hid = hid.astype(BF16)
        hidden[rows, columns] = hid
        term = dot(hid, output_weight[:, columns], ((1,), (1,)))
        if column == 0:
            projected[...] = term
        else:
            projected[...] += term

    gather(0)
    norm(0, 0, points)
    for member in range(members):
        if member + 1 < members:
            gather(member + 1)
        for column in range(0, width, tile):
            if member + 1 < members:
                size = points * tile // width
                norm(member + 1, points * column // width, size)
            layer(member, column)
        outputs[member] = projected[...].T[: outputs.shape[1], :]


def own_rows(count, width):
    half_rows = width // 2
    for half in range(2):
        mask = turn(count, here_index(), half)
        for first, rows in chunks(width, count):
            size = rows >> (count - 1)
            for block in range(rows // size):
                start = (1 - (core_index() ^ half)) * half_rows + first + (block ^ mask) * size
                yield half * half_rows + first + block * size, size, pl.multiple_of(start, size)


def narrow_rows(count, width):
    rows = chunks(width, count)[-1][1]
    size = rows >> (count - 1)
    sides = width // 2 // rows
    for half in range(2):
        mask = turn(count, here_index(), half)
        for block in range(rows // size):
            row = half * (width // 2) + block * sides * size
            starts = tuple(row + side * size for side in range(sides))
            yield starts, size, 1 - (core_index() ^ half), pl.multiple_of((block ^ mask) * size, size)


def transpose_kernel(count, normed, normed_t):
    width = normed.shape[1]
    blocks = {}
    for row, size, there in own_rows(count, width):
        stop = row + size
        while row < stop:
            group, offset = row // LANES, row % LANES
            if group not in blocks:
                blocks = {group: normed[:, group * LANES : (group + 1) * LANES].T}
            part = min(stop - row, LANES - offset)
            normed_t[pl.ds(pl.multiple_of(there, 16), part), :] = blocks[group][offset : offset + part]
            row, there = row + part, there + part


def score_kernel(
    outputs, others, base, score_weight, output_weight, slope, normed_t,
    loss, grad_pre, grad_pred_t, sent,
    grad_pred, grad_wide,
):
    members, variables, points = outputs.shape
    width = slope.shape[1]
    total = 2 * members
    weight = score_weight[...]
    grad_wide[...] = jnp.zeros_like(grad_wide)
    grad_pred[...] = jnp.zeros_like(grad_pred)
    values = [outputs[m] for m in range(members)]
    grads = [None] * members
    pair_grads = [jnp.zeros((variables, points), F32) for _ in range(members)]
    errors = jnp.zeros((variables, points), F32)
    pairs = jnp.full((variables, points), members * SMOOTH_SQ**0.5, F32)
    for m in range(members):
        diff = values[m] + base[...]
        square = diff * diff + SMOOTH_SQ
        inverse = lax.rsqrt(square)
        errors = errors + square * inverse
        grads[m] = diff * inverse
        for n in range(m + 1, members):
            diff = values[m] - values[n]
            square = diff * diff + SMOOTH_SQ
            inverse = lax.rsqrt(square)
            pairs = pairs + 2.0 * (square * inverse)
            pair_grads[m] = pair_grads[m] + diff * inverse
            pair_grads[n] = pair_grads[n] - diff * inverse
        for n in range(members):
            diff = values[m] - others[n]
            square = diff * diff + SMOOTH_SQ
            inverse = lax.rsqrt(square)
            pairs = pairs + square * inverse
            pair_grads[m] = pair_grads[m] + diff * inverse
    score = weight * (errors * (1.0 / total) - pairs * (1.0 / (2.0 * total * (total - 1))))
    loss[...] = jnp.sum(jnp.sum(score, axis=0, keepdims=True), axis=1, keepdims=True)
    for m in range(members):
        grad = weight * (grads[m] * (1.0 / total) - pair_grads[m] * (1.0 / (total * (total - 1))))
        columns = slice(m * points, (m + 1) * points)
        grad_wide[:variables, columns] = grad
        grad_pred[columns, :] = grad_wide[:, columns].T.astype(BF16)
    grad_pred_t[...] = grad_wide[...].astype(BF16)
    for m in range(members):
        rows = slice(m * points, (m + 1) * points)
        for column in range(0, width, 256):
            columns = slice(column, column + 256)
            grad_hid = dot(grad_pred[rows, :], output_weight[:, columns])
            grad_pre[rows, columns] = (grad_hid * slope[rows, columns].astype(F32)).astype(BF16)
    products(normed_t, grad_pre, slice(0, sent.shape[0]), sent)


def products(normed_t, grad_pre, rows, target):
    width = grad_pre.shape[1]
    for column in range(0, width, 256):
        columns = slice(column, column + 256)
        target[:, columns] = dot(normed_t[rows, :], grad_pre[:, columns]).astype(target.dtype)


def product_kernel(first, normed_t, grad_pre, *refs):
    target = refs[-1]
    products(normed_t, grad_pre, slice(first, first + target.shape[0]), target)
    if len(refs) > 1:
        target[:, grad_pre.shape[1] :] = refs[0][...]


def sent_kernel(count, normed_t, grad_pre, grad_pred_t, hidden, sent, kept_narrow):
    width = grad_pre.shape[1]
    first, rows = chunks(width, count)[-1]
    products(normed_t, grad_pre, slice(first, first + rows), sent)
    value = dot(grad_pred_t[...], hidden[...]).T
    for starts, size, own, place_row in narrow_rows(count, width):
        here = pl.ds(place_row, size)
        for side, row in enumerate(starts):
            part = value[row : row + size]
            lanes = slice(side * LANES, (side + 1) * LANES)

            @pl.when(own == 1)
            def _():
                kept_narrow[here, lanes] = part

            @pl.when(own == 0)
            def _():
                sent[here, width + lanes.start : width + lanes.stop] = part.astype(BF16)


def backward_kernel(member, grad_pre, hidden_weight, normed, gain, deviation, adj_t, *refs):
    before, (small, inner, near, far, product, rows_grad) = refs[:-6], refs[-6:]
    nodes, width = inner.shape
    points = adj_t.shape[1]
    inverse_gain = 1.0 / gain[...]
    for column in range(0, width, 256):
        columns = slice(column, column + 256)
        product[:, columns] = dot(
            grad_pre[member * points : (member + 1) * points, :], hidden_weight[columns, :], ((1,), (1,))
        )

    def step(index, total):
        here = pl.ds(pl.multiple_of(index * 32, 32), 32)
        there = pl.ds(pl.multiple_of(member * points + index * 32, 32), 32)
        value = product[here, :]
        zn = normed[there, :].astype(F32)
        both = value * zn
        scaled = value * gain[...]
        mean = jnp.sum(scaled, axis=1, keepdims=True) * (1.0 / width)
        slant = jnp.sum(both, axis=1, keepdims=True) * (1.0 / width)
        grad = deviation[there, :] * (scaled - mean - (zn * inverse_gain) * slant)
        rows_grad[here, :] = grad.astype(BF16)
        return total + jnp.sum(both.reshape(4, 8, width), axis=0)

    total = before[0][...] if before else jnp.zeros((8, width), F32)
    total = lax.fori_loop(0, points // 32, step, total, unroll=4)
    value = dot(adj_t[...], rows_grad[...])
    value = value[:LANES] + value[LANES:]
    below, above = value[:RIM], value[RIM + nodes : nodes + 2 * RIM]
    odd = (here_index() & 1) == 1
    near[...] = jnp.where(odd, below, above).astype(BF16)
    far[...] = jnp.where(odd, above, below).astype(BF16)
    inner[...] = value[RIM : RIM + nodes]
    if not before:
        small[...] = total
        return
    row = jnp.concatenate(
        [
            jnp.sum(total, axis=0, keepdims=True) * inverse_gain,
            jnp.broadcast_to(before[1][...], (1, small.shape[1] - width)),
        ],
        axis=1,
    )
    upper = row.astype(BF16).astype(F32)
    index = jax.lax.broadcasted_iota(jnp.int32, (8, row.shape[1]), 0)
    small[...] = jnp.where(index == 0, upper, jnp.where(index == 1, row - upper, 0.0)).astype(BF16)


def latent_kernel(*refs):
    grad_latent = refs[-1]
    members, nodes = grad_latent.shape[:2]
    inner, (near, far) = refs[:members], refs[members:-1]
    odd = (here_index() & 1) == 1
    for member in range(members):
        low = jnp.where(odd, near[member].astype(F32), far[member].astype(F32))
        high = jnp.where(odd, far[member].astype(F32), near[member].astype(F32))
        value = inner[member]
        grad_latent[member, :RIM, :] = value[:RIM, :] + low
        grad_latent[member, RIM : nodes - RIM, :] = value[RIM : nodes - RIM, :]
        grad_latent[member, nodes - RIM :, :] = value[nodes - RIM :, :] + high


def write_rows(count, chunk, side, source, target, wide, start, sems):
    width = target.shape[1]
    first, rows = chunks(width, count)[chunk]
    size = rows >> (count - 1)
    half = core_index() ^ side
    mask = jnp.where(half == 0, turn(count, here_index(), 0), turn(count, here_index(), 1))
    copies = []
    for block in range(rows // size):
        here = slice(block * size, (block + 1) * size)
        there = slice(start + block * size, start + (block + 1) * size)
        wide[there, :] = source[here, :width].astype(F32)
        row = half * (width // 2) + first + (block ^ mask) * size
        copy = pltpu.make_async_copy(
            wide.at[there, :],
            target.at[pl.ds(pl.multiple_of(row, size), size), :],
            sems.at[block],
        )
        copy.start()
        copies.append(copy)
    return copies


def write_kernel(count, parts, *refs):
    sources, (target, wide, sems) = refs[: len(parts)], refs[-3:]
    copies = []
    start = 0
    for i, ((chunk, side), source) in enumerate(zip(parts, sources)):
        copies += write_rows(count, chunk, side, source, target, wide, start, sems.at[i])
        start += source.shape[0]
    for copy in copies:
        copy.wait()


def last_write_kernel(
    count, own, other, small, other_small, before,
    target, grad_out_t, grad_gain, loss,
    wide, narrow, narrow_t, gain_row, loss_cell, sems, last_sems,
):
    del before
    width = target.shape[1]
    last = len(chunks(width, count)) - 1
    copies = write_rows(count, last, 1, other, target, wide, 0, sems)
    for starts, size, mine, place_row in narrow_rows(count, width):
        here = pl.ds(place_row, size)
        for side, row in enumerate(starts):
            lanes = slice(width + side * LANES, width + (side + 1) * LANES)
            value = jnp.where(mine == 1, own[here, lanes].astype(F32), other[here, lanes].astype(F32))
            narrow[row : row + size, :] = value
    narrow_t[...] = narrow[...].T[: grad_out_t.shape[0], :]
    total = small[...].astype(F32) + other_small[...].astype(F32)
    total = total[:1] + total[1:2]
    gain_row[...] = total[:, :width]
    loss_cell[...] = total[:, width : width + 1]
    copies += fetch((narrow_t, gain_row, loss_cell), (grad_out_t, grad_gain, loss), last_sems)
    for copy in copies:
        copy.wait()


def add_parts(mine, other):
    return (mine.astype(F32) + other.astype(F32)).astype(BF16)


def unpack(small):
    return small[:1].astype(F32) + small[1:2].astype(F32)


def swap_with(value, small, bits):
    rows = value.shape[0]
    other = swap_bits(jnp.concatenate([value, small]), bits)
    total = unpack(small) + unpack(other[rows:])
    upper = total.astype(BF16)
    lower = (total - upper.astype(F32)).astype(BF16)
    rest = jnp.zeros((small.shape[0] - 2, small.shape[1]), BF16)
    return other[:rows], jnp.concatenate([upper, lower, rest])


class Sum:
    def __init__(self, value, count):
        self.value, self.small = value, None
        forth = orders(count)
        self.stages = forth + forth[-2::-1]
        self.halvings, self.stage = count - 1, 0

    def start(self, *others):
        rows = self.value.shape[0] // 2 if self.stage < self.halvings else 0
        sent = self.value[:rows] if rows else self.value
        if others:
            sent = after(sent, *others)
        bits = self.stages[self.stage]
        last = self.stage == len(self.stages) - 1
        if self.small is not None and (0 < self.stage <= self.halvings or last):
            self.other, self.small = swap_with(sent, self.small, bits)
        else:
            self.other = swap_bits(sent, bits)
        return sent

    def finish(self, *others):
        other = after(self.other, *others) if others else self.other
        if self.stage < self.halvings:
            self.value = add_parts(self.value[other.shape[0] :], other)
        elif self.stage == self.halvings:
            self.value = add_parts(self.value, other)
        else:
            self.value = jnp.concatenate([other, self.value])
        self.stage += 1


def after(value, *others):
    return lax.optimization_barrier((value, *others))[0]


def in_hbm(*values):
    return [pltpu.with_memory_space_constraint(value, pltpu.HBM) for value in values]


def cost(flops, moved):
    return pl.CostEstimate(flops=flops, bytes_accessed=moved, transcendentals=0)


def local(
    latent,
    edge_node_index,
    edge_mask,
    edge_weight,
    valid,
    area,
    state,
    target,
    var_weight,
    gain,
    hidden_weight,
    output_weight,
):
    members, nodes, width = latent.shape
    points, variables = state.shape
    rows = members * points
    count = lax.axis_size("space").bit_length() - 1
    space = lax.axis_index("space")
    parts = chunks(width, count)
    odd = (space & 1) == 1
    low, high = latent[:, :RIM], latent[:, nodes - RIM :]
    near, far = jnp.where(odd, low, high), jnp.where(odd, high, low)
    far = swap_pairs(far, "space", 1)
    near = swap_pairs(after(near, far) if False else near, "space", 0)

    adj, adj_t, score_weight, projection, gain, own, base, hidden_weight = pl.pallas_call(
        prepare_kernel,
        out_shape=(
            pltpu.VMEM((points, 2 * LANES), BF16),
            pltpu.VMEM((2 * LANES, points), BF16),
            pltpu.VMEM((variables, points), F32),
            pltpu.VMEM((LANES, width), BF16),
            pltpu.VMEM((1, width), F32),
            pltpu.VMEM(latent.shape, BF16),
            pltpu.VMEM((variables, points), F32),
            pltpu.VMEM((width, width), BF16),
        ),
        in_specs=[HBM] * 12,
        out_specs=(VMEM,) * 8,
        scratch_shapes=[
            pltpu.VMEM(edge_mask.T.shape, jnp.int32),
            pltpu.VMEM(edge_mask.T.shape, jnp.int32),
            pltpu.VMEM(edge_mask.T.shape, F32),
            pltpu.VMEM((1, points), jnp.int32),
            pltpu.VMEM((1, points), F32),
            pltpu.VMEM((1, variables), F32),
            pltpu.VMEM((variables, width), BF16),
            pltpu.VMEM((variables, points), F32),
            pltpu.VMEM((variables, points), F32),
            pltpu.SemaphoreType.DMA((12,)),
        ],
        compiler_params=PARAMS,
        name="prepare",
    )(
            *in_hbm(
            edge_node_index.T,
            edge_mask.T,
            edge_weight.T,
            valid.reshape(1, points),
            area.reshape(1, points),
            var_weight.reshape(1, variables),
            output_weight.T,
            gain.reshape(1, width),
            latent,
            state.T,
            target.T,
            hidden_weight,
        ),
    )
    normed, hidden, slope, outputs, deviation = pl.pallas_call(
        forward_kernel,
        out_shape=(
            pltpu.VMEM((rows, width), BF16),
            pltpu.VMEM((rows, width), BF16),
            pltpu.VMEM((rows, width), BF16),
            jax.ShapeDtypeStruct((members, variables, points), F32),
            pltpu.VMEM((rows, 1), F32),
        ),
        in_specs=[VMEM] * 7,
        out_specs=(VMEM,) * 5,
        scratch_shapes=[
            pltpu.VMEM((members, 2 * LANES, width), BF16),
            pltpu.VMEM((members, points, width), F32),
            pltpu.VMEM((points, LANES), F32),
        ],
        compiler_params=PARAMS,
        name="forward",
    )(adj, near, own, far, gain, hidden_weight, projection)
    others = swap_cores(outputs)
    normed_t = pl.pallas_call(
        lambda *refs: transpose_kernel(count, *refs),
        out_shape=pltpu.VMEM((width, rows), BF16),
        in_specs=[VMEM],
        out_specs=VMEM,
        compiler_params=PARAMS,
        cost_estimate=cost(10**9, 4 * 10**6),
        name="transpose",
    )(normed)
    loss, grad_pre, grad_pred_t, sent = pl.pallas_call(
        score_kernel,
        out_shape=(
            jax.ShapeDtypeStruct((1, 1), F32),
            pltpu.VMEM((rows, width), BF16),
            pltpu.VMEM((LANES, rows), BF16),
            jax.ShapeDtypeStruct((parts[0][1], width), BF16),
        ),
        in_specs=[VMEM] * 7,
        out_specs=(VMEM,) * 4,
        scratch_shapes=[pltpu.VMEM((rows, LANES), BF16), pltpu.VMEM((LANES, rows), F32)],
        compiler_params=PARAMS,
        name="score",
    )(outputs, others, base, score_weight, projection, slope, normed_t)

    def product(first, size, dtype, *narrow):
        columns = width + sum(value.shape[1] for value in narrow)
        return pl.pallas_call(
            lambda *refs: product_kernel(first, *refs),
            out_shape=jax.ShapeDtypeStruct((size, columns), dtype),
            in_specs=[VMEM] * (2 + len(narrow)),
            out_specs=VMEM,
            compiler_params=PARAMS,
            cost_estimate=cost(10**9, 2 * 10**6),
            name="product",
        )(normed_t, grad_pre, *narrow)

    last = len(parts) - 1
    last_rows = parts[last][1]
    extra = LANES * (width // 2 // last_rows)
    received, sums, token = [swap_cores(sent)], [], ()
    for chunk, (first, size) in enumerate(parts):
        if chunk + 1 < last:
            sent = product(*parts[chunk + 1], BF16)
            received.append(swap_cores(sent))
        elif chunk + 1 == last:
            sent, kept_narrow = pl.pallas_call(
                lambda *refs: sent_kernel(count, *refs),
                out_shape=(
                    jax.ShapeDtypeStruct((last_rows, width + extra), BF16),
                    pltpu.VMEM((last_rows, extra), F32),
                ),
                in_specs=[VMEM] * 4,
                out_specs=(VMEM,) * 2,
                compiler_params=PARAMS,
                cost_estimate=cost(10**9, 4 * 10**6),
                name="sent",
            )(normed_t, grad_pre, after(grad_pred_t, *token), hidden)
            received.append(swap_cores(sent))
        kept = product(width // 2 + first, size, F32, *([kept_narrow] if chunk == last else []))
        sums.append(Sum(add_parts(kept, received[chunk]), count))
        token = (sums[-1].start(*token),)

    def backward(member, adj_t, *before):
        last = len(before) > 1
        return pl.pallas_call(
            lambda *refs: backward_kernel(member, *refs),
            out_shape=(
                jax.ShapeDtypeStruct((8, width + extra), BF16) if last else pltpu.VMEM((8, width), F32),
                pltpu.VMEM((nodes, width), F32),
                jax.ShapeDtypeStruct((RIM, width), BF16),
                jax.ShapeDtypeStruct((RIM, width), BF16),
            ),
            in_specs=[VMEM] * (6 + len(before)),
            out_specs=(VMEM,) * 4,
            scratch_shapes=[pltpu.VMEM((points, width), F32), pltpu.VMEM((points, width), BF16)],
            compiler_params=PARAMS,
            cost_estimate=cost(3 * 10**9, 4 * 10**6),
            name="backward",
        )(grad_pre, hidden_weight, normed, gain, deviation, adj_t, *before)

    done = []
    for stage in range(2 * count - 1):
        for chunk in range(last + 1):
            if stage == 0 and len(done) < members:
                before = (done[-1][0],) if done else ()
                if len(done) == members - 1:
                    before = before + (loss,)
                done.append(backward(len(done), after(adj_t, *token), *before))
                token = token + (done[-1][1],)
                if len(done) == members:
                    sums[last].small = done[-1][0]
            sums[chunk].finish(*token)
            token = ()
            if stage < 2 * count - 2:
                token = (sums[chunk].start(),)
            if stage == 3 and chunk == last:
                inner, near, far = zip(*(part[1:] for part in done))
                near, far = after(jnp.stack(near), *token), after(jnp.stack(far), *token)
                near, far = swap_pairs(near, "space", 0), swap_pairs(far, "space", 1)
    grad_latent = pl.pallas_call(
        latent_kernel,
        out_shape=jax.ShapeDtypeStruct((members, nodes, width), F32),
        in_specs=[VMEM] * (members + 2),
        out_specs=VMEM,
        compiler_params=PARAMS,
        cost_estimate=cost(10**6, 10**6),
        name="latent",
    )(*inner, near, far)

    own = [chunk.value for chunk in sums]
    other = [swap_cores(value) for value in own]
    small = sums[last].small
    other_small = swap_cores(small)
    hidden_shape = jax.ShapeDtypeStruct((width, width), F32)
    blocks = 1 << (count - 1)

    def write(pieces, sources, *before):
        height = sum(source.shape[0] for source in sources)
        return pl.pallas_call(
            lambda *refs: write_kernel(count, pieces, *refs),
            out_shape=hidden_shape,
            in_specs=[VMEM] * len(sources) + [HBM] * len(before),
            out_specs=HBM,
            scratch_shapes=[
                pltpu.VMEM((height, width), F32),
                pltpu.SemaphoreType.DMA((len(pieces), blocks)),
            ],
            input_output_aliases={len(sources): 0} if before else {},
            compiler_params=PARAMS,
            cost_estimate=cost(10**6, 6 * 10**6),
            name="write",
        )(*sources, *before)

    grad_hidden = ()
    for chunk in range(last - 1):
        grad_hidden = (write([(chunk, 0), (chunk, 1)], [own[chunk], other[chunk]], *grad_hidden),)
    grad_hidden = write(
        [(last - 1, 0), (last - 1, 1), (last, 0)], [own[last - 1], other[last - 1], own[last]], *grad_hidden
    )
    grad_hidden, grad_out, grad_gain, loss = pl.pallas_call(
        lambda *refs: last_write_kernel(count, *refs),
        out_shape=(
            hidden_shape,
            jax.ShapeDtypeStruct((variables, width), F32),
            jax.ShapeDtypeStruct((1, width), F32),
            jax.ShapeDtypeStruct((1, 1), F32),
        ),
        in_specs=[VMEM] * 4 + [HBM],
        out_specs=(HBM,) * 4,
        scratch_shapes=[
            pltpu.VMEM((last_rows, width), F32),
            pltpu.VMEM((width, LANES), F32),
            pltpu.VMEM((variables, width), F32),
            pltpu.VMEM((1, width), F32),
            pltpu.VMEM((1, 1), F32),
            pltpu.SemaphoreType.DMA((blocks,)),
            pltpu.SemaphoreType.DMA((3,)),
        ],
        input_output_aliases={4: 0},
        compiler_params=PARAMS,
        name="last_write",
    )(own[last], other[last], small, other_small, grad_hidden)
    return (loss.reshape(1), grad_hidden, grad_out.T, grad_gain.reshape(width), grad_latent)


def solution(mesh):
    in_specs = (
        P(("groups", "member"), "space", None),
        P(("groups", "space"), None),
        P(("groups", "space"), None),
        P(("groups", "space"), None),
        P(("groups", "space")),
        P(("groups", "space")),
        P(("groups", "space"), None),
        P(("groups", "space"), None),
        P(),
        P(),
        P(),
        P(),
    )
    out_specs = (
        P("groups"),
        P("groups", None),
        P("groups", None),
        P("groups"),
        P(("groups", "member"), "space", None),
    )
    return jax.shard_map(local, mesh=mesh, in_specs=in_specs, out_specs=out_specs, check_vma=False)
```

```python
import jax
import jax.numpy as jnp
from jax import lax
from jax.experimental import pallas as pl
from jax.experimental.pallas import tpu as pltpu
from jax.sharding import PartitionSpec as P

RIM = 16
SMOOTH_SQ = 0.01
LANES = 128
BF16 = jnp.bfloat16
F32 = jnp.float32
VMEM = pl.BlockSpec(memory_space=pltpu.VMEM)
HBM = pl.BlockSpec(memory_space=pltpu.HBM)
PARAMS = pltpu.CompilerParams(vmem_limit_bytes=16 * 1024 * 1024)


def swap_pairs(value, axis, first):
    count = lax.axis_size(axis)
    pairs = [(i, i + 1) for i in range(first, count - 1, 2)]
    return lax.ppermute(value, axis, pairs + [(b, a) for a, b in pairs])


def swap_cores(value):
    return lax.ppermute(value, "member", [(0, 1), (1, 0)])


def swap_bits(value, bits):
    pairs = [
        (s * 2 + c, (s ^ (1 << bits[c])) * 2 + c)
        for s in range(lax.axis_size("space"))
        for c in range(2)
    ]
    return lax.ppermute(value, ("space", "member"), pairs)


def orders(count):
    return [(0, 1), (1, 0)] + [(bit, bit) for bit in range(2, count)]


LIGHT = pl.CostEstimate(flops=1, bytes_accessed=1, transcendentals=0)


def here_index():
    return lax.axis_index("space")


def core_index():
    return lax.axis_index("member")


def chunks(width, count):
    half, unit = width // 2, 16 << (count - 1)
    last = max(unit, half // 2)
    return [(0, half - last), (half - last, last)]


def turn(count, space, half):
    value = 0
    stages = orders(count)[:-1]
    for level, bits in enumerate(stages):
        value = value + ((1 - ((space >> bits[half]) & 1)) << (len(stages) - 1 - level))
    return value


def dot(a, b, dims=((1,), (0,))):
    return lax.dot_general(a, b, (dims, ((), ())), preferred_element_type=F32)


def fetch(sources, targets, sems):
    copies = [
        pltpu.make_async_copy(source, target, sems.at[i])
        for i, (source, target) in enumerate(zip(sources, targets))
    ]
    for copy in copies:
        copy.start()
    return copies


def prepare_kernel(
    index_in, mask_in, weight_in, valid_in, area_in, var_weight_in, projection_in, gain_in, own_in, state_in, target_in,
    hidden_weight_in, adj, adj_t, score_weight, projection, gain, own, base, hidden_weight,
    index, mask, weight, valid, area, var_weight, narrow, state, target, sems,
):
    sources = (
        index_in, mask_in, weight_in, valid_in, area_in, var_weight_in, projection_in, gain_in, own_in,
        state_in, target_in, hidden_weight_in,
    )
    targets = (index, mask, weight, valid, area, var_weight, narrow, gain, own, state, target, hidden_weight)
    copies = fetch(sources, targets, sems)
    for copy in copies[:6]:
        copy.wait()
    points = index.shape[1]
    variables = narrow.shape[0]
    nodes = jax.lax.broadcasted_iota(jnp.int32, (LANES, points), 0) + (here_index() * (own.shape[1]) - RIM)
    total = jnp.zeros((LANES, points), F32)
    for slot in range(index.shape[0]):
        coefficient = weight[slot : slot + 1, :] * mask[slot : slot + 1, :].astype(F32)
        total = total + jnp.where(index[slot : slot + 1, :] == nodes, coefficient, 0.0)
    upper = total.astype(BF16).astype(F32)
    lower = total - upper
    adj_t[:LANES, :] = upper.astype(BF16)
    adj_t[LANES:, :] = lower.astype(BF16)
    adj[:, :LANES] = upper.T.astype(BF16)
    adj[:, LANES:] = lower.T.astype(BF16)
    diagonal = jax.lax.broadcasted_iota(jnp.int32, (variables, variables), 0) == (
        jax.lax.broadcasted_iota(jnp.int32, (variables, variables), 1)
    )
    column = jnp.sum(jnp.where(diagonal, var_weight[...], 0.0), axis=1, keepdims=True)
    score_weight[...] = column * (valid[...].astype(F32) * area[...] / points)
    copies[6].wait()
    projection[...] = jnp.zeros_like(projection)
    projection[:variables, :] = narrow[...]
    for copy in copies[7:]:
        copy.wait()
    base[...] = state[...] - target[...]


def forward_kernel(
    adj, near, own, far, gain, hidden_weight, output_weight,
    normed, hidden, slope, outputs, deviation, extended, summed, projected,
):
    members, nodes, width = own.shape
    points = adj.shape[0]
    tile = 256
    odd = (here_index() & 1) == 1
    for member in range(members):
        for part in range(2):
            start = part * LANES
            extended[member, start : start + RIM, :] = jnp.where(odd, near[member], far[member])
            extended[member, start + RIM : start + RIM + nodes, :] = own[member]
            extended[member, start + RIM + nodes : start + 2 * RIM + nodes, :] = jnp.where(
                odd, far[member], near[member]
            )
            extended[member, start + 2 * RIM + nodes : start + LANES, :] = jnp.zeros(
                (LANES - 2 * RIM - nodes, width), BF16
            )

    def gather(member):
        summed[member] = dot(adj[...], extended[member])

    def norm(member, first, size):
        for row in range(first, first + size, 32):
            value = summed[member, row : row + 32, :]
            value = value - jnp.sum(value, axis=1, keepdims=True) * (1.0 / width)
            spread = jnp.sum(value * value, axis=1, keepdims=True) * (1.0 / width)
            inverse = lax.rsqrt(spread + 1e-05)
            target = slice(member * points + row, member * points + row + 32)
            deviation[target, :] = inverse
            normed[target, :] = (value * inverse * gain[...]).astype(BF16)

    def layer(member, column):
        rows = slice(member * points, (member + 1) * points)
        columns = slice(column, column + tile)
        pre = dot(normed[rows, :], hidden_weight[:, columns])
        sig = 0.5 * jnp.tanh(0.5 * pre) + 0.5
        hid = pre * sig
        slope[rows, columns] = (sig + hid * (1.0 - sig)).astype(BF16)
        hid = hid.astype(BF16)
        hidden[rows, columns] = hid
        term = dot(hid, output_weight[:, columns], ((1,), (1,)))
        if column == 0:
            projected[...] = term
        else:
            projected[...] += term

    gather(0)
    norm(0, 0, points)
    for member in range(members):
        if member + 1 < members:
            gather(member + 1)
        for column in range(0, width, tile):
            if member + 1 < members:
                size = points * tile // width
                norm(member + 1, points * column // width, size)
            layer(member, column)
        outputs[member] = projected[...].T[: outputs.shape[1], :]


def own_rows(count, width):
    half_rows = width // 2
    for half in range(2):
        mask = turn(count, here_index(), half)
        for first, rows in chunks(width, count):
            size = rows >> (count - 1)
            for block in range(rows // size):
                start = (1 - (core_index() ^ half)) * half_rows + first + (block ^ mask) * size
                yield half * half_rows + first + block * size, size, pl.multiple_of(start, size)


def narrow_rows(count, width):
    rows = chunks(width, count)[-1][1]
    size = rows >> (count - 1)
    sides = width // 2 // rows
    for half in range(2):
        mask = turn(count, here_index(), half)
        for block in range(rows // size):
            row = half * (width // 2) + block * sides * size
            starts = tuple(row + side * size for side in range(sides))
            yield starts, size, 1 - (core_index() ^ half), pl.multiple_of((block ^ mask) * size, size)


def smooth(diff):
    square = diff * diff + SMOOTH_SQ
    inverse = lax.rsqrt(square)
    return square * inverse, diff * inverse


def transpose_kernel(count, normed, outputs, base, normed_t, own_score, own_grad):
    width = normed.shape[1]
    members, variables, points = outputs.shape
    total = 2 * members
    values = [outputs[m] for m in range(members)]
    zero = jnp.zeros((variables, points), F32)
    grads, pair_grads = [zero] * members, [zero] * members
    errors, pairs = zero, jnp.full((variables, points), members * SMOOTH_SQ**0.5, F32)
    for m in range(members):
        size, grads[m] = smooth(values[m] + base[...])
        errors = errors + size
        for n in range(m + 1, members):
            size, grad = smooth(values[m] - values[n])
            pairs = pairs + 2.0 * size
            pair_grads[m] = pair_grads[m] + grad
            pair_grads[n] = pair_grads[n] - grad
    own_score[...] = errors * (1.0 / total) - pairs * (1.0 / (2.0 * total * (total - 1)))
    for m in range(members):
        own_grad[m] = grads[m] * (1.0 / total) - pair_grads[m] * (1.0 / (total * (total - 1)))
    blocks = {}
    for row, size, there in own_rows(count, width):
        stop = row + size
        while row < stop:
            group, offset = row // LANES, row % LANES
            if group not in blocks:
                blocks = {group: normed[:, group * LANES : (group + 1) * LANES].T}
            part = min(stop - row, LANES - offset)
            normed_t[pl.ds(pl.multiple_of(there, 16), part), :] = blocks[group][offset : offset + part]
            row, there = row + part, there + part


def score_kernel(
    outputs, others, own_score, own_grad, score_weight, output_weight, slope, normed_t,
    loss, grad_pre, grad_pred_t, sent,
    grad_pred, grad_wide,
):
    members, variables, points = outputs.shape
    width = slope.shape[1]
    total = 2 * members
    weight = score_weight[...]
    grad_wide[...] = jnp.zeros_like(grad_wide)
    grad_pred[...] = jnp.zeros_like(grad_pred)
    values = [outputs[m] for m in range(members)]
    pair_grads = [jnp.zeros((variables, points), F32) for _ in range(members)]
    pairs = jnp.zeros((variables, points), F32)
    for m in range(members):
        for n in range(members):
            size, grad = smooth(values[m] - others[n])
            pairs = pairs + size
            pair_grads[m] = pair_grads[m] + grad
    score = weight * (own_score[...] - pairs * (1.0 / (2.0 * total * (total - 1))))
    loss[...] = jnp.sum(jnp.sum(score, axis=0, keepdims=True), axis=1, keepdims=True)
    for m in range(members):
        grad = weight * (own_grad[m] - pair_grads[m] * (1.0 / (total * (total - 1))))
        columns = slice(m * points, (m + 1) * points)
        grad_wide[:variables, columns] = grad
        grad_pred[columns, :] = grad_wide[:, columns].T.astype(BF16)
    grad_pred_t[...] = grad_wide[...].astype(BF16)
    for m in range(members):
        rows = slice(m * points, (m + 1) * points)
        for column in range(0, width, 256):
            columns = slice(column, column + 256)
            grad_hid = dot(grad_pred[rows, :], output_weight[:, columns])
            grad_pre[rows, columns] = (grad_hid * slope[rows, columns].astype(F32)).astype(BF16)
    products(normed_t, grad_pre, slice(0, sent.shape[0]), sent)


def products(normed_t, grad_pre, rows, target):
    width = grad_pre.shape[1]
    for column in range(0, width, 256):
        columns = slice(column, column + 256)
        target[:, columns] = dot(normed_t[rows, :], grad_pre[:, columns]).astype(target.dtype)


def product_kernel(first, normed_t, grad_pre, received, *refs):
    narrow, (sent, kept) = refs[:-2], refs[-2:]
    width, rows = grad_pre.shape[1], sent.shape[0]
    for column in range(0, width, 256):
        columns = slice(column, column + 256)
        value = dot(normed_t[first : first + 2 * rows, :], grad_pre[:, columns])
        value = (value + received[:, columns].astype(F32)).astype(BF16)
        sent[:, columns] = value[:rows]
        kept[:, columns] = value[rows:]
    if narrow:
        value = (narrow[0][...] + received[:, width:].astype(F32)).astype(BF16)
        sent[:, width:] = value[:rows]
        kept[:, width:] = value[rows:]


def sent_kernel(count, normed_t, grad_pre, grad_pred_t, hidden, sent, kept_narrow):
    width = grad_pre.shape[1]
    first, rows = chunks(width, count)[-1]
    products(normed_t, grad_pre, slice(first, first + rows), sent)
    value = dot(grad_pred_t[...], hidden[...]).T
    for starts, size, own, place_row in narrow_rows(count, width):
        here = pl.ds(place_row, size)
        for side, row in enumerate(starts):
            part = value[row : row + size]
            lanes = slice(side * LANES, (side + 1) * LANES)

            @pl.when(own == 1)
            def _():
                kept_narrow[here, lanes] = part

            @pl.when(own == 0)
            def _():
                sent[here, width + lanes.start : width + lanes.stop] = part.astype(BF16)


def backward_kernel(member, grad_pre, hidden_weight, normed, gain, deviation, adj_t, *refs):
    before, (small, inner, near, far, product, rows_grad) = refs[:-6], refs[-6:]
    nodes, width = inner.shape
    points = adj_t.shape[1]
    inverse_gain = 1.0 / gain[...]
    for column in range(0, width, 256):
        columns = slice(column, column + 256)
        product[:, columns] = dot(
            grad_pre[member * points : (member + 1) * points, :], hidden_weight[columns, :], ((1,), (1,))
        )

    def step(index, total):
        here = pl.ds(pl.multiple_of(index * 32, 32), 32)
        there = pl.ds(pl.multiple_of(member * points + index * 32, 32), 32)
        value = product[here, :]
        zn = normed[there, :].astype(F32)
        both = value * zn
        scaled = value * gain[...]
        mean = jnp.sum(scaled, axis=1, keepdims=True) * (1.0 / width)
        slant = jnp.sum(both, axis=1, keepdims=True) * (1.0 / width)
        grad = deviation[there, :] * (scaled - mean - (zn * inverse_gain) * slant)
        rows_grad[here, :] = grad.astype(BF16)
        return total + jnp.sum(both.reshape(4, 8, width), axis=0)

    total = before[0][...] if before else jnp.zeros((8, width), F32)
    total = lax.fori_loop(0, points // 32, step, total, unroll=4)
    value = dot(adj_t[...], rows_grad[...])
    value = value[:LANES] + value[LANES:]
    below, above = value[:RIM], value[RIM + nodes : nodes + 2 * RIM]
    odd = (here_index() & 1) == 1
    near[...] = jnp.where(odd, below, above).astype(BF16)
    far[...] = jnp.where(odd, above, below).astype(BF16)
    inner[...] = value[RIM : RIM + nodes]
    if not before:
        small[...] = total
        return
    row = jnp.concatenate(
        [
            jnp.sum(total, axis=0, keepdims=True) * inverse_gain,
            jnp.broadcast_to(before[1][...], (1, small.shape[1] - width)),
        ],
        axis=1,
    )
    upper = row.astype(BF16).astype(F32)
    index = jax.lax.broadcasted_iota(jnp.int32, (8, row.shape[1]), 0)
    small[...] = jnp.where(index == 0, upper, jnp.where(index == 1, row - upper, 0.0)).astype(BF16)


def add_rims(inner, near, far, grad_latent):
    members, nodes = grad_latent.shape[:2]
    odd = (here_index() & 1) == 1
    for member in range(members):
        low = jnp.where(odd, near[member].astype(F32), far[member].astype(F32))
        high = jnp.where(odd, far[member].astype(F32), near[member].astype(F32))
        value = inner[member]
        grad_latent[member, :RIM, :] = value[:RIM, :] + low
        grad_latent[member, RIM : nodes - RIM, :] = value[RIM : nodes - RIM, :]
        grad_latent[member, nodes - RIM :, :] = value[nodes - RIM :, :] + high


def write_rows(count, chunk, side, source, target, wide, start, sems):
    width = target.shape[1]
    first, rows = chunks(width, count)[chunk]
    size = rows >> (count - 1)
    half = core_index() ^ side
    mask = jnp.where(half == 0, turn(count, here_index(), 0), turn(count, here_index(), 1))
    copies = []
    for block in range(rows // size):
        here = slice(block * size, (block + 1) * size)
        there = slice(start + block * size, start + (block + 1) * size)
        wide[there, :] = source[here, :width].astype(F32)
        row = half * (width // 2) + first + (block ^ mask) * size
        copy = pltpu.make_async_copy(
            wide.at[there, :],
            target.at[pl.ds(pl.multiple_of(row, size), size), :],
            sems.at[block],
        )
        copy.start()
        copies.append(copy)
    return copies


def write_kernel(count, pieces, members, *refs):
    sources, inner, (near, far) = refs[: len(pieces)], refs[len(pieces) :][:members], refs[len(pieces) + members :][:2]
    target, target_latent, wide, grad_latent, sems, last_sems = refs[len(pieces) + members + 2 :]
    add_rims(inner, near, far, grad_latent)
    copies = fetch((grad_latent,), (target_latent,), last_sems)
    start = 0
    for i, ((chunk, side), source) in enumerate(zip(pieces, sources)):
        copies += write_rows(count, chunk, side, source, target, wide, start, sems.at[i])
        start += source.shape[0]
    for copy in copies:
        copy.wait()


def last_write_kernel(
    count, own, other, small, other_small, before,
    target, grad_out_t, grad_gain, loss,
    wide, narrow, narrow_t, gain_row, loss_cell, sems, last_sems,
):
    del before
    width = target.shape[1]
    last = len(chunks(width, count)) - 1
    copies = write_rows(count, last, 1, other, target, wide, 0, sems)
    for starts, size, mine, place_row in narrow_rows(count, width):
        here = pl.ds(place_row, size)
        for side, row in enumerate(starts):
            lanes = slice(width + side * LANES, width + (side + 1) * LANES)
            value = jnp.where(mine == 1, own[here, lanes].astype(F32), other[here, lanes].astype(F32))
            narrow[row : row + size, :] = value
    narrow_t[...] = narrow[...].T[: grad_out_t.shape[0], :]
    total = small[...].astype(F32) + other_small[...].astype(F32)
    total = total[:1] + total[1:2]
    gain_row[...] = total[:, :width]
    loss_cell[...] = total[:, width : width + 1]
    copies += fetch((narrow_t, gain_row, loss_cell), (grad_out_t, grad_gain, loss), last_sems)
    for copy in copies:
        copy.wait()


def add_parts(mine, other):
    return (mine.astype(F32) + other.astype(F32)).astype(BF16)


def unpack(small):
    return small[:1].astype(F32) + small[1:2].astype(F32)


def swap_with(value, small, bits):
    rows = value.shape[0]
    other = swap_bits(jnp.concatenate([value, small]), bits)
    total = unpack(small) + unpack(other[rows:])
    upper = total.astype(BF16)
    lower = (total - upper.astype(F32)).astype(BF16)
    rest = jnp.zeros((small.shape[0] - 2, small.shape[1]), BF16)
    return other[:rows], jnp.concatenate([upper, lower, rest])


class Sum:
    def __init__(self, sent, kept, count):
        self.sent, self.value, self.small = sent, kept, None
        forth = orders(count)
        self.stages = forth + forth[-2::-1]
        self.halvings, self.stage = count - 1, 0

    def start(self, *others):
        rows = self.value.shape[0] // 2 if 0 < self.stage < self.halvings else 0
        sent = self.value[:rows] if rows else self.value
        if self.stage == 0:
            sent = self.sent
        if others:
            sent = after(sent, *others)
        bits = self.stages[self.stage]
        last = self.stage == len(self.stages) - 1
        if self.small is not None and (0 < self.stage <= self.halvings or last):
            self.other, self.small = swap_with(sent, self.small, bits)
        else:
            self.other = swap_bits(sent, bits)
        return sent

    def finish(self, *others):
        other = after(self.other, *others) if others else self.other
        if self.stage <= self.halvings:
            self.value = add_parts(self.value[-other.shape[0] :], other)
        else:
            self.value = jnp.concatenate([other, self.value])
        self.stage += 1


def after(value, *others):
    return lax.optimization_barrier((value, *others))[0]


def in_hbm(*values):
    return [pltpu.with_memory_space_constraint(value, pltpu.HBM) for value in values]


def local(
    latent,
    edge_node_index,
    edge_mask,
    edge_weight,
    valid,
    area,
    state,
    target,
    var_weight,
    gain,
    hidden_weight,
    output_weight,
):
    members, nodes, width = latent.shape
    points, variables = state.shape
    rows = members * points
    count = lax.axis_size("space").bit_length() - 1
    space = lax.axis_index("space")
    parts = chunks(width, count)
    odd = (space & 1) == 1
    low, high = latent[:, :RIM], latent[:, nodes - RIM :]
    near = swap_pairs(jnp.where(odd, low, high), "space", 0)
    far = swap_pairs(jnp.where(odd, high, low), "space", 1)

    adj, adj_t, score_weight, projection, gain, own, base, hidden_weight = pl.pallas_call(
        prepare_kernel,
        out_shape=(
            pltpu.VMEM((points, 2 * LANES), BF16),
            pltpu.VMEM((2 * LANES, points), BF16),
            pltpu.VMEM((variables, points), F32),
            pltpu.VMEM((LANES, width), BF16),
            pltpu.VMEM((1, width), F32),
            pltpu.VMEM(latent.shape, BF16),
            pltpu.VMEM((variables, points), F32),
            pltpu.VMEM((width, width), BF16),
        ),
        in_specs=[HBM] * 12,
        out_specs=(VMEM,) * 8,
        scratch_shapes=[
            pltpu.VMEM(edge_mask.T.shape, jnp.int32),
            pltpu.VMEM(edge_mask.T.shape, jnp.int32),
            pltpu.VMEM(edge_mask.T.shape, F32),
            pltpu.VMEM((1, points), jnp.int32),
            pltpu.VMEM((1, points), F32),
            pltpu.VMEM((1, variables), F32),
            pltpu.VMEM((variables, width), BF16),
            pltpu.VMEM((variables, points), F32),
            pltpu.VMEM((variables, points), F32),
            pltpu.SemaphoreType.DMA((12,)),
        ],
        compiler_params=PARAMS,
        name="prepare",
    )(
            *in_hbm(
            edge_node_index.T,
            edge_mask.T,
            edge_weight.T,
            valid.reshape(1, points),
            area.reshape(1, points),
            var_weight.reshape(1, variables),
            output_weight.T,
            gain.reshape(1, width),
            latent,
            state.T,
            target.T,
            hidden_weight,
        ),
    )
    normed, hidden, slope, outputs, deviation = pl.pallas_call(
        forward_kernel,
        out_shape=(
            pltpu.VMEM((rows, width), BF16),
            pltpu.VMEM((rows, width), BF16),
            pltpu.VMEM((rows, width), BF16),
            jax.ShapeDtypeStruct((members, variables, points), F32),
            pltpu.VMEM((rows, 1), F32),
        ),
        in_specs=[VMEM] * 7,
        out_specs=(VMEM,) * 5,
        scratch_shapes=[
            pltpu.VMEM((members, 2 * LANES, width), BF16),
            pltpu.VMEM((members, points, width), F32),
            pltpu.VMEM((points, LANES), F32),
        ],
        compiler_params=PARAMS,
        name="forward",
    )(adj, near, own, far, gain, hidden_weight, projection)
    others = swap_cores(outputs)
    normed_t, own_score, own_grad = pl.pallas_call(
        lambda *refs: transpose_kernel(count, *refs),
        out_shape=(
            pltpu.VMEM((width, rows), BF16),
            pltpu.VMEM((variables, points), F32),
            pltpu.VMEM((members, variables, points), F32),
        ),
        in_specs=[VMEM] * 3,
        out_specs=(VMEM,) * 3,
        compiler_params=PARAMS,
        cost_estimate=LIGHT,
        name="transpose",
    )(normed, outputs, base)
    loss, grad_pre, grad_pred_t, sent = pl.pallas_call(
        score_kernel,
        out_shape=(
            jax.ShapeDtypeStruct((1, 1), F32),
            pltpu.VMEM((rows, width), BF16),
            pltpu.VMEM((LANES, rows), BF16),
            jax.ShapeDtypeStruct((parts[0][1], width), BF16),
        ),
        in_specs=[VMEM] * 8,
        out_specs=(VMEM,) * 4,
        scratch_shapes=[pltpu.VMEM((rows, LANES), BF16), pltpu.VMEM((LANES, rows), F32)],
        compiler_params=PARAMS,
        name="score",
    )(outputs, others, own_score, own_grad, score_weight, projection, slope, normed_t)

    def product(first, size, received, *narrow):
        shape = jax.ShapeDtypeStruct((size // 2, received.shape[1]), BF16)
        return pl.pallas_call(
            lambda *refs: product_kernel(first, *refs),
            out_shape=(shape, shape),
            in_specs=[VMEM] * (3 + len(narrow)),
            out_specs=(VMEM, VMEM),
            compiler_params=PARAMS,
            cost_estimate=LIGHT,
            name="product",
        )(normed_t, grad_pre, received, *narrow)

    last = len(parts) - 1
    last_rows = parts[last][1]
    extra = LANES * (width // 2 // last_rows)
    received = swap_cores(sent)
    sent, kept_narrow = pl.pallas_call(
        lambda *refs: sent_kernel(count, *refs),
        out_shape=(
            jax.ShapeDtypeStruct((last_rows, width + extra), BF16),
            pltpu.VMEM((last_rows, extra), F32),
        ),
        in_specs=[VMEM] * 4,
        out_specs=(VMEM,) * 2,
        compiler_params=PARAMS,
        cost_estimate=LIGHT,
        name="sent",
    )(normed_t, grad_pre, grad_pred_t, hidden)
    sums, token = [], ()
    received = (received, swap_cores(sent))
    for chunk, (first, size) in enumerate(parts):
        narrow = [kept_narrow] if chunk == last else []
        sums.append(Sum(*product(width // 2 + first, size, after(received[chunk], *token), *narrow), count))
        token = (sums[-1].start(),)

    def backward(member, adj_t, *before):
        last = len(before) > 1
        return pl.pallas_call(
            lambda *refs: backward_kernel(member, *refs),
            out_shape=(
                jax.ShapeDtypeStruct((8, width + extra), BF16) if last else pltpu.VMEM((8, width), F32),
                pltpu.VMEM((nodes, width), F32),
                jax.ShapeDtypeStruct((RIM, width), BF16),
                jax.ShapeDtypeStruct((RIM, width), BF16),
            ),
            in_specs=[VMEM] * (6 + len(before)),
            out_specs=(VMEM,) * 4,
            scratch_shapes=[pltpu.VMEM((points, width), F32), pltpu.VMEM((points, width), BF16)],
            compiler_params=PARAMS,
            cost_estimate=LIGHT,
            name="backward",
        )(grad_pre, hidden_weight, normed, gain, deviation, adj_t, *before)

    done = []
    for stage in range(2 * count - 1):
        for chunk in range(last + 1):
            if stage == 0 and len(done) < members:
                before = (done[-1][0],) if done else ()
                if len(done) == members - 1:
                    before = before + (loss,)
                done.append(backward(len(done), after(adj_t, *token), *before))
                token = token + (done[-1][1],)
                if len(done) == members:
                    sums[last].small = done[-1][0]
            sums[chunk].finish(*(token if stage == 0 else ()))
            token = ()
            if stage < 2 * count - 2:
                token = (sums[chunk].start(),)
            if stage == 3 and chunk == last:
                inner, near, far = zip(*(part[1:] for part in done))
                near, far = after(jnp.stack(near), *token), after(jnp.stack(far), *token)
                near, far = swap_pairs(near, "space", 0), swap_pairs(far, "space", 1)
    own = [chunk.value for chunk in sums]
    other = [swap_cores(value) for value in own]
    small = sums[last].small
    other_small = swap_cores(small)
    hidden_shape = jax.ShapeDtypeStruct((width, width), F32)
    blocks = 1 << (count - 1)

    pieces = [(0, 0), (0, 1), (last, 0)]
    sources = [own[0], other[0], own[last]]
    latent_shape = (members, nodes, width)
    grad_hidden, grad_latent = pl.pallas_call(
        lambda *refs: write_kernel(count, pieces, members, *refs),
        out_shape=(hidden_shape, jax.ShapeDtypeStruct(latent_shape, F32)),
        in_specs=[VMEM] * (len(pieces) + members + 2),
        out_specs=(HBM, HBM),
        scratch_shapes=[
            pltpu.VMEM((sum(source.shape[0] for source in sources), width), F32),
            pltpu.VMEM(latent_shape, F32),
            pltpu.SemaphoreType.DMA((len(pieces), blocks)),
            pltpu.SemaphoreType.DMA((1,)),
        ],
        compiler_params=PARAMS,
        cost_estimate=LIGHT,
        name="write",
    )(*sources, *inner, near, far)
    grad_hidden, grad_out, grad_gain, loss = pl.pallas_call(
        lambda *refs: last_write_kernel(count, *refs),
        out_shape=(
            hidden_shape,
            jax.ShapeDtypeStruct((variables, width), F32),
            jax.ShapeDtypeStruct((1, width), F32),
            jax.ShapeDtypeStruct((1, 1), F32),
        ),
        in_specs=[VMEM] * 4 + [HBM],
        out_specs=(HBM,) * 4,
        scratch_shapes=[
            pltpu.VMEM((last_rows, width), F32),
            pltpu.VMEM((width, LANES), F32),
            pltpu.VMEM((variables, width), F32),
            pltpu.VMEM((1, width), F32),
            pltpu.VMEM((1, 1), F32),
            pltpu.SemaphoreType.DMA((blocks,)),
            pltpu.SemaphoreType.DMA((3,)),
        ],
        input_output_aliases={4: 0},
        compiler_params=PARAMS,
        name="last_write",
    )(own[last], other[last], small, other_small, grad_hidden)
    return (loss.reshape(1), grad_hidden, grad_out.T, grad_gain.reshape(width), grad_latent)


def solution(mesh):
    in_specs = (
        P(("groups", "member"), "space", None),
        P(("groups", "space"), None),
        P(("groups", "space"), None),
        P(("groups", "space"), None),
        P(("groups", "space")),
        P(("groups", "space")),
        P(("groups", "space"), None),
        P(("groups", "space"), None),
        P(),
        P(),
        P(),
        P(),
    )
    out_specs = (
        P("groups"),
        P("groups", None),
        P("groups", None),
        P("groups"),
        P(("groups", "member"), "space", None),
    )
    return jax.shard_map(local, mesh=mesh, in_specs=in_specs, out_specs=out_specs, check_vma=False)
```

```python
import jax
import jax.numpy as jnp
from jax import lax
from jax.experimental import pallas as pl
from jax.experimental.pallas import tpu as pltpu
from jax.sharding import PartitionSpec as P

RIM = 16
SMOOTH_SQ = 0.01
LANES = 128
BF16 = jnp.bfloat16
F32 = jnp.float32
VMEM = pl.BlockSpec(memory_space=pltpu.VMEM)
HBM = pl.BlockSpec(memory_space=pltpu.HBM)
PARAMS = pltpu.CompilerParams(vmem_limit_bytes=16 * 1024 * 1024)


def swap_pairs(value, axis, first):
    count = lax.axis_size(axis)
    pairs = [(i, i + 1) for i in range(first, count - 1, 2)]
    return lax.ppermute(value, axis, pairs + [(b, a) for a, b in pairs])


def swap_cores(value):
    return lax.ppermute(value, "member", [(0, 1), (1, 0)])


def swap_bits(value, bits):
    pairs = [
        (s * 2 + c, (s ^ (1 << bits[c])) * 2 + c)
        for s in range(lax.axis_size("space"))
        for c in range(2)
    ]
    return lax.ppermute(value, ("space", "member"), pairs)


def orders(count):
    return [(0, 1), (1, 0)] + [(bit, bit) for bit in range(2, count)]


LIGHT = pl.CostEstimate(flops=1, bytes_accessed=1, transcendentals=0)


def here_index():
    return lax.axis_index("space")


def core_index():
    return lax.axis_index("member")


def chunks(width, count):
    half, unit = width // 2, 16 << (count - 1)
    last = max(unit, half // 2)
    return [(0, half - last), (half - last, last)]


def turn(count, space, half):
    value = 0
    stages = orders(count)[:-1]
    for level, bits in enumerate(stages):
        value = value + ((1 - ((space >> bits[half]) & 1)) << (len(stages) - 1 - level))
    return value


def dot(a, b, dims=((1,), (0,))):
    return lax.dot_general(a, b, (dims, ((), ())), preferred_element_type=F32)


def fetch(sources, targets, sems):
    copies = [
        pltpu.make_async_copy(source, target, sems.at[i])
        for i, (source, target) in enumerate(zip(sources, targets))
    ]
    for copy in copies:
        copy.start()
    return copies


def prepare_kernel(
    index_in, mask_in, weight_in, valid_in, area_in, var_weight_in, projection_in, gain_in, own_in, state_in, target_in,
    hidden_weight_in, adj, adj_t, score_weight, projection, gain, own, base, hidden_weight,
    index, mask, weight, valid, area, var_weight, narrow, state, target, sems,
):
    sources = (
        index_in, mask_in, weight_in, valid_in, area_in, var_weight_in, projection_in, gain_in, own_in,
        state_in, target_in, hidden_weight_in,
    )
    targets = (index, mask, weight, valid, area, var_weight, narrow, gain, own, state, target, hidden_weight)
    copies = fetch(sources, targets, sems)
    for copy in copies[:6]:
        copy.wait()
    points = index.shape[1]
    variables = narrow.shape[0]
    nodes = jax.lax.broadcasted_iota(jnp.int32, (LANES, points), 0) + (here_index() * (own.shape[1]) - RIM)
    total = jnp.zeros((LANES, points), F32)
    for slot in range(index.shape[0]):
        coefficient = weight[slot : slot + 1, :] * mask[slot : slot + 1, :].astype(F32)
        total = total + jnp.where(index[slot : slot + 1, :] == nodes, coefficient, 0.0)
    upper = total.astype(BF16).astype(F32)
    lower = total - upper
    adj_t[:LANES, :] = upper.astype(BF16)
    adj_t[LANES:, :] = lower.astype(BF16)
    adj[:, :LANES] = upper.T.astype(BF16)
    adj[:, LANES:] = lower.T.astype(BF16)
    diagonal = jax.lax.broadcasted_iota(jnp.int32, (variables, variables), 0) == (
        jax.lax.broadcasted_iota(jnp.int32, (variables, variables), 1)
    )
    column = jnp.sum(jnp.where(diagonal, var_weight[...], 0.0), axis=1, keepdims=True)
    score_weight[...] = column * (valid[...].astype(F32) * area[...] / points)
    copies[6].wait()
    projection[...] = jnp.zeros_like(projection)
    projection[:variables, :] = narrow[...]
    for copy in copies[7:]:
        copy.wait()
    base[...] = state[...] - target[...]


def forward_kernel(
    adj, near, own, far, gain, hidden_weight, output_weight,
    normed, hidden, slope, outputs, deviation, extended, summed, projected,
):
    members, nodes, width = own.shape
    points = adj.shape[0]
    tile = 512
    odd = (here_index() & 1) == 1
    for member in range(members):
        for part in range(2):
            start = part * LANES
            extended[member, start : start + RIM, :] = jnp.where(odd, near[member], far[member])
            extended[member, start + RIM : start + RIM + nodes, :] = own[member]
            extended[member, start + RIM + nodes : start + 2 * RIM + nodes, :] = jnp.where(
                odd, far[member], near[member]
            )
            extended[member, start + 2 * RIM + nodes : start + LANES, :] = jnp.zeros(
                (LANES - 2 * RIM - nodes, width), BF16
            )

    def gather(member):
        summed[member] = dot(adj[...], extended[member])

    def norm(member, first, size):
        for row in range(first, first + size, 32):
            value = summed[member, row : row + 32, :]
            value = value - jnp.sum(value, axis=1, keepdims=True) * (1.0 / width)
            spread = jnp.sum(value * value, axis=1, keepdims=True) * (1.0 / width)
            inverse = lax.rsqrt(spread + 1e-05)
            target = slice(member * points + row, member * points + row + 32)
            deviation[target, :] = inverse
            normed[target, :] = (value * inverse * gain[...]).astype(BF16)

    def layer(member, column):
        rows = slice(member * points, (member + 1) * points)
        columns = slice(column, column + tile)
        pre = dot(normed[rows, :], hidden_weight[:, columns])
        sig = 0.5 * jnp.tanh(0.5 * pre) + 0.5
        hid = pre * sig
        slope[rows, columns] = (sig + hid * (1.0 - sig)).astype(BF16)
        hid = hid.astype(BF16)
        hidden[rows, columns] = hid
        term = dot(hid, output_weight[:, columns], ((1,), (1,)))
        if column == 0:
            projected[...] = term
        else:
            projected[...] += term

    gather(0)
    norm(0, 0, points)
    for member in range(members):
        if member + 1 < members:
            gather(member + 1)
        for column in range(0, width, tile):
            if member + 1 < members:
                size = points * tile // width
                norm(member + 1, points * column // width, size)
            layer(member, column)
        outputs[member] = projected[...].T[: outputs.shape[1], :]


def own_rows(count, width):
    half_rows = width // 2
    for half in range(2):
        mask = turn(count, here_index(), half)
        for first, rows in chunks(width, count):
            size = rows >> (count - 1)
            for block in range(rows // size):
                start = (1 - (core_index() ^ half)) * half_rows + first + (block ^ mask) * size
                yield half * half_rows + first + block * size, size, pl.multiple_of(start, size)


def narrow_rows(count, width):
    rows = chunks(width, count)[-1][1]
    size = rows >> (count - 1)
    sides = width // 2 // rows
    for half in range(2):
        mask = turn(count, here_index(), half)
        for block in range(rows // size):
            row = half * (width // 2) + block * sides * size
            starts = tuple(row + side * size for side in range(sides))
            yield starts, size, 1 - (core_index() ^ half), pl.multiple_of((block ^ mask) * size, size)


def smooth(diff):
    square = diff * diff + SMOOTH_SQ
    inverse = lax.rsqrt(square)
    return square * inverse, diff * inverse


def transpose_kernel(count, normed, outputs, base, normed_t, own_score, own_grad):
    width = normed.shape[1]
    members, variables, points = outputs.shape
    total = 2 * members
    values = [outputs[m] for m in range(members)]
    zero = jnp.zeros((variables, points), F32)
    grads, pair_grads = [zero] * members, [zero] * members
    errors, pairs = zero, jnp.full((variables, points), members * SMOOTH_SQ**0.5, F32)
    for m in range(members):
        size, grads[m] = smooth(values[m] + base[...])
        errors = errors + size
        for n in range(m + 1, members):
            size, grad = smooth(values[m] - values[n])
            pairs = pairs + 2.0 * size
            pair_grads[m] = pair_grads[m] + grad
            pair_grads[n] = pair_grads[n] - grad
    own_score[...] = errors * (1.0 / total) - pairs * (1.0 / (2.0 * total * (total - 1)))
    for m in range(members):
        own_grad[m] = grads[m] * (1.0 / total) - pair_grads[m] * (1.0 / (total * (total - 1)))
    blocks = {}
    for row, size, there in own_rows(count, width):
        stop = row + size
        while row < stop:
            group, offset = row // LANES, row % LANES
            if group not in blocks:
                blocks = {group: normed[:, group * LANES : (group + 1) * LANES].T}
            part = min(stop - row, LANES - offset)
            normed_t[pl.ds(pl.multiple_of(there, 16), part), :] = blocks[group][offset : offset + part]
            row, there = row + part, there + part


def score_kernel(
    outputs, others, own_score, own_grad, score_weight, output_weight, slope, normed_t,
    loss, grad_pre, grad_pred_t, sent,
    grad_pred, grad_wide,
):
    members, variables, points = outputs.shape
    width = slope.shape[1]
    total = 2 * members
    weight = score_weight[...]
    grad_wide[...] = jnp.zeros_like(grad_wide)
    grad_pred[...] = jnp.zeros_like(grad_pred)
    values = [outputs[m] for m in range(members)]
    pair_grads = [jnp.zeros((variables, points), F32) for _ in range(members)]
    pairs = jnp.zeros((variables, points), F32)
    for m in range(members):
        for n in range(members):
            size, grad = smooth(values[m] - others[n])
            pairs = pairs + size
            pair_grads[m] = pair_grads[m] + grad
    score = weight * (own_score[...] - pairs * (1.0 / (2.0 * total * (total - 1))))
    loss[...] = jnp.sum(jnp.sum(score, axis=0, keepdims=True), axis=1, keepdims=True)
    for m in range(members):
        grad = weight * (own_grad[m] - pair_grads[m] * (1.0 / (total * (total - 1))))
        columns = slice(m * points, (m + 1) * points)
        grad_wide[:variables, columns] = grad
        grad_pred[columns, :] = grad_wide[:, columns].T.astype(BF16)
    grad_pred_t[...] = grad_wide[...].astype(BF16)
    for m in range(members):
        rows = slice(m * points, (m + 1) * points)
        for column in range(0, width, 512):
            columns = slice(column, column + 512)
            grad_hid = dot(grad_pred[rows, :], output_weight[:, columns])
            grad_pre[rows, columns] = (grad_hid * slope[rows, columns].astype(F32)).astype(BF16)
    products(normed_t, grad_pre, slice(0, sent.shape[0]), sent)


def products(normed_t, grad_pre, rows, target):
    width = grad_pre.shape[1]
    for column in range(0, width, 512):
        columns = slice(column, column + 512)
        target[:, columns] = dot(normed_t[rows, :], grad_pre[:, columns]).astype(target.dtype)


def product_kernel(first, normed_t, grad_pre, received, *refs):
    narrow, (sent, kept) = refs[:-2], refs[-2:]
    width, rows = grad_pre.shape[1], sent.shape[0]
    for column in range(0, width, 512):
        columns = slice(column, column + 512)
        value = dot(normed_t[first : first + 2 * rows, :], grad_pre[:, columns])
        value = (value + received[:, columns].astype(F32)).astype(BF16)
        sent[:, columns] = value[:rows]
        kept[:, columns] = value[rows:]
    if narrow:
        value = (narrow[0][...] + received[:, width:].astype(F32)).astype(BF16)
        sent[:, width:] = value[:rows]
        kept[:, width:] = value[rows:]


def sent_kernel(count, normed_t, grad_pre, grad_pred_t, hidden, sent, kept_narrow):
    width = grad_pre.shape[1]
    first, rows = chunks(width, count)[-1]
    products(normed_t, grad_pre, slice(first, first + rows), sent)
    value = dot(grad_pred_t[...], hidden[...]).T
    for starts, size, own, place_row in narrow_rows(count, width):
        here = pl.ds(place_row, size)
        for side, row in enumerate(starts):
            part = value[row : row + size]
            lanes = slice(side * LANES, (side + 1) * LANES)

            @pl.when(own == 1)
            def _():
                kept_narrow[here, lanes] = part

            @pl.when(own == 0)
            def _():
                sent[here, width + lanes.start : width + lanes.stop] = part.astype(BF16)


def backward_kernel(member, grad_pre, hidden_weight, normed, gain, deviation, adj_t, *refs):
    before, (small, inner, near, far, product, rows_grad) = refs[:-6], refs[-6:]
    nodes, width = inner.shape
    points = adj_t.shape[1]
    inverse_gain = 1.0 / gain[...]
    for column in range(0, width, 512):
        columns = slice(column, column + 512)
        product[:, columns] = dot(
            grad_pre[member * points : (member + 1) * points, :], hidden_weight[columns, :], ((1,), (1,))
        )

    def step(index, total):
        here = pl.ds(pl.multiple_of(index * 32, 32), 32)
        there = pl.ds(pl.multiple_of(member * points + index * 32, 32), 32)
        value = product[here, :]
        zn = normed[there, :].astype(F32)
        both = value * zn
        scaled = value * gain[...]
        mean = jnp.sum(scaled, axis=1, keepdims=True) * (1.0 / width)
        slant = jnp.sum(both, axis=1, keepdims=True) * (1.0 / width)
        grad = deviation[there, :] * (scaled - mean - (zn * inverse_gain) * slant)
        rows_grad[here, :] = grad.astype(BF16)
        return total + jnp.sum(both.reshape(4, 8, width), axis=0)

    total = before[0][...] if before else jnp.zeros((8, width), F32)
    total = lax.fori_loop(0, points // 32, step, total, unroll=4)
    value = dot(adj_t[...], rows_grad[...])
    value = value[:LANES] + value[LANES:]
    below, above = value[:RIM], value[RIM + nodes : nodes + 2 * RIM]
    odd = (here_index() & 1) == 1
    near[...] = jnp.where(odd, below, above).astype(BF16)
    far[...] = jnp.where(odd, above, below).astype(BF16)
    inner[...] = value[RIM : RIM + nodes]
    if not before:
        small[...] = total
        return
    row = jnp.concatenate(
        [
            jnp.sum(total, axis=0, keepdims=True) * inverse_gain,
            jnp.broadcast_to(before[1][...], (1, small.shape[1] - width)),
        ],
        axis=1,
    )
    upper = row.astype(BF16).astype(F32)
    index = jax.lax.broadcasted_iota(jnp.int32, (8, row.shape[1]), 0)
    small[...] = jnp.where(index == 0, upper, jnp.where(index == 1, row - upper, 0.0)).astype(BF16)


def add_rims(inner, near, far, grad_latent):
    members, nodes = grad_latent.shape[:2]
    odd = (here_index() & 1) == 1
    for member in range(members):
        low = jnp.where(odd, near[member].astype(F32), far[member].astype(F32))
        high = jnp.where(odd, far[member].astype(F32), near[member].astype(F32))
        value = inner[member]
        grad_latent[member, :RIM, :] = value[:RIM, :] + low
        grad_latent[member, RIM : nodes - RIM, :] = value[RIM : nodes - RIM, :]
        grad_latent[member, nodes - RIM :, :] = value[nodes - RIM :, :] + high


def write_rows(count, chunk, side, source, target, wide, start, sems):
    width = target.shape[1]
    first, rows = chunks(width, count)[chunk]
    size = rows >> (count - 1)
    half = core_index() ^ side
    mask = jnp.where(half == 0, turn(count, here_index(), 0), turn(count, here_index(), 1))
    copies = []
    for block in range(rows // size):
        here = slice(block * size, (block + 1) * size)
        there = slice(start + block * size, start + (block + 1) * size)
        wide[there, :] = source[here, :width].astype(F32)
        row = half * (width // 2) + first + (block ^ mask) * size
        copy = pltpu.make_async_copy(
            wide.at[there, :],
            target.at[pl.ds(pl.multiple_of(row, size), size), :],
            sems.at[block],
        )
        copy.start()
        copies.append(copy)
    return copies


def write_kernel(count, pieces, members, *refs):
    sources, inner, (near, far) = refs[: len(pieces)], refs[len(pieces) :][:members], refs[len(pieces) + members :][:2]
    target, target_latent, wide, grad_latent, sems, last_sems = refs[len(pieces) + members + 2 :]
    add_rims(inner, near, far, grad_latent)
    copies = fetch((grad_latent,), (target_latent,), last_sems)
    start = 0
    for i, ((chunk, side), source) in enumerate(zip(pieces, sources)):
        copies += write_rows(count, chunk, side, source, target, wide, start, sems.at[i])
        start += source.shape[0]
    for copy in copies:
        copy.wait()


def last_write_kernel(
    count, own, other, small, other_small, before,
    target, grad_out_t, grad_gain, loss,
    wide, narrow, narrow_t, gain_row, loss_cell, sems, last_sems,
):
    del before
    width = target.shape[1]
    last = len(chunks(width, count)) - 1
    copies = write_rows(count, last, 1, other, target, wide, 0, sems)
    for starts, size, mine, place_row in narrow_rows(count, width):
        here = pl.ds(place_row, size)
        for side, row in enumerate(starts):
            lanes = slice(width + side * LANES, width + (side + 1) * LANES)
            value = jnp.where(mine == 1, own[here, lanes].astype(F32), other[here, lanes].astype(F32))
            narrow[row : row + size, :] = value
    narrow_t[...] = narrow[...].T[: grad_out_t.shape[0], :]
    total = small[...].astype(F32) + other_small[...].astype(F32)
    total = total[:1] + total[1:2]
    gain_row[...] = total[:, :width]
    loss_cell[...] = total[:, width : width + 1]
    copies += fetch((narrow_t, gain_row, loss_cell), (grad_out_t, grad_gain, loss), last_sems)
    for copy in copies:
        copy.wait()


def add_parts(mine, other):
    return (mine.astype(F32) + other.astype(F32)).astype(BF16)


def unpack(small):
    return small[:1].astype(F32) + small[1:2].astype(F32)


def swap_with(value, small, bits):
    rows = value.shape[0]
    other = swap_bits(jnp.concatenate([value, small]), bits)
    total = unpack(small) + unpack(other[rows:])
    upper = total.astype(BF16)
    lower = (total - upper.astype(F32)).astype(BF16)
    rest = jnp.zeros((small.shape[0] - 2, small.shape[1]), BF16)
    return other[:rows], jnp.concatenate([upper, lower, rest])


class Sum:
    def __init__(self, sent, kept, count):
        self.sent, self.value, self.small = sent, kept, None
        forth = orders(count)
        self.stages = forth + forth[-2::-1]
        self.halvings, self.stage = count - 1, 0

    def start(self, *others):
        rows = self.value.shape[0] // 2 if 0 < self.stage < self.halvings else 0
        sent = self.value[:rows] if rows else self.value
        if self.stage == 0:
            sent = self.sent
        if others:
            sent = after(sent, *others)
        bits = self.stages[self.stage]
        last = self.stage == len(self.stages) - 1
        if self.small is not None and (0 < self.stage <= self.halvings or last):
            self.other, self.small = swap_with(sent, self.small, bits)
        else:
            self.other = swap_bits(sent, bits)
        return sent

    def finish(self, *others):
        other = after(self.other, *others) if others else self.other
        if self.stage <= self.halvings:
            self.value = add_parts(self.value[-other.shape[0] :], other)
        else:
            self.value = jnp.concatenate([other, self.value])
        self.stage += 1


def after(value, *others):
    return lax.optimization_barrier((value, *others))[0]


def in_hbm(*values):
    return [pltpu.with_memory_space_constraint(value, pltpu.HBM) for value in values]


def local(
    latent,
    edge_node_index,
    edge_mask,
    edge_weight,
    valid,
    area,
    state,
    target,
    var_weight,
    gain,
    hidden_weight,
    output_weight,
):
    members, nodes, width = latent.shape
    points, variables = state.shape
    rows = members * points
    count = lax.axis_size("space").bit_length() - 1
    space = lax.axis_index("space")
    parts = chunks(width, count)
    odd = (space & 1) == 1
    low, high = latent[:, :RIM], latent[:, nodes - RIM :]
    near = swap_pairs(jnp.where(odd, low, high), "space", 0)
    far = swap_pairs(jnp.where(odd, high, low), "space", 1)

    adj, adj_t, score_weight, projection, gain, own, base, hidden_weight = pl.pallas_call(
        prepare_kernel,
        out_shape=(
            pltpu.VMEM((points, 2 * LANES), BF16),
            pltpu.VMEM((2 * LANES, points), BF16),
            pltpu.VMEM((variables, points), F32),
            pltpu.VMEM((LANES, width), BF16),
            pltpu.VMEM((1, width), F32),
            pltpu.VMEM(latent.shape, BF16),
            pltpu.VMEM((variables, points), F32),
            pltpu.VMEM((width, width), BF16),
        ),
        in_specs=[HBM] * 12,
        out_specs=(VMEM,) * 8,
        scratch_shapes=[
            pltpu.VMEM(edge_mask.T.shape, jnp.int32),
            pltpu.VMEM(edge_mask.T.shape, jnp.int32),
            pltpu.VMEM(edge_mask.T.shape, F32),
            pltpu.VMEM((1, points), jnp.int32),
            pltpu.VMEM((1, points), F32),
            pltpu.VMEM((1, variables), F32),
            pltpu.VMEM((variables, width), BF16),
            pltpu.VMEM((variables, points), F32),
            pltpu.VMEM((variables, points), F32),
            pltpu.SemaphoreType.DMA((12,)),
        ],
        compiler_params=PARAMS,
        name="prepare",
    )(
            *in_hbm(
            edge_node_index.T,
            edge_mask.T,
            edge_weight.T,
            valid.reshape(1, points),
            area.reshape(1, points),
            var_weight.reshape(1, variables),
            output_weight.T,
            gain.reshape(1, width),
            latent,
            state.T,
            target.T,
            hidden_weight,
        ),
    )
    normed, hidden, slope, outputs, deviation = pl.pallas_call(
        forward_kernel,
        out_shape=(
            pltpu.VMEM((rows, width), BF16),
            pltpu.VMEM((rows, width), BF16),
            pltpu.VMEM((rows, width), BF16),
            jax.ShapeDtypeStruct((members, variables, points), F32),
            pltpu.VMEM((rows, 1), F32),
        ),
        in_specs=[VMEM] * 7,
        out_specs=(VMEM,) * 5,
        scratch_shapes=[
            pltpu.VMEM((members, 2 * LANES, width), BF16),
            pltpu.VMEM((members, points, width), F32),
            pltpu.VMEM((points, LANES), F32),
        ],
        compiler_params=PARAMS,
        name="forward",
    )(adj, near, own, far, gain, hidden_weight, projection)
    others = swap_cores(outputs)
    normed_t, own_score, own_grad = pl.pallas_call(
        lambda *refs: transpose_kernel(count, *refs),
        out_shape=(
            pltpu.VMEM((width, rows), BF16),
            pltpu.VMEM((variables, points), F32),
            pltpu.VMEM((members, variables, points), F32),
        ),
        in_specs=[VMEM] * 3,
        out_specs=(VMEM,) * 3,
        compiler_params=PARAMS,
        cost_estimate=LIGHT,
        name="transpose",
    )(normed, outputs, base)
    loss, grad_pre, grad_pred_t, sent = pl.pallas_call(
        score_kernel,
        out_shape=(
            jax.ShapeDtypeStruct((1, 1), F32),
            pltpu.VMEM((rows, width), BF16),
            pltpu.VMEM((LANES, rows), BF16),
            jax.ShapeDtypeStruct((parts[0][1], width), BF16),
        ),
        in_specs=[VMEM] * 8,
        out_specs=(VMEM,) * 4,
        scratch_shapes=[pltpu.VMEM((rows, LANES), BF16), pltpu.VMEM((LANES, rows), F32)],
        compiler_params=PARAMS,
        name="score",
    )(outputs, others, own_score, own_grad, score_weight, projection, slope, normed_t)

    def product(first, size, received, *narrow):
        shape = jax.ShapeDtypeStruct((size // 2, received.shape[1]), BF16)
        return pl.pallas_call(
            lambda *refs: product_kernel(first, *refs),
            out_shape=(shape, shape),
            in_specs=[VMEM] * (3 + len(narrow)),
            out_specs=(VMEM, VMEM),
            compiler_params=PARAMS,
            cost_estimate=LIGHT,
            name="product",
        )(normed_t, grad_pre, received, *narrow)

    last = len(parts) - 1
    last_rows = parts[last][1]
    extra = LANES * (width // 2 // last_rows)
    received = swap_cores(sent)
    sent, kept_narrow = pl.pallas_call(
        lambda *refs: sent_kernel(count, *refs),
        out_shape=(
            jax.ShapeDtypeStruct((last_rows, width + extra), BF16),
            pltpu.VMEM((last_rows, extra), F32),
        ),
        in_specs=[VMEM] * 4,
        out_specs=(VMEM,) * 2,
        compiler_params=PARAMS,
        cost_estimate=LIGHT,
        name="sent",
    )(normed_t, grad_pre, grad_pred_t, hidden)
    sums, token = [], ()
    received = (received, swap_cores(sent))
    for chunk, (first, size) in enumerate(parts):
        narrow = [kept_narrow] if chunk == last else []
        sums.append(Sum(*product(width // 2 + first, size, after(received[chunk], *token), *narrow), count))
        token = (sums[-1].start(),)

    def backward(member, adj_t, *before):
        last = len(before) > 1
        return pl.pallas_call(
            lambda *refs: backward_kernel(member, *refs),
            out_shape=(
                jax.ShapeDtypeStruct((8, width + extra), BF16) if last else pltpu.VMEM((8, width), F32),
                pltpu.VMEM((nodes, width), F32),
                jax.ShapeDtypeStruct((RIM, width), BF16),
                jax.ShapeDtypeStruct((RIM, width), BF16),
            ),
            in_specs=[VMEM] * (6 + len(before)),
            out_specs=(VMEM,) * 4,
            scratch_shapes=[pltpu.VMEM((points, width), F32), pltpu.VMEM((points, width), BF16)],
            compiler_params=PARAMS,
            cost_estimate=LIGHT,
            name="backward",
        )(grad_pre, hidden_weight, normed, gain, deviation, adj_t, *before)

    done = []
    for stage in range(2 * count - 1):
        for chunk in range(last + 1):
            if stage == 0 and len(done) < members:
                before = (done[-1][0],) if done else ()
                if len(done) == members - 1:
                    before = before + (loss,)
                done.append(backward(len(done), after(adj_t, *token), *before))
                token = token + (done[-1][1],)
                if len(done) == members:
                    sums[last].small = done[-1][0]
            sums[chunk].finish(*(token if stage == 0 else ()))
            token = ()
            if stage < 2 * count - 2:
                token = (sums[chunk].start(),)
            if stage == 3 and chunk == last:
                inner, near, far = zip(*(part[1:] for part in done))
                near, far = after(jnp.stack(near), *token), after(jnp.stack(far), *token)
                near, far = swap_pairs(near, "space", 0), swap_pairs(far, "space", 1)
    own = [chunk.value for chunk in sums]
    other = [swap_cores(value) for value in own]
    small = sums[last].small
    other_small = swap_cores(small)
    hidden_shape = jax.ShapeDtypeStruct((width, width), F32)
    blocks = 1 << (count - 1)

    pieces = [(0, 0), (0, 1), (last, 0)]
    sources = [own[0], other[0], own[last]]
    latent_shape = (members, nodes, width)
    grad_hidden, grad_latent = pl.pallas_call(
        lambda *refs: write_kernel(count, pieces, members, *refs),
        out_shape=(hidden_shape, jax.ShapeDtypeStruct(latent_shape, F32)),
        in_specs=[VMEM] * (len(pieces) + members + 2),
        out_specs=(HBM, HBM),
        scratch_shapes=[
            pltpu.VMEM((sum(source.shape[0] for source in sources), width), F32),
            pltpu.VMEM(latent_shape, F32),
            pltpu.SemaphoreType.DMA((len(pieces), blocks)),
            pltpu.SemaphoreType.DMA((1,)),
        ],
        compiler_params=PARAMS,
        cost_estimate=LIGHT,
        name="write",
    )(*sources, *inner, near, far)
    grad_hidden, grad_out, grad_gain, loss = pl.pallas_call(
        lambda *refs: last_write_kernel(count, *refs),
        out_shape=(
            hidden_shape,
            jax.ShapeDtypeStruct((variables, width), F32),
            jax.ShapeDtypeStruct((1, width), F32),
            jax.ShapeDtypeStruct((1, 1), F32),
        ),
        in_specs=[VMEM] * 4 + [HBM],
        out_specs=(HBM,) * 4,
        scratch_shapes=[
            pltpu.VMEM((last_rows, width), F32),
            pltpu.VMEM((width, LANES), F32),
            pltpu.VMEM((variables, width), F32),
            pltpu.VMEM((1, width), F32),
            pltpu.VMEM((1, 1), F32),
            pltpu.SemaphoreType.DMA((blocks,)),
            pltpu.SemaphoreType.DMA((3,)),
        ],
        input_output_aliases={4: 0},
        compiler_params=PARAMS,
        name="last_write",
    )(own[last], other[last], small, other_small, grad_hidden)
    return (loss.reshape(1), grad_hidden, grad_out.T, grad_gain.reshape(width), grad_latent)


def solution(mesh):
    in_specs = (
        P(("groups", "member"), "space", None),
        P(("groups", "space"), None),
        P(("groups", "space"), None),
        P(("groups", "space"), None),
        P(("groups", "space")),
        P(("groups", "space")),
        P(("groups", "space"), None),
        P(("groups", "space"), None),
        P(),
        P(),
        P(),
        P(),
    )
    out_specs = (
        P("groups"),
        P("groups", None),
        P("groups", None),
        P("groups"),
        P(("groups", "member"), "space", None),
    )
    return jax.shard_map(local, mesh=mesh, in_specs=in_specs, out_specs=out_specs, check_vma=False)
```

```python
import jax
import jax.numpy as jnp
from jax import lax
from jax.experimental import pallas as pl
from jax.experimental.pallas import tpu as pltpu
from jax.sharding import PartitionSpec as P

RIM = 16
SMOOTH_SQ = 0.01
LANES = 128
BF16 = jnp.bfloat16
F32 = jnp.float32
VMEM = pl.BlockSpec(memory_space=pltpu.VMEM)
HBM = pl.BlockSpec(memory_space=pltpu.HBM)
PARAMS = pltpu.CompilerParams(vmem_limit_bytes=16 * 1024 * 1024)


def swap_pairs(value, axis, first):
    count = lax.axis_size(axis)
    pairs = [(i, i + 1) for i in range(first, count - 1, 2)]
    return lax.ppermute(value, axis, pairs + [(b, a) for a, b in pairs])


def swap_cores(value):
    return lax.ppermute(value, "member", [(0, 1), (1, 0)])


def swap_bits(value, bits):
    pairs = [
        (s * 2 + c, (s ^ (1 << bits[c])) * 2 + c)
        for s in range(lax.axis_size("space"))
        for c in range(2)
    ]
    return lax.ppermute(value, ("space", "member"), pairs)


def orders(count):
    return [(0, 1), (1, 0)] + [(bit, bit) for bit in range(2, count)]


LIGHT = pl.CostEstimate(flops=1, bytes_accessed=1, transcendentals=0)


def here_index():
    return lax.axis_index("space")


def core_index():
    return lax.axis_index("member")


def chunks(width, count):
    half, unit = width // 2, 16 << (count - 1)
    last = max(unit, half // 2)
    return [(0, half - last), (half - last, last)]


def turn(count, space, half):
    value = 0
    stages = orders(count)[:-1]
    for level, bits in enumerate(stages):
        value = value + ((1 - ((space >> bits[half]) & 1)) << (len(stages) - 1 - level))
    return value


def dot(a, b, dims=((1,), (0,))):
    return lax.dot_general(a, b, (dims, ((), ())), preferred_element_type=F32)


def fetch(sources, targets, sems):
    copies = [
        pltpu.make_async_copy(source, target, sems.at[i])
        for i, (source, target) in enumerate(zip(sources, targets))
    ]
    for copy in copies:
        copy.start()
    return copies


def prepare_kernel(
    index_in, mask_in, weight_in, valid_in, area_in, var_weight_in, projection_in, gain_in, own_in, state_in, target_in,
    hidden_weight_in, adj, adj_t, score_weight, projection, gain, own, base, hidden_weight,
    index, mask, weight, valid, area, var_weight, narrow, state, target, sems,
):
    sources = (
        index_in, mask_in, weight_in, valid_in, area_in, var_weight_in, projection_in, gain_in, own_in,
        state_in, target_in, hidden_weight_in,
    )
    targets = (index, mask, weight, valid, area, var_weight, narrow, gain, own, state, target, hidden_weight)
    copies = fetch(sources, targets, sems)
    for copy in copies[:6]:
        copy.wait()
    points = index.shape[1]
    variables = narrow.shape[0]
    nodes = jax.lax.broadcasted_iota(jnp.int32, (LANES, points), 0) + (here_index() * (own.shape[1]) - RIM)
    total = jnp.zeros((LANES, points), F32)
    for slot in range(index.shape[0]):
        coefficient = weight[slot : slot + 1, :] * mask[slot : slot + 1, :].astype(F32)
        total = total + jnp.where(index[slot : slot + 1, :] == nodes, coefficient, 0.0)
    upper = total.astype(BF16).astype(F32)
    lower = total - upper
    adj_t[:LANES, :] = upper.astype(BF16)
    adj_t[LANES:, :] = lower.astype(BF16)
    adj[:, :LANES] = upper.T.astype(BF16)
    adj[:, LANES:] = lower.T.astype(BF16)
    diagonal = jax.lax.broadcasted_iota(jnp.int32, (variables, variables), 0) == (
        jax.lax.broadcasted_iota(jnp.int32, (variables, variables), 1)
    )
    column = jnp.sum(jnp.where(diagonal, var_weight[...], 0.0), axis=1, keepdims=True)
    score_weight[...] = column * (valid[...].astype(F32) * area[...] / points)
    copies[6].wait()
    projection[...] = jnp.zeros_like(projection)
    projection[:variables, :] = narrow[...]
    for copy in copies[7:]:
        copy.wait()
    base[...] = state[...] - target[...]


def forward_kernel(
    adj, near, own, far, gain, hidden_weight, output_weight,
    normed, hidden, slope, outputs, deviation, extended, summed, projected,
):
    members, nodes, width = own.shape
    points = adj.shape[0]
    tile = 1024
    odd = (here_index() & 1) == 1
    for member in range(members):
        for part in range(2):
            start = part * LANES
            extended[member, start : start + RIM, :] = jnp.where(odd, near[member], far[member])
            extended[member, start + RIM : start + RIM + nodes, :] = own[member]
            extended[member, start + RIM + nodes : start + 2 * RIM + nodes, :] = jnp.where(
                odd, far[member], near[member]
            )
            extended[member, start + 2 * RIM + nodes : start + LANES, :] = jnp.zeros(
                (LANES - 2 * RIM - nodes, width), BF16
            )

    def gather(member):
        summed[member] = dot(adj[...], extended[member])

    def norm(member, first, size):
        for row in range(first, first + size, 32):
            value = summed[member, row : row + 32, :]
            value = value - jnp.sum(value, axis=1, keepdims=True) * (1.0 / width)
            spread = jnp.sum(value * value, axis=1, keepdims=True) * (1.0 / width)
            inverse = lax.rsqrt(spread + 1e-05)
            target = slice(member * points + row, member * points + row + 32)
            deviation[target, :] = inverse
            normed[target, :] = (value * inverse * gain[...]).astype(BF16)

    def layer(member, column):
        rows = slice(member * points, (member + 1) * points)
        columns = slice(column, column + tile)
        pre = dot(normed[rows, :], hidden_weight[:, columns])
        sig = 0.5 * jnp.tanh(0.5 * pre) + 0.5
        hid = pre * sig
        slope[rows, columns] = (sig + hid * (1.0 - sig)).astype(BF16)
        hid = hid.astype(BF16)
        hidden[rows, columns] = hid
        term = dot(hid, output_weight[:, columns], ((1,), (1,)))
        if column == 0:
            projected[...] = term
        else:
            projected[...] += term

    gather(0)
    norm(0, 0, points)
    for member in range(members):
        if member + 1 < members:
            gather(member + 1)
        for column in range(0, width, tile):
            if member + 1 < members:
                size = points * tile // width
                norm(member + 1, points * column // width, size)
            layer(member, column)
        outputs[member] = projected[...].T[: outputs.shape[1], :]


def own_rows(count, width):
    half_rows = width // 2
    for half in range(2):
        mask = turn(count, here_index(), half)
        for first, rows in chunks(width, count):
            size = rows >> (count - 1)
            for block in range(rows // size):
                start = (1 - (core_index() ^ half)) * half_rows + first + (block ^ mask) * size
                yield half * half_rows + first + block * size, size, pl.multiple_of(start, size)


def narrow_rows(count, width):
    rows = chunks(width, count)[-1][1]
    size = rows >> (count - 1)
    sides = width // 2 // rows
    for half in range(2):
        mask = turn(count, here_index(), half)
        for block in range(rows // size):
            row = half * (width // 2) + block * sides * size
            starts = tuple(row + side * size for side in range(sides))
            yield starts, size, 1 - (core_index() ^ half), pl.multiple_of((block ^ mask) * size, size)


def smooth(diff):
    square = diff * diff + SMOOTH_SQ
    inverse = lax.rsqrt(square)
    return square * inverse, diff * inverse


def transpose_kernel(count, normed, outputs, base, normed_t, own_score, own_grad):
    width = normed.shape[1]
    members, variables, points = outputs.shape
    total = 2 * members
    values = [outputs[m] for m in range(members)]
    zero = jnp.zeros((variables, points), F32)
    grads, pair_grads = [zero] * members, [zero] * members
    errors, pairs = zero, jnp.full((variables, points), members * SMOOTH_SQ**0.5, F32)
    for m in range(members):
        size, grads[m] = smooth(values[m] + base[...])
        errors = errors + size
        for n in range(m + 1, members):
            size, grad = smooth(values[m] - values[n])
            pairs = pairs + 2.0 * size
            pair_grads[m] = pair_grads[m] + grad
            pair_grads[n] = pair_grads[n] - grad
    own_score[...] = errors * (1.0 / total) - pairs * (1.0 / (2.0 * total * (total - 1)))
    for m in range(members):
        own_grad[m] = grads[m] * (1.0 / total) - pair_grads[m] * (1.0 / (total * (total - 1)))
    blocks = {}
    for row, size, there in own_rows(count, width):
        stop = row + size
        while row < stop:
            group, offset = row // LANES, row % LANES
            if group not in blocks:
                blocks = {group: normed[:, group * LANES : (group + 1) * LANES].T}
            part = min(stop - row, LANES - offset)
            normed_t[pl.ds(pl.multiple_of(there, 16), part), :] = blocks[group][offset : offset + part]
            row, there = row + part, there + part


def score_kernel(
    outputs, others, own_score, own_grad, score_weight, output_weight, slope, normed_t,
    loss, grad_pre, grad_pred_t, sent,
    grad_pred, grad_wide,
):
    members, variables, points = outputs.shape
    width = slope.shape[1]
    total = 2 * members
    weight = score_weight[...]
    grad_wide[...] = jnp.zeros_like(grad_wide)
    grad_pred[...] = jnp.zeros_like(grad_pred)
    values = [outputs[m] for m in range(members)]
    pair_grads = [jnp.zeros((variables, points), F32) for _ in range(members)]
    pairs = jnp.zeros((variables, points), F32)
    for m in range(members):
        for n in range(members):
            size, grad = smooth(values[m] - others[n])
            pairs = pairs + size
            pair_grads[m] = pair_grads[m] + grad
    score = weight * (own_score[...] - pairs * (1.0 / (2.0 * total * (total - 1))))
    loss[...] = jnp.sum(jnp.sum(score, axis=0, keepdims=True), axis=1, keepdims=True)
    for m in range(members):
        grad = weight * (own_grad[m] - pair_grads[m] * (1.0 / (total * (total - 1))))
        columns = slice(m * points, (m + 1) * points)
        grad_wide[:variables, columns] = grad
        grad_pred[columns, :] = grad_wide[:, columns].T.astype(BF16)
    grad_pred_t[...] = grad_wide[...].astype(BF16)
    for m in range(members):
        rows = slice(m * points, (m + 1) * points)
        for column in range(0, width, 512):
            columns = slice(column, column + 512)
            grad_hid = dot(grad_pred[rows, :], output_weight[:, columns])
            grad_pre[rows, columns] = (grad_hid * slope[rows, columns].astype(F32)).astype(BF16)
    products(normed_t, grad_pre, slice(0, sent.shape[0]), sent)


def products(normed_t, grad_pre, rows, target):
    width = grad_pre.shape[1]
    for column in range(0, width, 512):
        columns = slice(column, column + 512)
        target[:, columns] = dot(normed_t[rows, :], grad_pre[:, columns]).astype(target.dtype)


def product_kernel(first, normed_t, grad_pre, received, *refs):
    narrow, (sent, kept) = refs[:-2], refs[-2:]
    width, rows = grad_pre.shape[1], sent.shape[0]
    for column in range(0, width, 512):
        columns = slice(column, column + 512)
        value = dot(normed_t[first : first + 2 * rows, :], grad_pre[:, columns])
        value = (value + received[:, columns].astype(F32)).astype(BF16)
        sent[:, columns] = value[:rows]
        kept[:, columns] = value[rows:]
    if narrow:
        value = (narrow[0][...] + received[:, width:].astype(F32)).astype(BF16)
        sent[:, width:] = value[:rows]
        kept[:, width:] = value[rows:]


def sent_kernel(count, normed_t, grad_pre, grad_pred_t, hidden, sent, kept_narrow):
    width = grad_pre.shape[1]
    first, rows = chunks(width, count)[-1]
    products(normed_t, grad_pre, slice(first, first + rows), sent)
    value = dot(grad_pred_t[...], hidden[...]).T
    for starts, size, own, place_row in narrow_rows(count, width):
        here = pl.ds(place_row, size)
        for side, row in enumerate(starts):
            part = value[row : row + size]
            lanes = slice(side * LANES, (side + 1) * LANES)

            @pl.when(own == 1)
            def _():
                kept_narrow[here, lanes] = part

            @pl.when(own == 0)
            def _():
                sent[here, width + lanes.start : width + lanes.stop] = part.astype(BF16)


def backward_kernel(member, grad_pre, hidden_weight, normed, gain, deviation, adj_t, *refs):
    before, (small, inner, near, far, product, rows_grad) = refs[:-6], refs[-6:]
    nodes, width = inner.shape
    points = adj_t.shape[1]
    inverse_gain = 1.0 / gain[...]
    for column in range(0, width, 512):
        columns = slice(column, column + 512)
        product[:, columns] = dot(
            grad_pre[member * points : (member + 1) * points, :], hidden_weight[columns, :], ((1,), (1,))
        )

    def step(index, total):
        here = pl.ds(pl.multiple_of(index * 32, 32), 32)
        there = pl.ds(pl.multiple_of(member * points + index * 32, 32), 32)
        value = product[here, :]
        zn = normed[there, :].astype(F32)
        both = value * zn
        scaled = value * gain[...]
        mean = jnp.sum(scaled, axis=1, keepdims=True) * (1.0 / width)
        slant = jnp.sum(both, axis=1, keepdims=True) * (1.0 / width)
        grad = deviation[there, :] * (scaled - mean - (zn * inverse_gain) * slant)
        rows_grad[here, :] = grad.astype(BF16)
        return total + jnp.sum(both.reshape(4, 8, width), axis=0)

    total = before[0][...] if before else jnp.zeros((8, width), F32)
    total = lax.fori_loop(0, points // 32, step, total, unroll=4)
    value = dot(adj_t[...], rows_grad[...])
    value = value[:LANES] + value[LANES:]
    below, above = value[:RIM], value[RIM + nodes : nodes + 2 * RIM]
    odd = (here_index() & 1) == 1
    near[...] = jnp.where(odd, below, above).astype(BF16)
    far[...] = jnp.where(odd, above, below).astype(BF16)
    inner[...] = value[RIM : RIM + nodes]
    if not before:
        small[...] = total
        return
    row = jnp.concatenate(
        [
            jnp.sum(total, axis=0, keepdims=True) * inverse_gain,
            jnp.broadcast_to(before[1][...], (1, small.shape[1] - width)),
        ],
        axis=1,
    )
    upper = row.astype(BF16).astype(F32)
    index = jax.lax.broadcasted_iota(jnp.int32, (8, row.shape[1]), 0)
    small[...] = jnp.where(index == 0, upper, jnp.where(index == 1, row - upper, 0.0)).astype(BF16)


def add_rims(inner, near, far, grad_latent):
    members, nodes = grad_latent.shape[:2]
    odd = (here_index() & 1) == 1
    for member in range(members):
        low = jnp.where(odd, near[member].astype(F32), far[member].astype(F32))
        high = jnp.where(odd, far[member].astype(F32), near[member].astype(F32))
        value = inner[member]
        grad_latent[member, :RIM, :] = value[:RIM, :] + low
        grad_latent[member, RIM : nodes - RIM, :] = value[RIM : nodes - RIM, :]
        grad_latent[member, nodes - RIM :, :] = value[nodes - RIM :, :] + high


def write_rows(count, chunk, side, source, target, wide, start, sems):
    width = target.shape[1]
    first, rows = chunks(width, count)[chunk]
    size = rows >> (count - 1)
    half = core_index() ^ side
    mask = jnp.where(half == 0, turn(count, here_index(), 0), turn(count, here_index(), 1))
    copies = []
    for block in range(rows // size):
        here = slice(block * size, (block + 1) * size)
        there = slice(start + block * size, start + (block + 1) * size)
        wide[there, :] = source[here, :width].astype(F32)
        row = half * (width // 2) + first + (block ^ mask) * size
        copy = pltpu.make_async_copy(
            wide.at[there, :],
            target.at[pl.ds(pl.multiple_of(row, size), size), :],
            sems.at[block],
        )
        copy.start()
        copies.append(copy)
    return copies


def write_kernel(count, pieces, members, *refs):
    sources, inner, (near, far) = refs[: len(pieces)], refs[len(pieces) :][:members], refs[len(pieces) + members :][:2]
    target, target_latent, wide, grad_latent, sems, last_sems = refs[len(pieces) + members + 2 :]
    add_rims(inner, near, far, grad_latent)
    copies = fetch((grad_latent,), (target_latent,), last_sems)
    start = 0
    for i, ((chunk, side), source) in enumerate(zip(pieces, sources)):
        copies += write_rows(count, chunk, side, source, target, wide, start, sems.at[i])
        start += source.shape[0]
    for copy in copies:
        copy.wait()


def last_write_kernel(
    count, own, other, small, other_small, before,
    target, grad_out_t, grad_gain, loss,
    wide, narrow, narrow_t, gain_row, loss_cell, sems, last_sems,
):
    del before
    width = target.shape[1]
    last = len(chunks(width, count)) - 1
    copies = write_rows(count, last, 1, other, target, wide, 0, sems)
    for starts, size, mine, place_row in narrow_rows(count, width):
        here = pl.ds(place_row, size)
        for side, row in enumerate(starts):
            lanes = slice(width + side * LANES, width + (side + 1) * LANES)
            value = jnp.where(mine == 1, own[here, lanes].astype(F32), other[here, lanes].astype(F32))
            narrow[row : row + size, :] = value
    narrow_t[...] = narrow[...].T[: grad_out_t.shape[0], :]
    total = small[...].astype(F32) + other_small[...].astype(F32)
    total = total[:1] + total[1:2]
    gain_row[...] = total[:, :width]
    loss_cell[...] = total[:, width : width + 1]
    copies += fetch((narrow_t, gain_row, loss_cell), (grad_out_t, grad_gain, loss), last_sems)
    for copy in copies:
        copy.wait()


def add_parts(mine, other):
    return (mine.astype(F32) + other.astype(F32)).astype(BF16)


def unpack(small):
    return small[:1].astype(F32) + small[1:2].astype(F32)


def swap_with(value, small, bits):
    rows = value.shape[0]
    other = swap_bits(jnp.concatenate([value, small]), bits)
    total = unpack(small) + unpack(other[rows:])
    upper = total.astype(BF16)
    lower = (total - upper.astype(F32)).astype(BF16)
    rest = jnp.zeros((small.shape[0] - 2, small.shape[1]), BF16)
    return other[:rows], jnp.concatenate([upper, lower, rest])


class Sum:
    def __init__(self, sent, kept, count):
        self.sent, self.value, self.small = sent, kept, None
        forth = orders(count)
        self.stages = forth + forth[-2::-1]
        self.halvings, self.stage = count - 1, 0

    def start(self, *others):
        rows = self.value.shape[0] // 2 if 0 < self.stage < self.halvings else 0
        sent = self.value[:rows] if rows else self.value
        if self.stage == 0:
            sent = self.sent
        if others:
            sent = after(sent, *others)
        bits = self.stages[self.stage]
        last = self.stage == len(self.stages) - 1
        if self.small is not None and (0 < self.stage <= self.halvings or last):
            self.other, self.small = swap_with(sent, self.small, bits)
        else:
            self.other = swap_bits(sent, bits)
        return sent

    def finish(self, *others):
        other = after(self.other, *others) if others else self.other
        if self.stage <= self.halvings:
            self.value = add_parts(self.value[-other.shape[0] :], other)
        else:
            self.value = jnp.concatenate([other, self.value])
        self.stage += 1


def after(value, *others):
    return lax.optimization_barrier((value, *others))[0]


def in_hbm(*values):
    return [pltpu.with_memory_space_constraint(value, pltpu.HBM) for value in values]


def local(
    latent,
    edge_node_index,
    edge_mask,
    edge_weight,
    valid,
    area,
    state,
    target,
    var_weight,
    gain,
    hidden_weight,
    output_weight,
):
    members, nodes, width = latent.shape
    points, variables = state.shape
    rows = members * points
    count = lax.axis_size("space").bit_length() - 1
    space = lax.axis_index("space")
    parts = chunks(width, count)
    odd = (space & 1) == 1
    low, high = latent[:, :RIM], latent[:, nodes - RIM :]
    near = swap_pairs(jnp.where(odd, low, high), "space", 0)
    far = swap_pairs(jnp.where(odd, high, low), "space", 1)

    adj, adj_t, score_weight, projection, gain, own, base, hidden_weight = pl.pallas_call(
        prepare_kernel,
        out_shape=(
            pltpu.VMEM((points, 2 * LANES), BF16),
            pltpu.VMEM((2 * LANES, points), BF16),
            pltpu.VMEM((variables, points), F32),
            pltpu.VMEM((LANES, width), BF16),
            pltpu.VMEM((1, width), F32),
            pltpu.VMEM(latent.shape, BF16),
            pltpu.VMEM((variables, points), F32),
            pltpu.VMEM((width, width), BF16),
        ),
        in_specs=[HBM] * 12,
        out_specs=(VMEM,) * 8,
        scratch_shapes=[
            pltpu.VMEM(edge_mask.T.shape, jnp.int32),
            pltpu.VMEM(edge_mask.T.shape, jnp.int32),
            pltpu.VMEM(edge_mask.T.shape, F32),
            pltpu.VMEM((1, points), jnp.int32),
            pltpu.VMEM((1, points), F32),
            pltpu.VMEM((1, variables), F32),
            pltpu.VMEM((variables, width), BF16),
            pltpu.VMEM((variables, points), F32),
            pltpu.VMEM((variables, points), F32),
            pltpu.SemaphoreType.DMA((12,)),
        ],
        compiler_params=PARAMS,
        name="prepare",
    )(
            *in_hbm(
            edge_node_index.T,
            edge_mask.T,
            edge_weight.T,
            valid.reshape(1, points),
            area.reshape(1, points),
            var_weight.reshape(1, variables),
            output_weight.T,
            gain.reshape(1, width),
            latent,
            state.T,
            target.T,
            hidden_weight,
        ),
    )
    normed, hidden, slope, outputs, deviation = pl.pallas_call(
        forward_kernel,
        out_shape=(
            pltpu.VMEM((rows, width), BF16),
            pltpu.VMEM((rows, width), BF16),
            pltpu.VMEM((rows, width), BF16),
            jax.ShapeDtypeStruct((members, variables, points), F32),
            pltpu.VMEM((rows, 1), F32),
        ),
        in_specs=[VMEM] * 7,
        out_specs=(VMEM,) * 5,
        scratch_shapes=[
            pltpu.VMEM((members, 2 * LANES, width), BF16),
            pltpu.VMEM((members, points, width), F32),
            pltpu.VMEM((points, LANES), F32),
        ],
        compiler_params=PARAMS,
        name="forward",
    )(adj, near, own, far, gain, hidden_weight, projection)
    others = swap_cores(outputs)
    normed_t, own_score, own_grad = pl.pallas_call(
        lambda *refs: transpose_kernel(count, *refs),
        out_shape=(
            pltpu.VMEM((width, rows), BF16),
            pltpu.VMEM((variables, points), F32),
            pltpu.VMEM((members, variables, points), F32),
        ),
        in_specs=[VMEM] * 3,
        out_specs=(VMEM,) * 3,
        compiler_params=PARAMS,
        cost_estimate=LIGHT,
        name="transpose",
    )(normed, outputs, base)
    loss, grad_pre, grad_pred_t, sent = pl.pallas_call(
        score_kernel,
        out_shape=(
            jax.ShapeDtypeStruct((1, 1), F32),
            pltpu.VMEM((rows, width), BF16),
            pltpu.VMEM((LANES, rows), BF16),
            jax.ShapeDtypeStruct((parts[0][1], width), BF16),
        ),
        in_specs=[VMEM] * 8,
        out_specs=(VMEM,) * 4,
        scratch_shapes=[pltpu.VMEM((rows, LANES), BF16), pltpu.VMEM((LANES, rows), F32)],
        compiler_params=PARAMS,
        name="score",
    )(outputs, others, own_score, own_grad, score_weight, projection, slope, normed_t)

    def product(first, size, received, *narrow):
        shape = jax.ShapeDtypeStruct((size // 2, received.shape[1]), BF16)
        return pl.pallas_call(
            lambda *refs: product_kernel(first, *refs),
            out_shape=(shape, shape),
            in_specs=[VMEM] * (3 + len(narrow)),
            out_specs=(VMEM, VMEM),
            compiler_params=PARAMS,
            cost_estimate=LIGHT,
            name="product",
        )(normed_t, grad_pre, received, *narrow)

    last = len(parts) - 1
    last_rows = parts[last][1]
    extra = LANES * (width // 2 // last_rows)
    received = swap_cores(sent)
    sent, kept_narrow = pl.pallas_call(
        lambda *refs: sent_kernel(count, *refs),
        out_shape=(
            jax.ShapeDtypeStruct((last_rows, width + extra), BF16),
            pltpu.VMEM((last_rows, extra), F32),
        ),
        in_specs=[VMEM] * 4,
        out_specs=(VMEM,) * 2,
        compiler_params=PARAMS,
        cost_estimate=LIGHT,
        name="sent",
    )(normed_t, grad_pre, grad_pred_t, hidden)
    sums, token = [], ()
    received = (received, swap_cores(sent))
    for chunk, (first, size) in enumerate(parts):
        narrow = [kept_narrow] if chunk == last else []
        sums.append(Sum(*product(width // 2 + first, size, after(received[chunk], *token), *narrow), count))
        token = (sums[-1].start(),)

    def backward(member, adj_t, *before):
        last = len(before) > 1
        return pl.pallas_call(
            lambda *refs: backward_kernel(member, *refs),
            out_shape=(
                jax.ShapeDtypeStruct((8, width + extra), BF16) if last else pltpu.VMEM((8, width), F32),
                pltpu.VMEM((nodes, width), F32),
                jax.ShapeDtypeStruct((RIM, width), BF16),
                jax.ShapeDtypeStruct((RIM, width), BF16),
            ),
            in_specs=[VMEM] * (6 + len(before)),
            out_specs=(VMEM,) * 4,
            scratch_shapes=[pltpu.VMEM((points, width), F32), pltpu.VMEM((points, width), BF16)],
            compiler_params=PARAMS,
            cost_estimate=LIGHT,
            name="backward",
        )(grad_pre, hidden_weight, normed, gain, deviation, adj_t, *before)

    done = []
    for stage in range(2 * count - 1):
        for chunk in range(last + 1):
            if stage == 0 and len(done) < members:
                before = (done[-1][0],) if done else ()
                if len(done) == members - 1:
                    before = before + (loss,)
                done.append(backward(len(done), after(adj_t, *token), *before))
                token = token + (done[-1][1],)
                if len(done) == members:
                    sums[last].small = done[-1][0]
            sums[chunk].finish(*(token if stage == 0 else ()))
            token = ()
            if stage < 2 * count - 2:
                token = (sums[chunk].start(),)
            if stage == 3 and chunk == last:
                inner, near, far = zip(*(part[1:] for part in done))
                near, far = after(jnp.stack(near), *token), after(jnp.stack(far), *token)
                near, far = swap_pairs(near, "space", 0), swap_pairs(far, "space", 1)
    own = [chunk.value for chunk in sums]
    other = [swap_cores(value) for value in own]
    small = sums[last].small
    other_small = swap_cores(small)
    hidden_shape = jax.ShapeDtypeStruct((width, width), F32)
    blocks = 1 << (count - 1)

    pieces = [(0, 0), (0, 1), (last, 0)]
    sources = [own[0], other[0], own[last]]
    latent_shape = (members, nodes, width)
    grad_hidden, grad_latent = pl.pallas_call(
        lambda *refs: write_kernel(count, pieces, members, *refs),
        out_shape=(hidden_shape, jax.ShapeDtypeStruct(latent_shape, F32)),
        in_specs=[VMEM] * (len(pieces) + members + 2),
        out_specs=(HBM, HBM),
        scratch_shapes=[
            pltpu.VMEM((sum(source.shape[0] for source in sources), width), F32),
            pltpu.VMEM(latent_shape, F32),
            pltpu.SemaphoreType.DMA((len(pieces), blocks)),
            pltpu.SemaphoreType.DMA((1,)),
        ],
        compiler_params=PARAMS,
        cost_estimate=LIGHT,
        name="write",
    )(*sources, *inner, near, far)
    grad_hidden, grad_out, grad_gain, loss = pl.pallas_call(
        lambda *refs: last_write_kernel(count, *refs),
        out_shape=(
            hidden_shape,
            jax.ShapeDtypeStruct((variables, width), F32),
            jax.ShapeDtypeStruct((1, width), F32),
            jax.ShapeDtypeStruct((1, 1), F32),
        ),
        in_specs=[VMEM] * 4 + [HBM],
        out_specs=(HBM,) * 4,
        scratch_shapes=[
            pltpu.VMEM((last_rows, width), F32),
            pltpu.VMEM((width, LANES), F32),
            pltpu.VMEM((variables, width), F32),
            pltpu.VMEM((1, width), F32),
            pltpu.VMEM((1, 1), F32),
            pltpu.SemaphoreType.DMA((blocks,)),
            pltpu.SemaphoreType.DMA((3,)),
        ],
        input_output_aliases={4: 0},
        compiler_params=PARAMS,
        name="last_write",
    )(own[last], other[last], small, other_small, grad_hidden)
    return (loss.reshape(1), grad_hidden, grad_out.T, grad_gain.reshape(width), grad_latent)


def solution(mesh):
    in_specs = (
        P(("groups", "member"), "space", None),
        P(("groups", "space"), None),
        P(("groups", "space"), None),
        P(("groups", "space"), None),
        P(("groups", "space")),
        P(("groups", "space")),
        P(("groups", "space"), None),
        P(("groups", "space"), None),
        P(),
        P(),
        P(),
        P(),
    )
    out_specs = (
        P("groups"),
        P("groups", None),
        P("groups", None),
        P("groups"),
        P(("groups", "member"), "space", None),
    )
    return jax.shard_map(local, mesh=mesh, in_specs=in_specs, out_specs=out_specs, check_vma=False)
```
